128 devices in a mesh: dp: 8 (over x, core), seq: 16 (over z, y).
Axes of the slice: x: 4, y: 4, z: 4, core: 2. Of those that a mesh axis runs over, the one named last changes fastest.
Arguments:
- depths: int32 [8, 4096], P('dp', 'seq'), may hold values from 1 to 3, as said below
- owners: int32 [2, 8, 4096], P(None, 'dp', 'seq'), may hold values from 0 to 15, as said below
- cotangent: bfloat16 [2, 8, 4096, 2048], P(None, 'dp', 'seq'), may hold values from -48 to 48
- query_early: bfloat16 [8, 768, 2048], P('dp', 'seq'), may hold values from -20 to 20
- keyval_early: bfloat16 [8, 768, 2, 2048], P('dp', 'seq'), may hold values from -20 to 20
- query_late: bfloat16 [8, 384, 2048], P('dp', 'seq'), may hold values from -20 to 20
- keyval_late: bfloat16 [8, 384, 2, 2048], P('dp', 'seq'), may hold values from -20 to 20
- out_weight: bfloat16 [2048, 2048], replicated, may hold values from -0.125 to 0.125
Outputs:
- dquery_early: bfloat16 [8, 768, 2048], P('dp', 'seq')
- dkeyval_early: bfloat16 [8, 768, 2, 2048], P('dp', 'seq')
- dquery_late: bfloat16 [8, 384, 2048], P('dp', 'seq')
- dkeyval_late: bfloat16 [8, 384, 2, 2048], P('dp', 'seq')
- dweight: float32 [2048, 2048], P(('dp', 'seq'))
The draws below stay inside these ranges and needn't reach their ends.
Inputs may be any that keep to these rules, and one draw needn't show every extreme that they name: `depths`: A token is active at the earlier recursion when its depth is 2 or more and at the later one when it is 3. Every sequence has exactly 768 tokens active at the earlier recursion and 384 at the later; in each block of 256 positions the count at the later recursion is a multiple of 16 and the count at the earlier one is twice it. owners[0] holds the earlier recursion, owners[1] the later; entries of tokens not active at that recursion carry no meaning. A block of 256 positions sends the same number of its active tokens to every device along seq, at most 4 at the later recursion and 8 at the earlier, and some block sends exactly that many; every device receives exactly 24 and 48 tokens.
All inputs are finite; a program needn't handle non-finite values.
Results may differ from the reference program's by a relative error of at most 0.024.
Values may be sent and summed in bfloat16 or wider, within the bound.
A program may use at most 128 MiB of HBM per device.

```python
import jax
import jax.numpy as jnp
from jax import lax

HEADS = 16
HEAD_DIM = 128
WIDTH = 2048
TOK_DEV = 256
SLOTS_LATE = 24
PEAK_LATE = 4
ATTN = 2048
SLOTS_EARLY = 48
SEQS = 8
SEQ_LEN = 4096
KEYS_EARLY = 768
KEYS_LATE = 384
N_SEQ = 16


def route_plan(key):

    def one_sequence(seq_key):
        parts = jax.random.split(seq_key, 5)
        busy = jax.random.randint(parts[0], (), 0, N_SEQ)
        units = jnp.arange(N_SEQ * PEAK_LATE, dtype=jnp.int32)
        unit_source = units // PEAK_LATE
        shuffled = jax.random.permutation(parts[1], N_SEQ * PEAK_LATE).astype(jnp.int32)
        shuffled = jnp.where(unit_source == busy, N_SEQ * PEAK_LATE + units, shuffled)
        standing = jnp.argsort(jnp.argsort(shuffled))
        chosen = (standing < SLOTS_LATE - PEAK_LATE).astype(jnp.int32)
        sources = jnp.arange(N_SEQ, dtype=jnp.int32)
        per_pair = jnp.sum(chosen.reshape(N_SEQ, PEAK_LATE), axis=1) + jnp.where(sources == busy, PEAK_LATE, 0)
        late_count = N_SEQ * per_pair
        early_count = 2 * late_count
        jitter = jax.random.randint(parts[2], (N_SEQ, TOK_DEV), 0, 65536)
        scored = jitter * TOK_DEV + jnp.arange(TOK_DEV, dtype=jnp.int32)[None, :]
        ranking = jnp.argsort(jnp.argsort(scored, axis=1), axis=1)
        depth = 1 + (ranking < early_count[:, None]).astype(jnp.int32) + (ranking < late_count[:, None]).astype(jnp.int32)
        owner_lists = []
        for section in range(2):
            active = depth > section + 1
            flags = active.astype(jnp.int32)
            before = jnp.cumsum(flags, axis=1) - flags
            mixing = jax.random.randint(jax.random.fold_in(parts[3], section), (N_SEQ, N_SEQ), 0, 65536)
            mixing = mixing * N_SEQ + sources[None, :]
            targets = jnp.argsort(mixing, axis=1).astype(jnp.int32)
            picked = jnp.take_along_axis(targets, before % N_SEQ, axis=1)
            filler = jax.random.randint(jax.random.fold_in(parts[4], section), (N_SEQ, TOK_DEV), 0, N_SEQ)
            owner_lists.append(jnp.where(active, picked, filler).reshape(-1))
        return (depth.reshape(-1).astype(jnp.int32), jnp.stack(owner_lists).astype(jnp.int32))
    depth, owner = jax.vmap(one_sequence)(jax.random.split(key, SEQS))
    return (depth, jnp.swapaxes(owner, 0, 1))


def clipped_normal(key, shape):
    return jnp.clip(jax.random.normal(key, shape, jnp.float32), -4.0, 4.0)


def draw_depths(key, part):
    depth, owner = route_plan(key)
    return depth


def draw_owners(key, part):
    depth, owner = route_plan(key)
    return owner


def draw_query_early(key, part):
    key = jax.random.fold_in(key, 3)
    query = clipped_normal(key, (SEQS, KEYS_EARLY, ATTN))
    return query.astype(jnp.bfloat16)


def draw_keyval_early(key, part):
    base = clipped_normal(jax.random.fold_in(key, 101), (SEQS, KEYS_EARLY, ATTN))
    key = jax.random.fold_in(key, 4)
    keyed = base
    value = 2.0 * clipped_normal(key, (SEQS, KEYS_EARLY, ATTN))
    return jnp.stack([keyed, value], axis=2).astype(jnp.bfloat16)


def draw_query_late(key, part):
    key = jax.random.fold_in(key, 5)
    query = clipped_normal(key, (SEQS, KEYS_LATE, ATTN))
    return query.astype(jnp.bfloat16)


def draw_keyval_late(key, part):
    base = clipped_normal(jax.random.fold_in(key, 202), (SEQS, KEYS_LATE, ATTN))
    key = jax.random.fold_in(key, 6)
    keyed = base
    value = 2.0 * clipped_normal(key, (SEQS, KEYS_LATE, ATTN))
    return jnp.stack([keyed, value], axis=2).astype(jnp.bfloat16)


def block_scale(key, shape, cuts, least, top_value):
    level = 1.0
    for dim, blocks in cuts:
        draws = jax.random.uniform(jax.random.fold_in(jax.random.fold_in(key, 6), dim), (blocks,), jnp.float32, least / len(cuts), top_value / len(cuts))
        level = level * jnp.repeat(jnp.exp(draws), shape[dim] // blocks).reshape((-1,) + (1,) * (len(shape) - 1 - dim))
    return level


def gaussian(key, shape, width, most, pieces=(), kind=jnp.bfloat16):
    result = jax.random.normal(key, shape, jnp.float32) * width
    if len(pieces) > 0:
        result = block_scale(key, shape, pieces, -0.22, 0.18) * result
    return jnp.clip(result, min=-most, max=most).astype(kind)


def setup_inputs(seed: int = 0) -> dict:
    splits = jax.random.split(jax.random.key(seed), 9)
    depths = draw_depths(jax.random.fold_in(splits[8], 71), 0)
    owners = draw_owners(jax.random.fold_in(splits[8], 71), 0)
    cotangent = gaussian(splits[2], (2, SEQS, SEQ_LEN, WIDTH), 8.0, 48.0, ((1, 8), (2, 16)))
    query_early = draw_query_early(jax.random.fold_in(splits[8], 71), 0)
    keyval_early = draw_keyval_early(jax.random.fold_in(splits[8], 71), 0)
    query_late = draw_query_late(jax.random.fold_in(splits[8], 71), 0)
    keyval_late = draw_keyval_late(jax.random.fold_in(splits[8], 71), 0)
    out_weight = gaussian(splits[7], (ATTN, WIDTH), ATTN ** -0.5, 0.125)
    return {"depths": depths, "owners": owners, "cotangent": cotangent, "query_early": query_early, "keyval_early": keyval_early, "query_late": query_late, "keyval_late": keyval_late, "out_weight": out_weight}


def slot_places(active, owner, slots):
    flags = active.reshape(N_SEQ, TOK_DEV).astype(jnp.int32)
    before = jnp.cumsum(flags, axis=1) - flags
    per_pair = jnp.sum(flags, axis=1) // N_SEQ
    offset = jnp.cumsum(per_pair) - per_pair
    target = owner.reshape(N_SEQ, TOK_DEV).astype(jnp.int32) * slots + offset[:, None] + before // N_SEQ
    target = jnp.where(flags > 0, target, N_SEQ * slots).reshape(-1).astype(jnp.int32)
    positions = jnp.arange(SEQ_LEN, dtype=jnp.int32)
    filled = jnp.zeros((N_SEQ * slots + 1,), jnp.int32).at[target].set(positions)
    return filled[:-1]


def head_backward(items, places):
    query, keys, values, dout = items
    rows = query.shape[0]
    score_scale = HEAD_DIM ** -0.5
    scores = jnp.dot(query, keys.T, preferred_element_type=jnp.float32) * score_scale
    visible = places[None, :] <= places[:, None]
    scores = jnp.where(visible, scores, jnp.float32(-1e30))
    top = jnp.max(scores, axis=1, keepdims=True)
    weights = jnp.exp(scores - top)
    probs = weights / jnp.sum(weights, axis=1, keepdims=True)
    probs_bf = probs.astype(jnp.bfloat16)
    attended = jnp.dot(probs_bf, values, preferred_element_type=jnp.float32).astype(jnp.bfloat16)
    delta = jnp.sum(dout.astype(jnp.float32) * attended.astype(jnp.float32), axis=1, keepdims=True)
    dprobs = jnp.dot(dout, values.T, preferred_element_type=jnp.float32)
    dscores = (probs * (dprobs - delta)).astype(jnp.bfloat16)
    dquery = (jnp.dot(dscores, keys, preferred_element_type=jnp.float32) * score_scale).astype(jnp.bfloat16)
    block = rows // N_SEQ
    gathered_score_matrix = dscores.astype(jnp.float32).reshape(N_SEQ, block, rows)
    gathered_probabilities = probs_bf.astype(jnp.float32).reshape(N_SEQ, block, rows)
    gathered_query_rows = query.astype(jnp.float32).reshape(N_SEQ, block, HEAD_DIM)
    gathered_output_gradient = dout.astype(jnp.float32).reshape(N_SEQ, block, HEAD_DIM)
    key_pieces = (jnp.einsum("xdc,xdy->xcy", gathered_score_matrix, gathered_query_rows) * score_scale).astype(jnp.bfloat16)
    value_pieces = jnp.einsum("xdc,xdy->xcy", gathered_probabilities, gathered_output_gradient).astype(jnp.bfloat16)
    dkey = jnp.sum(key_pieces.astype(jnp.float32), axis=0).astype(jnp.bfloat16)
    dvalue = jnp.sum(value_pieces.astype(jnp.float32), axis=0).astype(jnp.bfloat16)
    return attended, dquery, dkey, dvalue


def recursion_backward(query, keyval, grads, places, out_weight):
    rows = query.shape[0]
    rows_in = jnp.take(grads, places, axis=0)
    dout = jnp.dot(rows_in, out_weight.T, preferred_element_type=jnp.float32).astype(jnp.bfloat16)

    def split_heads(matrix):
        return matrix.reshape(rows, HEADS, HEAD_DIM).transpose(1, 0, 2)

    def join_heads(stacked):
        return stacked.transpose(1, 0, 2).reshape(rows, HEADS * HEAD_DIM)

    heads = (split_heads(query), split_heads(keyval[:, 0]), split_heads(keyval[:, 1]), split_heads(dout))
    attended, dquery, dkey, dvalue = lax.map(lambda items: head_backward(items, places), heads)
    dkeyval = jnp.stack([join_heads(dkey), join_heads(dvalue)], axis=1)
    return join_heads(attended), join_heads(dquery), dkeyval, rows_in


def reference(depths, owners, cotangent, query_early, keyval_early, query_late, keyval_late, out_weight):
    def one_sequence(items):
        depth, owner, grads, early_query, early_keyval, late_query, late_keyval = items
        early_places = slot_places(depth > 1, owner[0], SLOTS_EARLY)
        late_places = slot_places(depth > 2, owner[1], SLOTS_LATE)
        early_attn, early_dquery, early_dkeyval, early_rows = recursion_backward(early_query, early_keyval, grads[0], early_places, out_weight)
        late_attn, late_dquery, late_dkeyval, late_rows = recursion_backward(late_query, late_keyval, grads[1], late_places, out_weight)
        partial_grad = jnp.dot(early_attn.T, early_rows, preferred_element_type=jnp.float32) + jnp.dot(late_attn.T, late_rows, preferred_element_type=jnp.float32)
        return early_dquery, early_dkeyval, late_dquery, late_dkeyval, partial_grad

    results = lax.map(one_sequence, (depths, jnp.swapaxes(owners, 0, 1), jnp.swapaxes(cotangent, 0, 1), query_early, keyval_early, query_late, keyval_late))
    return results[0], results[1], results[2], results[3], jnp.sum(results[4], axis=0)
```

```python
import jax
import jax.numpy as jnp
from jax import lax
from jax.experimental import pallas as pl
from jax.experimental.pallas import tpu as pltpu
from jax.sharding import PartitionSpec as P

MESH = pl.DeviceIdType.MESH
F32, BF16, I32 = jnp.float32, jnp.bfloat16, jnp.int32

N = 16
DP = 8
E = 128
W = 2048
TOK = 256
NE, NL = 48, 24
NLP = 32
ROWS = NE + NLP
KE, KL = N * NE, N * NL
SCALE = E**-0.5


def dot(a, b):
    return lax.dot_general(a, b, (((1,), (0,)), ((), ())), preferred_element_type=F32)


def dot_nt(a, b):
    return lax.dot_general(a, b, (((1,), (1,)), ((), ())), preferred_element_type=F32)


def dot_tn(a, b):
    return lax.dot_general(a, b, (((0,), (0,)), ((), ())), preferred_element_type=F32)


def iota(shape, dim):
    return lax.broadcasted_iota(I32, shape, dim)


def onehot(mask):
    return jnp.where(mask, 1.0, 0.0).astype(BF16)


def kernel(
    depths, owners, cot, qkv, weight,
    out, dw,
    cotv, wv, rows_send, rows_recv, meta_send, meta_recv, qkv_recv, rows_all,
    dout_send, dout_recv, att_send, att_recv, dqkv_send, part_send, part_recv,
    probs_e, probs_bf_e, ds_e, probs_l, probs_bf_l, ds_l,
    local_sem, send, recv, gsend, grecv,
):
    d = lax.axis_index("dp")
    s = lax.axis_index("seq")
    chip = lax.div(d, 2)
    core = lax.rem(d, 2)
    partner = chip * 2 + 1 - core
    target_dp = lax.div(s, 2)
    parity = lax.rem(s, 2)

    cot_copy = pltpu.make_async_copy(cot, cotv, local_sem.at[0])
    weight_copy = pltpu.make_async_copy(weight, wv, local_sem.at[1])
    cot_copy.start()
    weight_copy.start()

    barrier = pltpu.get_barrier_semaphore()

    def greet(to_dp, to_seq):
        pl.semaphore_signal(barrier, inc=1, device_id=(to_dp, to_seq), device_id_type=MESH)

    def greet_seq(i, _):
        greet(d, lax.rem(s + i, N))
        return 0

    lax.fori_loop(1, N, greet_seq, 0)
    greet(partner, s)
    for i in range(1, 4):
        greet(lax.rem(chip + i, 4) * 2 + core, s)

    def greet_heads(i, _):
        from_dp, from_seq = lax.div(i, 2), 2 * d + lax.rem(i, 2)

        @pl.when(jnp.logical_or(from_dp != d, from_seq != s))
        def _():
            greet(from_dp, from_seq)

        return 0

    lax.fori_loop(0, 2 * DP, greet_heads, 0)

    depth = depths[...]
    active_e, active_l = depth > 1, depth > 2
    owner_e, owner_l = owners[0], owners[1]
    flags = jnp.where(
        iota((16, TOK), 0) < 8,
        jnp.broadcast_to(active_e.astype(F32), (16, TOK)),
        jnp.broadcast_to(active_l.astype(F32), (16, TOK)),
    ).astype(BF16)
    below = onehot(iota((TOK, TOK), 0) < iota((TOK, TOK), 1))
    before = dot(flags, below).astype(I32)
    rank_e, rank_l = before[0:1] >> 4, before[8:9] >> 4
    token = (iota((N, TOK), 1) + 1).astype(F32)
    lane = iota((N, TOK), 0)
    spread_e = jnp.where((lane == owner_e) & active_e, token, 0.0).astype(BF16)
    spread_l = jnp.where((lane == owner_l) & active_l, token, 0.0).astype(BF16)
    line = iota((E, TOK), 0)
    meta_send[0:N] = dot_nt(spread_e, onehot(line == s * 8 + rank_e))
    meta_send[N : 2 * N] = dot_nt(spread_l, onehot(line == s * 4 + rank_l))

    cot_copy.wait()
    line = iota((TOK, TOK), 0)
    base = jnp.where(active_e, owner_e * 16 + rank_e, -64)
    packed = dot(onehot(line == base), cotv[0, :, 0:1024])
    packed += dot(onehot(line == base + 8), cotv[0, :, 1024:2048])
    rows_send[:, :, 0:1024] = packed.reshape(N, 16, 1024).astype(BF16)
    base = jnp.where(active_l, owner_l * 16 + rank_l, -64)
    packed = dot(onehot(line == base), cotv[1, :, 0:512])
    for q in range(1, 4):
        packed += dot(onehot(line == base + 4 * q), cotv[1, :, q * 512 : (q + 1) * 512])
    rows_send[:, :, 1024:1536] = packed.reshape(N, 16, 512).astype(BF16)

    elsewhere = jnp.where(target_dp == d, 0, 1)
    pl.semaphore_wait(barrier, N - 1 + 4 + N - 1 + elsewhere)

    def remote(src, dst, phase, to, sender, to_dp):
        return pltpu.make_async_remote_copy(
            src_ref=src,
            dst_ref=dst,
            send_sem=send.at[phase, to],
            recv_sem=recv.at[phase, sender],
            device_id=(to_dp, to),
            device_id_type=MESH,
        )

    def exchange(phase, src, dst):
        def step(i, _):
            to = lax.rem(s + i, N)
            remote(src(to), dst(s), phase, to, s, d).start()
            return 0

        lax.fori_loop(1, N, step, 0)
        pltpu.make_async_copy(src(s), dst(s), recv.at[phase, s]).start()

    def arrive(phase, src, dst):
        def step(i, _):
            sender = lax.rem(s + i, N)
            remote(src(sender), dst(sender), phase, sender, sender, d).wait_recv()
            return 0

        lax.fori_loop(1, N, step, 0)
        pltpu.make_async_copy(src(s), dst(s), recv.at[phase, s]).wait()

    def sent(phase, src, dst):
        def step(i, _):
            to = lax.rem(s + i, N)
            remote(src(to), dst(s), phase, to, s, d).wait_send()
            return 0

        lax.fori_loop(1, N, step, 0)

    def columns(ref, j):
        return ref.at[:, pl.ds(pl.multiple_of(j * E, E), E)]

    META = (0, lambda j: meta_send, lambda j: meta_recv.at[j])
    ROW = (1, lambda j: rows_send.at[j], lambda j: rows_recv.at[j])
    QKV = (2, lambda j: columns(qkv, j), lambda j: qkv_recv.at[j])
    DOUT = (3, lambda j: columns(dout_send, j), lambda j: dout_recv.at[j])
    GRAD = (4, lambda j: dqkv_send.at[j], lambda j: columns(out, j))
    PART = (5, lambda j: part_send.at[j], lambda j: part_recv.at[j])

    exchange(*META)
    exchange(*ROW)
    exchange(*QKV)

    arrive(*META)
    token_e = jnp.zeros((N, E), F32)
    token_l = jnp.zeros((N, E), F32)
    for j in range(N):
        token_e += meta_recv[j, 0:N]
        token_l += meta_recv[j, N : 2 * N]

    def tables(token, shift, slots, padded):
        peak = 1 << shift
        valid = onehot(token > 0.0)
        src, dst = iota((E, E), 0), iota((E, E), 1)
        offset = dot(valid, onehot((src >> shift) < (dst >> shift)))[0:1].astype(I32)
        in_lane = iota((1, E), 1)
        slot = jnp.where(token[0:1] > 0.0, offset + (in_lane & (peak - 1)), -1)
        select = onehot(iota((padded, E), 0) == slot)
        low = token.astype(BF16)
        high = jnp.where(token > 0.0, (iota((N, E), 1) >> shift).astype(F32), 0.0).astype(BF16)
        cols = dot_nt(select, high) * 256.0 + dot_nt(select, low) - 1.0
        total = N * slots
        mult = 1366 if slots == NE else 2731
        in_row = iota((padded, total), 1)
        tile = onehot(in_row - ((in_row * mult) >> 16) * slots == iota((padded, total), 0))
        wide_high = dot(dot_nt(high, select).astype(BF16), tile)
        wide_low = dot(dot_nt(low, select).astype(BF16), tile)
        in_row = iota((N, total), 1)
        mine = ((in_row * mult) >> 16) == iota((N, total), 0)
        row = jnp.sum(
            jnp.where(mine, wide_high * 256.0 + wide_low - 1.0, 0.0), axis=0, keepdims=True
        )
        src, dst = iota((E, TOK), 0), iota((E, TOK), 1)
        offset = dot(valid, onehot((src >> shift) < (dst >> 4)))[0:1].astype(I32)
        count = dot(valid, onehot((src >> shift) == (dst >> 4)))[0:1].astype(I32)
        in_lane = iota((1, TOK), 1)
        rank = in_lane & (peak - 1)
        slot = jnp.where(rank < count, offset + rank, -1)
        part = (in_lane & 15) >> shift
        return cols, row, slot, part

    cols_e, row_e, slot_e, part_e = tables(token_e, 3, NE, NE)
    cols_l, row_l, slot_l, part_l = tables(token_l, 2, NL, NLP)

    arrive(*ROW)
    for h in range(2):
        pick = onehot((iota((NE, TOK), 0) == slot_e) & (part_e == h))
        got = dot(pick, rows_recv[:, :, 0:1024].reshape(TOK, 1024))
        rows_all[d, 0:NE, h * 1024 : (h + 1) * 1024] = got.astype(BF16)
    for q in range(4):
        pick = onehot((iota((NLP, TOK), 0) == slot_l) & (part_l == q))
        got = dot(pick, rows_recv[:, :, 1024:1536].reshape(TOK, 512))
        rows_all[d, NE:ROWS, q * 512 : (q + 1) * 512] = got.astype(BF16)

    def gather(block, index, to_dp):
        return pltpu.make_async_remote_copy(
            src_ref=rows_all.at[block],
            dst_ref=rows_all.at[block],
            send_sem=gsend.at[index],
            recv_sem=grecv.at[block],
            device_id=(to_dp, s),
            device_id_type=MESH,
        )

    def same_core(i):
        return lax.rem(chip + i, 4) * 2 + core

    gather(d, 0, partner).start()
    for i in (2, 1, 3):
        gather(d, i, same_core(i)).start()

    weight_copy.wait()
    mine = rows_all[d]
    for c in range(8):
        part = dot_nt(mine, wv[c * 256 : (c + 1) * 256, :])
        dout_send[:, c * 256 : (c + 1) * 256] = part.astype(BF16)
    exchange(*DOUT)

    arrive(*QKV)

    def late(ref, first):
        wide = ref[:, first : first + NLP, :].astype(F32)[:, 0:NL, :]
        return wide.reshape(KL, E)

    def softmax(query, key, value, row, col):
        scores = dot_nt(query, key) * SCALE
        scores = jnp.where(row <= col, scores, -1e30)
        top = jnp.max(scores, axis=1, keepdims=True)
        weights = jnp.exp(scores - top)
        probs = weights / jnp.sum(weights, axis=1, keepdims=True)
        probs_bf = probs.astype(BF16)
        return probs, probs_bf, dot(probs_bf, value)

    key_e = qkv_recv[:, NE : 2 * NE, :].reshape(KE, E)
    value_e = qkv_recv[:, 2 * NE : 3 * NE, :].reshape(KE, E)
    for b in range(4):
        query = qkv_recv[4 * b : 4 * b + 4, 0:NE, :].reshape(4 * NE, E)
        col = jnp.concatenate([cols_e[:, o : o + 1] for o in range(4 * b, 4 * b + 4)], axis=0)
        probs, probs_bf, attended = softmax(query, key_e, value_e, row_e, col)
        probs_e[b * 192 : (b + 1) * 192] = probs
        probs_bf_e[b * 192 : (b + 1) * 192] = probs_bf
        att_send[4 * b : 4 * b + 4, 0:NE, :] = attended.reshape(4, NE, E).astype(BF16)
    query_l = late(qkv_recv, 144).astype(BF16)
    key_l = late(qkv_recv, 176).astype(BF16)
    value_l = late(qkv_recv, 208).astype(BF16)
    gap = jnp.zeros((8, NLP - NL, E), F32)
    for b in range(2):
        query = query_l[b * 192 : (b + 1) * 192]
        col = jnp.concatenate([cols_l[0:NL, o : o + 1] for o in range(8 * b, 8 * b + 8)], axis=0)
        probs, probs_bf, attended = softmax(query, key_l, value_l, row_l, col)
        probs_l[b * 192 : (b + 1) * 192] = probs
        probs_bf_l[b * 192 : (b + 1) * 192] = probs_bf
        attended = jnp.concatenate([attended.reshape(8, NL, E), gap], axis=1)
        att_send[8 * b : 8 * b + 8, NE:ROWS, :] = attended.astype(BF16)

    ATT = 6

    def att_copy(to):
        return remote(att_send.at[to], att_recv.at[d, parity], ATT, to, d * 2 + parity, target_dp)

    def att_local():
        return pltpu.make_async_copy(
            att_send.at[s], att_recv.at[d, parity], recv.at[ATT, d * 2 + parity]
        )

    def att_step(i, _):
        att_copy(lax.rem(s + i, N)).start()
        return 0

    lax.fori_loop(1, N, att_step, 0)

    @pl.when(target_dp == d)
    def _():
        att_local().start()

    @pl.when(target_dp != d)
    def _():
        att_copy(s).start()

    for i in (1, 3, 2):
        gather(same_core(i), i, partner).wait_recv()
        gather(same_core(i), 3 + i, partner).start()

    arrive(*DOUT)

    def backward(query, key, value, dout, attended, probs):
        delta = jnp.sum(dout.astype(F32) * attended.astype(F32), axis=1, keepdims=True)
        dprobs = dot_nt(dout, value)
        dscores = (probs * (dprobs - delta)).astype(BF16)
        return dscores, dot(dscores, key) * SCALE

    for b in range(4):
        dout = dout_recv[4 * b : 4 * b + 4, 0:NE, :].reshape(192, E)
        attended = att_send[4 * b : 4 * b + 4, 0:NE, :].reshape(192, E)
        query = None
        dscores, dquery = backward(
            query, key_e, value_e, dout, attended, probs_e[b * 192 : (b + 1) * 192]
        )
        ds_e[b * 192 : (b + 1) * 192] = dscores
        dqkv_send[4 * b : 4 * b + 4, 0:NE, :] = dquery.reshape(4, NE, E).astype(BF16)
    dout_l = late(dout_recv, NE).astype(BF16)
    attended_l = late(att_send, NE)
    for b in range(2):
        dscores, dquery = backward(
            None, key_l, value_l, dout_l[b * 192 : (b + 1) * 192],
            attended_l[b * 192 : (b + 1) * 192], probs_l[b * 192 : (b + 1) * 192]
        )
        ds_l[b * 192 : (b + 1) * 192] = dscores
        dquery = jnp.concatenate([dquery.reshape(8, NL, E), gap], axis=1)
        dqkv_send[8 * b : 8 * b + 8, 144:176, :] = dquery.astype(BF16)
    query_e = qkv_recv[:, 0:NE, :].reshape(KE, E)
    dout_e = dout_recv[:, 0:NE, :].reshape(KE, E)
    for c in range(2):
        dkey = dot_tn(ds_e[:, c * 384 : (c + 1) * 384], query_e) * SCALE
        dqkv_send[8 * c : 8 * c + 8, NE : 2 * NE, :] = dkey.reshape(8, NE, E).astype(BF16)
        dvalue = dot_tn(probs_bf_e[:, c * 384 : (c + 1) * 384], dout_e)
        dqkv_send[8 * c : 8 * c + 8, 2 * NE : 3 * NE, :] = dvalue.reshape(8, NE, E).astype(BF16)
    gap = jnp.zeros((N, NLP - NL, E), F32)
    dkey = dot_tn(ds_l[...], query_l) * SCALE
    dkey = jnp.concatenate([dkey.reshape(N, NL, E), gap], axis=1)
    dqkv_send[:, 176:208, :] = dkey.astype(BF16)
    dvalue = dot_tn(probs_bf_l[...], dout_l)
    dvalue = jnp.concatenate([dvalue.reshape(N, NL, E), gap], axis=1)
    dqkv_send[:, 208:240, :] = dvalue.astype(BF16)
    exchange(*GRAD)

    def att_wait(i, _):
        sender = lax.div(i, 2)
        remote(
            att_send.at[0], att_recv.at[sender, lax.rem(i, 2)], ATT, s, i, target_dp
        ).wait_recv()
        return 0

    lax.fori_loop(0, 2 * DP, att_wait, 0)
    gather(partner, 0, partner).wait_recv()
    for i in (1, 3, 2):
        gather(lax.rem(chip + i, 4) * 2 + 1 - core, i, partner).wait_recv()
    rows = rows_all[...].reshape(DP * ROWS, W)
    for p in range(2):
        attended = att_recv[:, p].reshape(DP * ROWS, E)
        for c in range(4):
            part = dot_tn(attended, rows[:, c * 512 : (c + 1) * 512])
            part_send[8 * p : 8 * p + 8, :, c * 512 : (c + 1) * 512] = part.reshape(
                8, 16, 512
            ).astype(BF16)
    exchange(*PART)
    arrive(*PART)
    total = part_recv[0].astype(F32)
    for j in range(1, N):
        total += part_recv[j].astype(F32)
    dw[...] = total
    arrive(*GRAD)

    for phase in (META, ROW, QKV, DOUT, GRAD, PART):
        sent(*phase)

    def att_sent(i, _):
        att_copy(lax.rem(s + i, N)).wait_send()
        return 0

    lax.fori_loop(1, N, att_sent, 0)

    @pl.when(target_dp != d)
    def _():
        att_copy(s).wait_send()

    for i in range(7):
        gather(d, i, partner).wait_send()


def shards(
    depths, owners, cotangent, query_early, keyval_early, query_late, keyval_late, out_weight
):
    def late(rows):
        return jnp.pad(rows, ((0, NLP - NL), (0, 0)))

    qkv = jnp.concatenate(
        [
            query_early[0],
            keyval_early[0, :, 0],
            keyval_early[0, :, 1],
            late(query_late[0]),
            late(keyval_late[0, :, 0]),
            late(keyval_late[0, :, 1]),
        ],
        axis=0,
    )
    vmem = pl.BlockSpec(memory_space=pltpu.VMEM)
    hbm = pl.BlockSpec(memory_space=pl.ANY)
    grads, dweight = pl.pallas_call(
        kernel,
        out_shape=(
            jax.ShapeDtypeStruct((3 * ROWS, W), BF16),
            jax.ShapeDtypeStruct((N, W), F32),
        ),
        in_specs=[vmem, vmem, hbm, hbm, hbm],
        out_specs=(hbm, vmem),
        scratch_shapes=[
            pltpu.VMEM((2, TOK, W), BF16),
            pltpu.VMEM((W, W), BF16),
            pltpu.VMEM((N, 16, 1536), BF16),
            pltpu.VMEM((N, 16, 1536), BF16),
            pltpu.VMEM((2 * N, E), F32),
            pltpu.VMEM((N, 2 * N, E), F32),
            pltpu.VMEM((N, 3 * ROWS, E), BF16),
            pltpu.VMEM((DP, ROWS, W), BF16),
            pltpu.VMEM((ROWS, W), BF16),
            pltpu.VMEM((N, ROWS, E), BF16),
            pltpu.VMEM((N, ROWS, E), BF16),
            pltpu.VMEM((DP, 2, ROWS, E), BF16),
            pltpu.VMEM((N, 3 * ROWS, E), BF16),
            pltpu.VMEM((N, N, W), BF16),
            pltpu.VMEM((N, N, W), BF16),
            pltpu.VMEM((KE, KE), F32),
            pltpu.VMEM((KE, KE), BF16),
            pltpu.VMEM((KE, KE), BF16),
            pltpu.VMEM((KL, KL), F32),
            pltpu.VMEM((KL, KL), BF16),
            pltpu.VMEM((KL, KL), BF16),
            pltpu.SemaphoreType.DMA((2,)),
            pltpu.SemaphoreType.DMA((7, N)),
            pltpu.SemaphoreType.DMA((7, N)),
            pltpu.SemaphoreType.DMA((7,)),
            pltpu.SemaphoreType.DMA((DP,)),
        ],
        compiler_params=pltpu.CompilerParams(
            collective_id=0, has_side_effects=True, vmem_limit_bytes=56 * 1024 * 1024
        ),
        cost_estimate=pl.CostEstimate(
            flops=3_000_000_000, bytes_accessed=20_000_000, transcendentals=800_000
        ),
        name="rows_attention_weight",
    )(depths, owners[:, 0], cotangent[:, 0], qkv, out_weight)

    def pair(first, second, count):
        return jnp.stack(
            [grads[first : first + count], grads[second : second + count]], axis=1
        )[None]

    return (
        grads[None, 0:NE],
        pair(NE, 2 * NE, NE),
        grads[None, 144 : 144 + NL],
        pair(176, 208, NL),
        dweight,
    )


def solution(mesh):
    in_specs = (
        P("dp", "seq"),
        P(None, "dp", "seq"),
        P(None, "dp", "seq", None),
        P("dp", "seq", None),
        P("dp", "seq", None, None),
        P("dp", "seq", None),
        P("dp", "seq", None, None),
        P(),
    )
    out_specs = (
        P("dp", "seq", None),
        P("dp", "seq", None, None),
        P("dp", "seq", None),
        P("dp", "seq", None, None),
        P(("dp", "seq"), None),
    )
    return jax.shard_map(shards, mesh=mesh, in_specs=in_specs, out_specs=out_specs, check_vma=False)
```

```python
import jax
import jax.numpy as jnp
from jax import lax
from jax.experimental import pallas as pl
from jax.experimental.pallas import tpu as pltpu
from jax.sharding import PartitionSpec as P

MESH = pl.DeviceIdType.MESH
F32, BF16, I32 = jnp.float32, jnp.bfloat16, jnp.int32

N = 16
DP = 8
E = 128
W = 2048
TOK = 256
NE, NL = 48, 24
NLP = 32
ROWS = NE + NLP
QKV_ROWS = 3 * NE + 80
OTHERS = (
    (2, 2), (1, 2), (2, 1), (2, 3), (3, 2), (0, 2), (2, 0), (1, 1),
    (3, 3), (1, 3), (3, 1), (0, 1), (1, 0), (0, 3), (3, 0),
)
KE, KL = N * NE, N * NL
SCALE = E**-0.5


def dot(a, b):
    return lax.dot_general(a, b, (((1,), (0,)), ((), ())), preferred_element_type=F32)


def dot_nt(a, b):
    return lax.dot_general(a, b, (((1,), (1,)), ((), ())), preferred_element_type=F32)


def dot_tn(a, b):
    return lax.dot_general(a, b, (((0,), (0,)), ((), ())), preferred_element_type=F32)


def iota(shape, dim):
    return lax.broadcasted_iota(I32, shape, dim)


def onehot(mask):
    return jnp.where(mask, 1.0, 0.0).astype(BF16)


def kernel(
    depths, owners, cot, query_early, keyval_early, query_late, keyval_late, weight,
    out, dw,
    cotv, wv, ql_v, kve_v, kvl_v, qkv_send,
    rows_send, rows_recv, meta_send, meta_recv, qkv_recv, rows_all,
    dout_send, dout_recv, att_send, att_recv, dqkv_send,
    sum1_send, sum1_recv, sum2_send, sum2_recv,
    probs_e, probs_bf_e, ds_e, probs_l, probs_bf_l, ds_l,
    local_sem, send, recv, gsend, grecv, sum_send, sum_recv,
):
    d = lax.axis_index("dp")
    s = lax.axis_index("seq")
    chip = lax.div(d, 2)
    core = lax.rem(d, 2)
    partner = chip * 2 + 1 - core
    z, y = lax.div(s, 4), lax.rem(s, 4)

    def head_of(j):
        return lax.rem(chip + lax.div(j, 4) + 2 * core, 4) * 4 + lax.rem(j, 4)

    def holder(of_dp, head):
        turn = lax.div(head, 4) + 8 - lax.div(of_dp, 2) - 2 * lax.rem(of_dp, 2)
        return lax.rem(turn, 4) * 4 + lax.rem(head, 4)

    my_head = head_of(s)
    target_dp = lax.div(my_head, 2)
    parity = lax.rem(my_head, 2)

    cot_copy = pltpu.make_async_copy(cot, cotv, local_sem.at[0])
    weight_copy = pltpu.make_async_copy(weight, wv, local_sem.at[1])
    operands = [
        pltpu.make_async_copy(keyval_early, kve_v, local_sem.at[2]),
        pltpu.make_async_copy(keyval_late, kvl_v, local_sem.at[3]),
        pltpu.make_async_copy(query_early.at[0], qkv_send.at[0:NE], local_sem.at[4]),
        pltpu.make_async_copy(query_late, ql_v, local_sem.at[5]),
    ]
    cot_copy.start()
    for copy in operands:
        copy.start()
    weight_copy.start()

    barrier = pltpu.get_barrier_semaphore()

    def greet(to_dp, to_seq):
        pl.semaphore_signal(barrier, inc=1, device_id=(to_dp, to_seq), device_id_type=MESH)

    def greet_seq(i, _):
        greet(d, lax.rem(s + i, N))
        return 0

    lax.fori_loop(1, N, greet_seq, 0)
    greet(partner, s)
    for i in range(1, 4):
        greet(lax.rem(chip + i, 4) * 2 + core, s)

    def greet_heads(i, _):
        from_dp = lax.div(i, 2)
        from_seq = holder(from_dp, 2 * d + lax.rem(i, 2))

        @pl.when(jnp.logical_or(from_dp != d, from_seq != s))
        def _():
            greet(from_dp, from_seq)

        return 0

    lax.fori_loop(0, 2 * DP, greet_heads, 0)

    depth = depths[...]
    active_e, active_l = depth > 1, depth > 2
    owner_e, owner_l = owners[0], owners[1]
    flags = jnp.where(
        iota((16, TOK), 0) < 8,
        jnp.broadcast_to(active_e.astype(F32), (16, TOK)),
        jnp.broadcast_to(active_l.astype(F32), (16, TOK)),
    ).astype(BF16)
    below = onehot(iota((TOK, TOK), 0) < iota((TOK, TOK), 1))
    before = dot(flags, below).astype(I32)
    rank_e, rank_l = before[0:1] >> 4, before[8:9] >> 4
    token = (iota((8, TOK), 1) + 1).astype(F32).astype(BF16)
    line = iota((E, TOK), 0)
    meta_e = dot_nt(token, onehot((line == owner_e * 8 + rank_e) & active_e))
    meta_l = dot_nt(token, onehot((line == owner_l * 4 + rank_l) & active_l))
    meta_send[...] = jnp.where(iota((8, E), 0) < 4, meta_e, meta_l)

    cot_copy.wait()
    line = iota((TOK, TOK), 0)
    base = jnp.where(active_e, owner_e * 16 + rank_e, -64)
    packed = dot(onehot(line == base), cotv[0, :, 0:1024])
    packed += dot(onehot(line == base + 8), cotv[0, :, 1024:2048])
    rows_send[:, :, 0:1024] = packed.reshape(N, 16, 1024).astype(BF16)
    base = jnp.where(active_l, owner_l * 16 + rank_l, -64)
    packed = dot(onehot(line == base), cotv[1, :, 0:512])
    for q in range(1, 4):
        packed += dot(onehot(line == base + 4 * q), cotv[1, :, q * 512 : (q + 1) * 512])
    rows_send[:, :, 1024:1536] = packed.reshape(N, 16, 512).astype(BF16)

    for copy in operands:
        copy.wait()
    qkv_send[NE : 2 * NE] = kve_v[0, :, 0, :]
    qkv_send[2 * NE : 3 * NE] = kve_v[0, :, 1, :]
    for c in range(4):
        cut = slice(c * 512, (c + 1) * 512)
        pair = kvl_v[0, :, :, cut].astype(F32)
        qkv_send[3 * NE : QKV_ROWS, cut] = jnp.concatenate(
            [ql_v[0, :, cut].astype(F32), pair[:, 0], pair[:, 1], jnp.zeros((8, 512), F32)], axis=0
        ).astype(BF16)

    elsewhere = jnp.where(target_dp == d, 0, 1)
    pl.semaphore_wait(barrier, N - 1 + 4 + N - 1 + elsewhere)

    def remote(src, dst, phase, to, sender, to_dp):
        return pltpu.make_async_remote_copy(
            src_ref=src,
            dst_ref=dst,
            send_sem=send.at[phase, to],
            recv_sem=recv.at[phase, sender],
            device_id=(to_dp, to),
            device_id_type=MESH,
        )

    def other(dz, dy):
        to_z = lax.rem(z + jnp.where(core == 0, dz, 4 - dz), 4)
        to_y = lax.rem(y + jnp.where(core == 0, dy, 4 - dy), 4)
        return to_z * 4 + to_y

    def exchange(phase, src, dst):
        for dz, dy in OTHERS:
            to = other(dz, dy)
            remote(src(to), dst(s), phase, to, s, d).start()
        pltpu.make_async_copy(src(s), dst(s), recv.at[phase, s]).start()

    def arrive(phase, src, dst):
        def step(i, _):
            sender = lax.rem(s + i, N)
            remote(src(sender), dst(sender), phase, sender, sender, d).wait_recv()
            return 0

        lax.fori_loop(1, N, step, 0)
        pltpu.make_async_copy(src(s), dst(s), recv.at[phase, s]).wait()

    def sent(phase, src, dst):
        def step(i, _):
            to = lax.rem(s + i, N)
            remote(src(to), dst(s), phase, to, s, d).wait_send()
            return 0

        lax.fori_loop(1, N, step, 0)

    def columns(ref, j):
        return ref.at[:, pl.ds(pl.multiple_of(head_of(j) * E, E), E)]

    META = (0, lambda j: meta_send, lambda j: meta_recv.at[j])
    ROW = (1, lambda j: rows_send.at[j], lambda j: rows_recv.at[j])
    QKV = (2, lambda j: columns(qkv_send, j), lambda j: qkv_recv.at[j])
    DOUT = (3, lambda j: columns(dout_send, j), lambda j: dout_recv.at[j])
    GRAD = (4, lambda j: dqkv_send.at[j], lambda j: columns(out, j))

    exchange(*META)
    exchange(*ROW)
    exchange(*QKV)

    arrive(*META)

    def spread(first, shift):
        lane = iota((N, E), 1)
        mine = (lane >> shift) == iota((N, E), 0)
        wide = jnp.concatenate(
            [jnp.where(mine, meta_recv[j, first : first + 1], 0.0) for j in range(N)], axis=0
        )
        low = (1 << shift) - 1
        same = onehot((iota((E, E), 0) & low) == (iota((E, E), 1) & low))
        wide = dot(wide.astype(BF16), same)
        total = jnp.zeros((N, E), F32)
        for j in range(N):
            total += jnp.where((lane >> shift) == j, wide[j * N : (j + 1) * N], 0.0)
        return total

    token_e = spread(0, 3)
    token_l = spread(4, 2)

    def tables(token, shift, slots, padded):
        peak = 1 << shift
        valid = onehot(token > 0.0)
        src, dst = iota((E, E), 0), iota((E, E), 1)
        offset = dot(valid, onehot((src >> shift) < (dst >> shift)))[0:1].astype(I32)
        in_lane = iota((1, E), 1)
        slot = jnp.where(token[0:1] > 0.0, offset + (in_lane & (peak - 1)), -1)
        select = onehot(iota((padded, E), 0) == slot)
        low = token.astype(BF16)
        high = jnp.where(token > 0.0, (iota((N, E), 1) >> shift).astype(F32), 0.0).astype(BF16)
        cols = dot_nt(select, high) * 256.0 + dot_nt(select, low) - 1.0
        total = N * slots
        mult = 1366 if slots == NE else 2731
        in_row = iota((padded, total), 1)
        tile = onehot(in_row - ((in_row * mult) >> 16) * slots == iota((padded, total), 0))
        wide_high = dot(dot_nt(high, select).astype(BF16), tile)
        wide_low = dot(dot_nt(low, select).astype(BF16), tile)
        in_row = iota((N, total), 1)
        mine = ((in_row * mult) >> 16) == iota((N, total), 0)
        row = jnp.sum(
            jnp.where(mine, wide_high * 256.0 + wide_low - 1.0, 0.0), axis=0, keepdims=True
        )
        src, dst = iota((E, TOK), 0), iota((E, TOK), 1)
        offset = dot(valid, onehot((src >> shift) < (dst >> 4)))[0:1].astype(I32)
        count = dot(valid, onehot((src >> shift) == (dst >> 4)))[0:1].astype(I32)
        in_lane = iota((1, TOK), 1)
        rank = in_lane & (peak - 1)
        slot = jnp.where(rank < count, offset + rank, -1)
        part = (in_lane & 15) >> shift
        return cols, row, slot, part

    cols_e, row_e, slot_e, part_e = tables(token_e, 3, NE, NE)
    cols_l, row_l, slot_l, part_l = tables(token_l, 2, NL, NLP)

    arrive(*ROW)
    for h in range(2):
        pick = onehot((iota((NE, TOK), 0) == slot_e) & (part_e == h))
        got = dot(pick, rows_recv[:, :, 0:1024].reshape(TOK, 1024))
        rows_all[d, 0:NE, h * 1024 : (h + 1) * 1024] = got.astype(BF16)
    for q in range(4):
        pick = onehot((iota((NLP, TOK), 0) == slot_l) & (part_l == q))
        got = dot(pick, rows_recv[:, :, 1024:1536].reshape(TOK, 512))
        rows_all[d, NE:ROWS, q * 512 : (q + 1) * 512] = got.astype(BF16)

    def gather(block, index, to_dp):
        return pltpu.make_async_remote_copy(
            src_ref=rows_all.at[block],
            dst_ref=rows_all.at[block],
            send_sem=gsend.at[index],
            recv_sem=grecv.at[block],
            device_id=(to_dp, s),
            device_id_type=MESH,
        )

    def same_core(i):
        return lax.rem(chip + i, 4) * 2 + core

    gather(d, 0, partner).start()
    for i in (2, 1, 3):
        gather(d, i, same_core(i)).start()

    weight_copy.wait()
    mine = rows_all[d]
    for c in range(8):
        part = dot_nt(mine, wv[c * 256 : (c + 1) * 256, :])
        dout_send[:, c * 256 : (c + 1) * 256] = part.astype(BF16)
    exchange(*DOUT)

    arrive(*QKV)

    def late(wide, part):
        return wide[:, part * NL : (part + 1) * NL].reshape(KL, E)

    def softmax(query, key, value, row, col):
        scores = dot_nt(query, key) * SCALE
        scores = jnp.where(row <= col, scores, -1e30)
        top = jnp.max(scores, axis=1, keepdims=True)
        weights = jnp.exp(scores - top)
        probs = weights / jnp.sum(weights, axis=1, keepdims=True)
        probs_bf = probs.astype(BF16)
        return probs, probs_bf, dot(probs_bf, value)

    key_e = qkv_recv[:, NE : 2 * NE, :].reshape(KE, E)
    value_e = qkv_recv[:, 2 * NE : 3 * NE, :].reshape(KE, E)
    for b in range(4):
        query = qkv_recv[4 * b : 4 * b + 4, 0:NE, :].reshape(4 * NE, E)
        col = jnp.concatenate([cols_e[:, o : o + 1] for o in range(4 * b, 4 * b + 4)], axis=0)
        probs, probs_bf, attended = softmax(query, key_e, value_e, row_e, col)
        probs_e[b * 192 : (b + 1) * 192] = probs
        probs_bf_e[b * 192 : (b + 1) * 192] = probs_bf
        att_send[4 * b : 4 * b + 4, 0:NE, :] = attended.reshape(4, NE, E).astype(BF16)
    wide = qkv_recv[:, 3 * NE : QKV_ROWS, :].astype(F32)
    query_l, key_l, value_l = (late(wide, part).astype(BF16) for part in range(3))
    gap = jnp.zeros((8, NLP - NL, E), F32)
    for b in range(2):
        query = query_l[b * 192 : (b + 1) * 192]
        col = jnp.concatenate([cols_l[0:NL, o : o + 1] for o in range(8 * b, 8 * b + 8)], axis=0)
        probs, probs_bf, attended = softmax(query, key_l, value_l, row_l, col)
        probs_l[b * 192 : (b + 1) * 192] = probs
        probs_bf_l[b * 192 : (b + 1) * 192] = probs_bf
        attended = jnp.concatenate([attended.reshape(8, NL, E), gap], axis=1)
        att_send[8 * b : 8 * b + 8, NE:ROWS, :] = attended.astype(BF16)

    ATT = 5

    def att_copy(to):
        return remote(att_send.at[to], att_recv.at[d, parity], ATT, to, d * 2 + parity, target_dp)

    def att_local():
        return pltpu.make_async_copy(
            att_send.at[s], att_recv.at[d, parity], recv.at[ATT, d * 2 + parity]
        )

    for dz, dy in OTHERS:
        att_copy(other(dz, dy)).start()

    @pl.when(target_dp == d)
    def _():
        att_local().start()

    @pl.when(target_dp != d)
    def _():
        att_copy(s).start()

    arrive(*DOUT)

    def backward(query, key, value, dout, attended, probs):
        delta = jnp.sum(dout.astype(F32) * attended.astype(F32), axis=1, keepdims=True)
        dprobs = dot_nt(dout, value)
        dscores = (probs * (dprobs - delta)).astype(BF16)
        return dscores, dot(dscores, key) * SCALE

    for b in range(4):
        dout = dout_recv[4 * b : 4 * b + 4, 0:NE, :].reshape(192, E)
        attended = att_send[4 * b : 4 * b + 4, 0:NE, :].reshape(192, E)
        query = None
        dscores, dquery = backward(
            query, key_e, value_e, dout, attended, probs_e[b * 192 : (b + 1) * 192]
        )
        ds_e[b * 192 : (b + 1) * 192] = dscores
        dqkv_send[4 * b : 4 * b + 4, 0:NE, :] = dquery.reshape(4, NE, E).astype(BF16)
    dout_l = late(dout_recv[:, NE:ROWS, :].astype(F32), 0).astype(BF16)
    attended_l = late(att_send[:, NE:ROWS, :].astype(F32), 0)
    dquery_l = []
    for b in range(2):
        dscores, dquery = backward(
            None, key_l, value_l, dout_l[b * 192 : (b + 1) * 192],
            attended_l[b * 192 : (b + 1) * 192], probs_l[b * 192 : (b + 1) * 192]
        )
        ds_l[b * 192 : (b + 1) * 192] = dscores
        dquery_l.append(dquery)
    query_e = qkv_recv[:, 0:NE, :].reshape(KE, E)
    dout_e = dout_recv[:, 0:NE, :].reshape(KE, E)
    for c in range(2):
        dkey = dot_tn(ds_e[:, c * 384 : (c + 1) * 384], query_e) * SCALE
        dqkv_send[8 * c : 8 * c + 8, NE : 2 * NE, :] = dkey.reshape(8, NE, E).astype(BF16)
        dvalue = dot_tn(probs_bf_e[:, c * 384 : (c + 1) * 384], dout_e)
        dqkv_send[8 * c : 8 * c + 8, 2 * NE : 3 * NE, :] = dvalue.reshape(8, NE, E).astype(BF16)
    dquery = jnp.concatenate(dquery_l, axis=0)
    dkey = dot_tn(ds_l[...], query_l) * SCALE
    dvalue = dot_tn(probs_bf_l[...], dout_l)
    parts = [part.reshape(N, NL, E) for part in (dquery, dkey, dvalue)]
    parts.append(jnp.zeros((N, 8, E), F32))
    dqkv_send[:, 3 * NE : QKV_ROWS, :] = jnp.concatenate(parts, axis=1).astype(BF16)
    exchange(*GRAD)

    for i in (1, 3, 2):
        gather(same_core(i), i, partner).wait_recv()
        gather(same_core(i), 3 + i, partner).start()

    def att_wait(i, _):
        sender = lax.div(i, 2)
        remote(
            att_send.at[0], att_recv.at[sender, lax.rem(i, 2)], ATT, s, i, target_dp
        ).wait_recv()
        return 0

    lax.fori_loop(0, 2 * DP, att_wait, 0)
    gather(partner, 0, partner).wait_recv()
    for i in (1, 3, 2):
        gather(lax.rem(chip + i, 4) * 2 + 1 - core, i, partner).wait_recv()
    rows = rows_all[...].reshape(DP * ROWS, W)
    for p in range(2):
        attended = att_recv[:, p].reshape(DP * ROWS, E)
        for c in range(4):
            half, cut = c // 2, slice((c % 2) * 512, (c % 2) * 512 + 512)
            part = dot_tn(attended, rows[:, c * 512 : (c + 1) * 512])
            part = part.reshape(2, 4, 16, 512).astype(BF16)
            if half == 0:
                sum1_send[0, 2 * p : 2 * p + 2, :, :, cut] = part
            else:
                for i in range(2):
                    for j in range(4):
                        sum1_send[1, j, 2 * p + i, :, cut] = part[i, j]

    def along(half, stage, i):
        if half == stage:
            to = lax.rem(z + i, 4)
            return to, to * 4 + y
        to = lax.rem(y + i, 4)
        return to, z * 4 + to

    def sum_copy(half, stage, i):
        source, target = (sum1_send, sum1_recv) if stage == 0 else (sum2_send, sum2_recv)
        to, device = along(half, stage, i)
        return pltpu.make_async_remote_copy(
            src_ref=source.at[half, to],
            dst_ref=target.at[half, i - 1],
            send_sem=sum_send.at[stage, half, i - 1],
            recv_sem=sum_recv.at[stage, half, i - 1],
            device_id=(d, device),
            device_id_type=MESH,
        )

    for i in (2, 1, 3):
        for half in range(2):
            sum_copy(half, 0, i).start()
    for half in range(2):
        for i in range(1, 4):
            sum_copy(half, 0, i).wait_recv()
        total = sum1_send[half, z if half == 0 else y].astype(F32)
        for i in range(3):
            total += sum1_recv[half, i].astype(F32)
        sum2_send[half] = total.astype(BF16)
        for i in (2, 1, 3):
            sum_copy(half, 1, i).start()
    for half in range(2):
        for i in range(1, 4):
            sum_copy(half, 1, i).wait_recv()
        total = sum2_send[half, y if half == 0 else z].astype(F32)
        for i in range(3):
            total += sum2_recv[half, i].astype(F32)
        dw[:, half * 1024 : (half + 1) * 1024] = total
    arrive(*GRAD)

    for phase in (META, ROW, QKV, DOUT, GRAD):
        sent(*phase)

    def att_sent(i, _):
        att_copy(lax.rem(s + i, N)).wait_send()
        return 0

    lax.fori_loop(1, N, att_sent, 0)

    @pl.when(target_dp != d)
    def _():
        att_copy(s).wait_send()

    for i in range(7):
        gather(d, i, partner).wait_send()
    for stage in range(2):
        for half in range(2):
            for i in range(1, 4):
                sum_copy(half, stage, i).wait_send()


def finish(grads, dw, dquery_early, dkeyval_early, dquery_late, dkeyval_late, dweight):
    dquery_early[0] = grads[0:NE]
    dkeyval_early[0] = jnp.stack([grads[NE : 2 * NE], grads[2 * NE : 3 * NE]], axis=1)
    late = grads[3 * NE : QKV_ROWS].astype(F32)
    dquery_late[0] = late[0:NL].astype(BF16)
    dkeyval_late[0] = jnp.stack(
        [late[NL : 2 * NL].astype(BF16), late[2 * NL : 3 * NL].astype(BF16)], axis=1
    )
    dweight[...] = dw[...]


def shards(
    depths, owners, cotangent, query_early, keyval_early, query_late, keyval_late, out_weight
):
    vmem = pl.BlockSpec(memory_space=pltpu.VMEM)
    hbm = pl.BlockSpec(memory_space=pl.ANY)
    grads, dw = pl.pallas_call(
        kernel,
        out_shape=(
            jax.ShapeDtypeStruct((QKV_ROWS, W), BF16),
            jax.ShapeDtypeStruct((N, W), F32),
        ),
        in_specs=[vmem, vmem] + [hbm] * 6,
        out_specs=(hbm, vmem),
        scratch_shapes=[
            pltpu.VMEM((2, TOK, W), BF16),
            pltpu.VMEM((W, W), BF16),
            pltpu.VMEM((1, NL, W), BF16),
            pltpu.VMEM((1, NE, 2, W), BF16),
            pltpu.VMEM((1, NL, 2, W), BF16),
            pltpu.VMEM((QKV_ROWS, W), BF16),
            pltpu.VMEM((N, 16, 1536), BF16),
            pltpu.VMEM((N, 16, 1536), BF16),
            pltpu.VMEM((8, E), F32),
            pltpu.VMEM((N, 8, E), F32),
            pltpu.VMEM((N, QKV_ROWS, E), BF16),
            pltpu.VMEM((DP, ROWS, W), BF16),
            pltpu.VMEM((ROWS, W), BF16),
            pltpu.VMEM((N, ROWS, E), BF16),
            pltpu.VMEM((N, ROWS, E), BF16),
            pltpu.VMEM((DP, 2, ROWS, E), BF16),
            pltpu.VMEM((N, QKV_ROWS, E), BF16),
            pltpu.VMEM((2, 4, 4, 16, W // 2), BF16),
            pltpu.VMEM((2, 3, 4, 16, W // 2), BF16),
            pltpu.VMEM((2, 4, 16, W // 2), BF16),
            pltpu.VMEM((2, 3, 16, W // 2), BF16),
            pltpu.VMEM((KE, KE), F32),
            pltpu.VMEM((KE, KE), BF16),
            pltpu.VMEM((KE, KE), BF16),
            pltpu.VMEM((KL, KL), F32),
            pltpu.VMEM((KL, KL), BF16),
            pltpu.VMEM((KL, KL), BF16),
            pltpu.SemaphoreType.DMA((6,)),
            pltpu.SemaphoreType.DMA((6, N)),
            pltpu.SemaphoreType.DMA((6, N)),
            pltpu.SemaphoreType.DMA((7,)),
            pltpu.SemaphoreType.DMA((DP,)),
            pltpu.SemaphoreType.DMA((2, 2, 3)),
            pltpu.SemaphoreType.DMA((2, 2, 3)),
        ],
        compiler_params=pltpu.CompilerParams(
            collective_id=0, has_side_effects=True, vmem_limit_bytes=56 * 1024 * 1024
        ),
        cost_estimate=pl.CostEstimate(
            flops=3_000_000_000, bytes_accessed=20_000_000, transcendentals=800_000
        ),
        name="rows_attention_weight",
    )(
        depths, owners, cotangent[:, 0], query_early, keyval_early, query_late, keyval_late,
        out_weight,
    )
    return pl.pallas_call(
        finish,
        out_shape=(
            jax.ShapeDtypeStruct(query_early.shape, BF16),
            jax.ShapeDtypeStruct(keyval_early.shape, BF16),
            jax.ShapeDtypeStruct(query_late.shape, BF16),
            jax.ShapeDtypeStruct(keyval_late.shape, BF16),
            jax.ShapeDtypeStruct((N, W), F32),
        ),
        in_specs=[vmem] * 2,
        out_specs=(vmem,) * 5,
        compiler_params=pltpu.CompilerParams(vmem_limit_bytes=32 * 1024 * 1024),
        name="outputs",
    )(grads, dw)


def solution(mesh):
    in_specs = (
        P("dp", "seq"),
        P(None, "dp", "seq"),
        P(None, "dp", "seq", None),
        P("dp", "seq", None),
        P("dp", "seq", None, None),
        P("dp", "seq", None),
        P("dp", "seq", None, None),
        P(),
    )
    out_specs = (
        P("dp", "seq", None),
        P("dp", "seq", None, None),
        P("dp", "seq", None),
        P("dp", "seq", None, None),
        P(("dp", "seq"), None),
    )
    return jax.shard_map(shards, mesh=mesh, in_specs=in_specs, out_specs=out_specs, check_vma=False)
```

```python
import jax
import jax.numpy as jnp
from jax import lax
from jax.experimental import pallas as pl
from jax.experimental.pallas import tpu as pltpu
from jax.sharding import PartitionSpec as P

MESH = pl.DeviceIdType.MESH
F32, BF16, I32 = jnp.float32, jnp.bfloat16, jnp.int32

N = 16
DP = 8
E = 128
W = 2048
TOK = 256
NE, NL = 48, 24
NLP = 32
ROWS = NE + NLP
QKV_ROWS = 3 * NE + 80
OTHERS = (
    (2, 2), (1, 2), (2, 1), (2, 3), (3, 2), (0, 2), (2, 0), (1, 1),
    (3, 3), (1, 3), (3, 1), (0, 1), (1, 0), (0, 3), (3, 0),
)
KE, KL = N * NE, N * NL
SCALE = E**-0.5


def dot(a, b):
    return lax.dot_general(a, b, (((1,), (0,)), ((), ())), preferred_element_type=F32)


def dot_nt(a, b):
    return lax.dot_general(a, b, (((1,), (1,)), ((), ())), preferred_element_type=F32)


def dot_tn(a, b):
    return lax.dot_general(a, b, (((0,), (0,)), ((), ())), preferred_element_type=F32)


def iota(shape, dim):
    return lax.broadcasted_iota(I32, shape, dim)


def onehot(mask):
    return jnp.where(mask, 1.0, 0.0).astype(BF16)


def kernel(
    depths, owners, cot, query_early, keyval_early, query_late, keyval_late, weight,
    out, dw,
    depth_v, owner_v, cotv, wv, ql_v, kve_v, kvl_v, qkv_send,
    rows_send, rows_recv, meta_send, meta_recv, qkv_recv, rows_all,
    dout_send, dout_recv, att_send, att_recv, dqkv_send,
    sum1_send, sum1_recv, sum2_send, sum2_recv,
    dw_v,
    probs_e, probs_bf_e, ds_e, probs_l, probs_bf_l, ds_l,
    local_sem, send, recv, gsend, grecv, sum_send, sum_recv,
):
    d = lax.axis_index("dp")
    s = lax.axis_index("seq")
    chip = lax.div(d, 2)
    core = lax.rem(d, 2)
    partner = chip * 2 + 1 - core
    z, y = lax.div(s, 4), lax.rem(s, 4)

    def head_of(j):
        return lax.rem(chip + lax.div(j, 4) + 2 * core, 4) * 4 + lax.rem(j, 4)

    def holder(of_dp, head):
        turn = lax.div(head, 4) + 8 - lax.div(of_dp, 2) - 2 * lax.rem(of_dp, 2)
        return lax.rem(turn, 4) * 4 + lax.rem(head, 4)

    def same_core(i):
        return lax.rem(chip + i, 4) * 2 + core

    my_head = head_of(s)
    target_dp = lax.div(my_head, 2)
    parity = lax.rem(my_head, 2)

    cot_copy = pltpu.make_async_copy(cot, cotv, local_sem.at[0])
    weight_copy = pltpu.make_async_copy(weight, wv, local_sem.at[1])
    routing = [
        pltpu.make_async_copy(depths, depth_v, local_sem.at[6]),
        pltpu.make_async_copy(owners, owner_v, local_sem.at[7]),
    ]
    operands = [
        pltpu.make_async_copy(keyval_early, kve_v, local_sem.at[2]),
        pltpu.make_async_copy(query_late, ql_v, local_sem.at[5]),
        pltpu.make_async_copy(keyval_late, kvl_v, local_sem.at[3]),
        pltpu.make_async_copy(query_early.at[0], qkv_send.at[0:NE], local_sem.at[4]),
    ]
    for copy in routing + operands:
        copy.start()
    cot_copy.start()
    weight_copy.start()

    barrier = pltpu.get_barrier_semaphore()

    def greet(to_dp, to_seq):
        pl.semaphore_signal(barrier, inc=1, device_id=(to_dp, to_seq), device_id_type=MESH)

    def greet_seq(i, _):
        greet(d, lax.rem(s + i, N))
        return 0

    lax.fori_loop(1, N, greet_seq, 0)
    greet(partner, s)
    for i in (1, 3):
        greet(same_core(i), s)

    def greet_heads(i, _):
        from_dp = lax.div(i, 2)
        from_seq = holder(from_dp, 2 * d + lax.rem(i, 2))

        @pl.when(jnp.logical_or(from_dp != d, from_seq != s))
        def _():
            greet(from_dp, from_seq)

        return 0

    lax.fori_loop(0, 2 * DP, greet_heads, 0)

    for copy in routing:
        copy.wait()
    depth = depth_v[...]
    active_e, active_l = depth > 1, depth > 2
    owner_e, owner_l = owner_v[0], owner_v[1]
    flags = jnp.where(
        iota((16, TOK), 0) < 8,
        jnp.broadcast_to(active_e.astype(F32), (16, TOK)),
        jnp.broadcast_to(active_l.astype(F32), (16, TOK)),
    ).astype(BF16)
    below = onehot(iota((TOK, TOK), 0) < iota((TOK, TOK), 1))
    before = dot(flags, below).astype(I32)
    rank_e, rank_l = before[0:1] >> 4, before[8:9] >> 4
    token = (iota((8, TOK), 1) + 1).astype(F32).astype(BF16)
    line = iota((E, TOK), 0)
    meta_e = dot_nt(token, onehot((line == owner_e * 8 + rank_e) & active_e))
    meta_l = dot_nt(token, onehot((line == owner_l * 4 + rank_l) & active_l))
    meta_send[...] = jnp.where(iota((8, E), 0) < 4, meta_e, meta_l)

    for copy in operands:
        copy.wait()
    qkv_send[NE : 2 * NE] = kve_v[0, :, 0, :]
    qkv_send[2 * NE : 3 * NE] = kve_v[0, :, 1, :]
    for c in range(4):
        cut = slice(c * 512, (c + 1) * 512)
        pair = kvl_v[0, :, :, cut].astype(F32)
        qkv_send[3 * NE : QKV_ROWS, cut] = jnp.concatenate(
            [ql_v[0, :, cut].astype(F32), pair[:, 0], pair[:, 1], jnp.zeros((8, 512), F32)], axis=0
        ).astype(BF16)

    cot_copy.wait()
    line = iota((TOK, TOK), 0)
    base = jnp.where(active_e, owner_e * 16 + rank_e, -64)
    packed = dot(onehot(line == base), cotv[0, :, 0:1024])
    packed += dot(onehot(line == base + 8), cotv[0, :, 1024:2048])
    rows_send[:, :, 0:1024] = packed.reshape(N, 16, 1024).astype(BF16)
    base = jnp.where(active_l, owner_l * 16 + rank_l, -64)
    packed = dot(onehot(line == base), cotv[1, :, 0:512])
    for q in range(1, 4):
        packed += dot(onehot(line == base + 4 * q), cotv[1, :, q * 512 : (q + 1) * 512])
    rows_send[:, :, 1024:1536] = packed.reshape(N, 16, 512).astype(BF16)

    elsewhere = jnp.where(target_dp == d, 0, 1)
    pl.semaphore_wait(barrier, N - 1 + 3 + N - 1 + elsewhere)

    def remote(src, dst, phase, to, to_dp):
        return pltpu.make_async_remote_copy(
            src_ref=src,
            dst_ref=dst,
            send_sem=send.at[phase],
            recv_sem=recv.at[phase],
            device_id=(to_dp, to),
            device_id_type=MESH,
        )

    def wait_bytes(ref, sem):
        pltpu.make_async_copy(ref, ref, sem).wait()

    def other(dz, dy):
        to_z = lax.rem(z + jnp.where(core == 0, dz, 4 - dz), 4)
        to_y = lax.rem(y + jnp.where(core == 0, dy, 4 - dy), 4)
        return to_z * 4 + to_y

    def exchange(phase, src, dst, whole):
        for dz, dy in OTHERS:
            to = other(dz, dy)
            remote(src(to), dst(s), phase, to, d).start()
        pltpu.make_async_copy(src(s), dst(s), recv.at[phase]).start()

    def arrive(phase, src, dst, whole):
        wait_bytes(whole, recv.at[phase])

    def columns(ref, j):
        return ref.at[:, pl.ds(pl.multiple_of(head_of(j) * E, E), E)]

    META = (0, lambda j: meta_send, lambda j: meta_recv.at[j], meta_recv)
    ROW = (1, lambda j: rows_send.at[j], lambda j: rows_recv.at[j], rows_recv)
    QKV = (2, lambda j: columns(qkv_send, j), lambda j: qkv_recv.at[j], qkv_recv)
    DOUT = (3, lambda j: columns(dout_send, j), lambda j: dout_recv.at[j], dout_recv)

    def grads(phase, first, last):
        return (
            phase,
            lambda j: dqkv_send.at[j, first:last],
            lambda j: columns(out.at[first:last], j),
            out.at[first:last],
        )

    GRAD_Q, GRAD_LATE = grads(4, 0, NE), grads(5, 3 * NE, QKV_ROWS)
    GRAD_KV = grads(6, NE, 3 * NE)
    ATT = 7

    exchange(*META)
    exchange(*ROW)
    exchange(*QKV)

    arrive(*META)

    def spread(first, shift):
        lane = iota((N, E), 1)
        mine = (lane >> shift) == iota((N, E), 0)
        wide = jnp.concatenate(
            [jnp.where(mine, meta_recv[j, first : first + 1], 0.0) for j in range(N)], axis=0
        )
        low = (1 << shift) - 1
        same = onehot((iota((E, E), 0) & low) == (iota((E, E), 1) & low))
        wide = dot(wide.astype(BF16), same)
        total = jnp.zeros((N, E), F32)
        for j in range(N):
            total += jnp.where((lane >> shift) == j, wide[j * N : (j + 1) * N], 0.0)
        return total

    token_e = spread(0, 3)
    token_l = spread(4, 2)

    def tables(token, shift, slots, padded):
        peak = 1 << shift
        valid = onehot(token > 0.0)
        src, dst = iota((E, E), 0), iota((E, E), 1)
        offset = dot(valid, onehot((src >> shift) < (dst >> shift)))[0:1].astype(I32)
        in_lane = iota((1, E), 1)
        slot = jnp.where(token[0:1] > 0.0, offset + (in_lane & (peak - 1)), -1)
        select = onehot(iota((padded, E), 0) == slot)
        low = token.astype(BF16)
        high = jnp.where(token > 0.0, (iota((N, E), 1) >> shift).astype(F32), 0.0).astype(BF16)
        cols = dot_nt(select, high) * 256.0 + dot_nt(select, low) - 1.0
        total = N * slots
        mult = 1366 if slots == NE else 2731
        in_row = iota((padded, total), 1)
        tile = onehot(in_row - ((in_row * mult) >> 16) * slots == iota((padded, total), 0))
        wide_high = dot(dot_nt(high, select).astype(BF16), tile)
        wide_low = dot(dot_nt(low, select).astype(BF16), tile)
        in_row = iota((N, total), 1)
        mine = ((in_row * mult) >> 16) == iota((N, total), 0)
        row = jnp.sum(
            jnp.where(mine, wide_high * 256.0 + wide_low - 1.0, 0.0), axis=0, keepdims=True
        )
        src, dst = iota((E, TOK), 0), iota((E, TOK), 1)
        offset = dot(valid, onehot((src >> shift) < (dst >> 4)))[0:1].astype(I32)
        count = dot(valid, onehot((src >> shift) == (dst >> 4)))[0:1].astype(I32)
        in_lane = iota((1, TOK), 1)
        rank = in_lane & (peak - 1)
        slot = jnp.where(rank < count, offset + rank, -1)
        part = (in_lane & 15) >> shift
        return cols, row, slot, part

    cols_e, row_e, slot_e, part_e = tables(token_e, 3, NE, NE)
    cols_l, row_l, slot_l, part_l = tables(token_l, 2, NL, NLP)

    arrive(*ROW)
    for h in range(2):
        pick = onehot((iota((NE, TOK), 0) == slot_e) & (part_e == h))
        got = dot(pick, rows_recv[:, :, 0:1024].reshape(TOK, 1024))
        rows_all[d, 0:NE, h * 1024 : (h + 1) * 1024] = got.astype(BF16)
    for q in range(4):
        pick = onehot((iota((NLP, TOK), 0) == slot_l) & (part_l == q))
        got = dot(pick, rows_recv[:, :, 1024:1536].reshape(TOK, 512))
        rows_all[d, NE:ROWS, q * 512 : (q + 1) * 512] = got.astype(BF16)

    def gather(block, kind, to_dp, half=None):
        part = rows_all.at[block]
        if half is not None:
            part = part.at[:, half * 1024 : (half + 1) * 1024]
        return pltpu.make_async_remote_copy(
            src_ref=part,
            dst_ref=part,
            send_sem=gsend,
            recv_sem=grecv.at[kind],
            device_id=(to_dp, s),
            device_id_type=MESH,
        )

    ahead, behind, far = same_core(1), same_core(3), same_core(2)
    FROM_BEHIND, FROM_AHEAD, FROM_FAR, FROM_PARTNER = range(4)
    gather(d, FROM_BEHIND, ahead).start()
    gather(d, FROM_AHEAD, behind).start()
    gather(d, FROM_PARTNER, partner).start()

    def gather_near():
        wait_bytes(rows_all.at[behind], grecv.at[FROM_BEHIND])
        gather(behind, FROM_FAR, ahead, 1).start()
        gather(behind, FROM_PARTNER, partner).start()
        wait_bytes(rows_all.at[ahead], grecv.at[FROM_AHEAD])
        gather(ahead, FROM_FAR, behind, 0).start()
        gather(ahead, FROM_PARTNER, partner).start()

    def gather_far():
        wait_bytes(rows_all.at[far], grecv.at[FROM_FAR])
        gather(far, FROM_PARTNER, partner).start()

    weight_copy.wait()
    mine = rows_all[d]
    for c in range(8):
        part = dot_nt(mine, wv[c * 256 : (c + 1) * 256, :])
        dout_send[:, c * 256 : (c + 1) * 256] = part.astype(BF16)
    exchange(*DOUT)

    arrive(*QKV)
    gather_near()

    def late(wide, part):
        return wide[:, part * NL : (part + 1) * NL].reshape(KL, E)

    def softmax(query, key, value, row, col):
        scores = dot_nt(query, key) * SCALE
        scores = jnp.where(row <= col, scores, -1e30)
        top = jnp.max(scores, axis=1, keepdims=True)
        weights = jnp.exp(scores - top)
        probs = weights / jnp.sum(weights, axis=1, keepdims=True)
        probs_bf = probs.astype(BF16)
        return probs, probs_bf, dot(probs_bf, value)

    def attended_out(first, last):
        def copy(to):
            return remote(
                att_send.at[to, first:last], att_recv.at[d, parity, first:last], ATT, to, target_dp
            )

        for dz, dy in OTHERS:
            copy(other(dz, dy)).start()

        @pl.when(target_dp == d)
        def _():
            pltpu.make_async_copy(
                att_send.at[s, first:last], att_recv.at[d, parity, first:last], recv.at[ATT]
            ).start()

        @pl.when(target_dp != d)
        def _():
            copy(s).start()

    key_e = qkv_recv[:, NE : 2 * NE, :].reshape(KE, E)
    value_e = qkv_recv[:, 2 * NE : 3 * NE, :].reshape(KE, E)
    for b in range(4):
        query = qkv_recv[4 * b : 4 * b + 4, 0:NE, :].reshape(4 * NE, E)
        col = jnp.concatenate([cols_e[:, o : o + 1] for o in range(4 * b, 4 * b + 4)], axis=0)
        probs, probs_bf, attended = softmax(query, key_e, value_e, row_e, col)
        probs_e[b * 192 : (b + 1) * 192] = probs
        probs_bf_e[b * 192 : (b + 1) * 192] = probs_bf
        att_send[4 * b : 4 * b + 4, 0:NE, :] = attended.reshape(4, NE, E).astype(BF16)
    attended_out(0, NE)
    wide = qkv_recv[:, 3 * NE : QKV_ROWS, :].astype(F32)
    query_l, key_l, value_l = (late(wide, part).astype(BF16) for part in range(3))
    gap = jnp.zeros((8, NLP - NL, E), F32)
    for b in range(2):
        query = query_l[b * 192 : (b + 1) * 192]
        col = jnp.concatenate([cols_l[0:NL, o : o + 1] for o in range(8 * b, 8 * b + 8)], axis=0)
        probs, probs_bf, attended = softmax(query, key_l, value_l, row_l, col)
        probs_l[b * 192 : (b + 1) * 192] = probs
        probs_bf_l[b * 192 : (b + 1) * 192] = probs_bf
        attended = jnp.concatenate([attended.reshape(8, NL, E), gap], axis=1)
        att_send[8 * b : 8 * b + 8, NE:ROWS, :] = attended.astype(BF16)
    attended_out(NE, ROWS)

    arrive(*DOUT)

    def backward(query, key, value, dout, attended, probs):
        delta = jnp.sum(dout.astype(F32) * attended.astype(F32), axis=1, keepdims=True)
        dprobs = dot_nt(dout, value)
        dscores = (probs * (dprobs - delta)).astype(BF16)
        return dscores, dot(dscores, key) * SCALE

    for b in range(4):
        dout = dout_recv[4 * b : 4 * b + 4, 0:NE, :].reshape(192, E)
        attended = att_send[4 * b : 4 * b + 4, 0:NE, :].reshape(192, E)
        query = None
        dscores, dquery = backward(
            query, key_e, value_e, dout, attended, probs_e[b * 192 : (b + 1) * 192]
        )
        ds_e[b * 192 : (b + 1) * 192] = dscores
        dqkv_send[4 * b : 4 * b + 4, 0:NE, :] = dquery.reshape(4, NE, E).astype(BF16)
    exchange(*GRAD_Q)
    dout_l = late(dout_recv[:, NE:ROWS, :].astype(F32), 0).astype(BF16)
    attended_l = late(att_send[:, NE:ROWS, :].astype(F32), 0)
    dquery_l = []
    for b in range(2):
        dscores, dquery = backward(
            None, key_l, value_l, dout_l[b * 192 : (b + 1) * 192],
            attended_l[b * 192 : (b + 1) * 192], probs_l[b * 192 : (b + 1) * 192]
        )
        ds_l[b * 192 : (b + 1) * 192] = dscores
        dquery_l.append(dquery)
    query_e = qkv_recv[:, 0:NE, :].reshape(KE, E)
    dout_e = dout_recv[:, 0:NE, :].reshape(KE, E)
    for c in range(2):
        dkey = dot_tn(ds_e[:, c * 384 : (c + 1) * 384], query_e) * SCALE
        dqkv_send[8 * c : 8 * c + 8, NE : 2 * NE, :] = dkey.reshape(8, NE, E).astype(BF16)
        dvalue = dot_tn(probs_bf_e[:, c * 384 : (c + 1) * 384], dout_e)
        dqkv_send[8 * c : 8 * c + 8, 2 * NE : 3 * NE, :] = dvalue.reshape(8, NE, E).astype(BF16)
    dquery = jnp.concatenate(dquery_l, axis=0)
    dkey = dot_tn(ds_l[...], query_l) * SCALE
    dvalue = dot_tn(probs_bf_l[...], dout_l)
    parts = [part.reshape(N, NL, E) for part in (dquery, dkey, dvalue)]
    parts.append(jnp.zeros((N, 8, E), F32))
    dqkv_send[:, 3 * NE : QKV_ROWS, :] = jnp.concatenate(parts, axis=1).astype(BF16)
    exchange(*GRAD_LATE)
    gather_far()

    wait_bytes(att_recv, recv.at[ATT])
    wait_bytes(rows_all.at[0:4], grecv.at[FROM_PARTNER])
    rows = rows_all[...].reshape(DP * ROWS, W)
    for p in range(2):
        attended = att_recv[:, p].reshape(DP * ROWS, E)
        for c in range(4):
            half, cut = c // 2, slice((c % 2) * 512, (c % 2) * 512 + 512)
            part = dot_tn(attended, rows[:, c * 512 : (c + 1) * 512])
            part = part.reshape(2, 4, 16, 512).astype(BF16)
            if half == 0:
                sum1_send[0, 2 * p : 2 * p + 2, :, :, cut] = part
            else:
                for i in range(2):
                    for j in range(4):
                        sum1_send[1, j, 2 * p + i, :, cut] = part[i, j]

    def along(half, stage, i):
        if half == stage:
            to = lax.rem(z + i, 4)
            return to, to * 4 + y
        to = lax.rem(y + i, 4)
        return to, z * 4 + to

    def sum_copy(half, stage, i):
        source, target = (sum1_send, sum1_recv) if stage == 0 else (sum2_send, sum2_recv)
        to, device = along(half, stage, i)
        return pltpu.make_async_remote_copy(
            src_ref=source.at[half, to],
            dst_ref=target.at[half, i - 1],
            send_sem=sum_send.at[stage],
            recv_sem=sum_recv.at[stage, half],
            device_id=(d, device),
            device_id_type=MESH,
        )

    for i in (2, 1, 3):
        for half in range(2):
            sum_copy(half, 0, i).start()
    exchange(*GRAD_KV)
    for half in range(2):
        wait_bytes(sum1_recv.at[half], sum_recv.at[0, half])
        total = sum1_send[half, z if half == 0 else y].astype(F32)
        for i in range(3):
            total += sum1_recv[half, i].astype(F32)
        sum2_send[half] = total.astype(BF16)
        for i in (2, 1, 3):
            sum_copy(half, 1, i).start()

    wait_bytes(meta_recv.at[1:N], send.at[META[0]])
    wait_bytes(rows_recv.at[1:N], send.at[ROW[0]])
    wait_bytes(qkv_recv.at[1:N], send.at[QKV[0]])
    wait_bytes(dout_recv.at[1:N], send.at[DOUT[0]])

    @pl.when(target_dp == d)
    def _():
        wait_bytes(att_send.at[1:N], send.at[ATT])

    @pl.when(target_dp != d)
    def _():
        wait_bytes(att_send, send.at[ATT])

    wait_bytes(rows_all.at[1:DP], gsend)
    wait_bytes(sum1_recv, sum_send.at[0])

    for half in range(2):
        wait_bytes(sum2_recv.at[half], sum_recv.at[1, half])
        total = sum2_send[half, y if half == 0 else z].astype(F32)
        for i in range(3):
            total += sum2_recv[half, i].astype(F32)
        dw_v[:, half * 1024 : (half + 1) * 1024] = total
    dw_copy = pltpu.make_async_copy(dw_v, dw, local_sem.at[0])
    dw_copy.start()
    wait_bytes(sum2_recv, sum_send.at[1])
    for grad, (first, last) in (
        (GRAD_Q, (0, NE)),
        (GRAD_LATE, (3 * NE, QKV_ROWS)),
        (GRAD_KV, (NE, 3 * NE)),
    ):
        wait_bytes(dqkv_send.at[1:N, first:last], send.at[grad[0]])
        arrive(*grad)
    dw_copy.wait()


def finish(
    grads, dw, dquery_early, dkeyval_early, dquery_late, dkeyval_late, dweight,
    early_v, query_v, late_v, dw_v, dkve_v, dql_v, dkvl_v, sem,
):
    loads = [
        pltpu.make_async_copy(source, target, sem.at[i])
        for i, (source, target) in enumerate(
            (
                (grads.at[NE : 3 * NE], early_v),
                (grads.at[3 * NE : QKV_ROWS], late_v),
                (grads.at[0:NE], query_v.at[0]),
                (dw, dw_v),
            )
        )
    ]
    for copy in loads:
        copy.start()
    stores = []

    def store(source, target):
        stores.append(pltpu.make_async_copy(source, target, sem.at[4 + len(stores)]))
        stores[-1].start()

    loads[0].wait()
    dkve_v[0] = jnp.stack([early_v[0:NE], early_v[NE : 2 * NE]], axis=1)
    store(dkve_v, dkeyval_early)
    loads[1].wait()
    late = late_v[...].astype(F32)
    dkvl_v[0] = jnp.stack(
        [late[NL : 2 * NL].astype(BF16), late[2 * NL : 3 * NL].astype(BF16)], axis=1
    )
    store(dkvl_v, dkeyval_late)
    dql_v[0] = late[0:NL].astype(BF16)
    store(dql_v, dquery_late)
    loads[2].wait()
    store(query_v, dquery_early)
    loads[3].wait()
    store(dw_v, dweight)
    for copy in stores:
        copy.wait()


def shards(
    depths, owners, cotangent, query_early, keyval_early, query_late, keyval_late, out_weight
):
    hbm = pl.BlockSpec(memory_space=pl.ANY)
    results = (
        jax.ShapeDtypeStruct(query_early.shape, BF16),
        jax.ShapeDtypeStruct(keyval_early.shape, BF16),
        jax.ShapeDtypeStruct(query_late.shape, BF16),
        jax.ShapeDtypeStruct(keyval_late.shape, BF16),
        jax.ShapeDtypeStruct((N, W), F32),
    )
    grads, dw = pl.pallas_call(
        kernel,
        out_shape=(jax.ShapeDtypeStruct((QKV_ROWS, W), BF16), results[4]),
        in_specs=[hbm] * 8,
        out_specs=(hbm,) * 2,
        scratch_shapes=[
            pltpu.VMEM((1, TOK), I32),
            pltpu.VMEM((2, 1, TOK), I32),
            pltpu.VMEM((2, TOK, W), BF16),
            pltpu.VMEM((W, W), BF16),
            pltpu.VMEM((1, NL, W), BF16),
            pltpu.VMEM((1, NE, 2, W), BF16),
            pltpu.VMEM((1, NL, 2, W), BF16),
            pltpu.VMEM((QKV_ROWS, W), BF16),
            pltpu.VMEM((N, 16, 1536), BF16),
            pltpu.VMEM((N, 16, 1536), BF16),
            pltpu.VMEM((8, E), F32),
            pltpu.VMEM((N, 8, E), F32),
            pltpu.VMEM((N, QKV_ROWS, E), BF16),
            pltpu.VMEM((DP, ROWS, W), BF16),
            pltpu.VMEM((ROWS, W), BF16),
            pltpu.VMEM((N, ROWS, E), BF16),
            pltpu.VMEM((N, ROWS, E), BF16),
            pltpu.VMEM((DP, 2, ROWS, E), BF16),
            pltpu.VMEM((N, QKV_ROWS, E), BF16),
            pltpu.VMEM((2, 4, 4, 16, W // 2), BF16),
            pltpu.VMEM((2, 3, 4, 16, W // 2), BF16),
            pltpu.VMEM((2, 4, 16, W // 2), BF16),
            pltpu.VMEM((2, 3, 16, W // 2), BF16),
            pltpu.VMEM((N, W), F32),
            pltpu.VMEM((KE, KE), F32),
            pltpu.VMEM((KE, KE), BF16),
            pltpu.VMEM((KE, KE), BF16),
            pltpu.VMEM((KL, KL), F32),
            pltpu.VMEM((KL, KL), BF16),
            pltpu.VMEM((KL, KL), BF16),
            pltpu.SemaphoreType.DMA((8,)),
            pltpu.SemaphoreType.DMA((8,)),
            pltpu.SemaphoreType.DMA((8,)),
            pltpu.SemaphoreType.DMA,
            pltpu.SemaphoreType.DMA((4,)),
            pltpu.SemaphoreType.DMA((2,)),
            pltpu.SemaphoreType.DMA((2, 2)),
        ],
        compiler_params=pltpu.CompilerParams(
            collective_id=0, has_side_effects=True, vmem_limit_bytes=56 * 1024 * 1024
        ),
        cost_estimate=pl.CostEstimate(
            flops=3_000_000_000, bytes_accessed=20_000_000, transcendentals=800_000
        ),
        name="rows_attention_weight",
    )(
        depths, owners, cotangent[:, 0], query_early, keyval_early, query_late, keyval_late,
        out_weight,
    )
    return pl.pallas_call(
        finish,
        out_shape=results,
        in_specs=[pl.BlockSpec(memory_space=pltpu.HBM)] * 2,
        out_specs=(hbm,) * 5,
        scratch_shapes=[
            pltpu.VMEM((2 * NE, W), BF16),
            pltpu.VMEM((1, NE, W), BF16),
            pltpu.VMEM((80, W), BF16),
            pltpu.VMEM((N, W), F32),
            pltpu.VMEM((1, NE, 2, W), BF16),
            pltpu.VMEM((1, NL, W), BF16),
            pltpu.VMEM((1, NL, 2, W), BF16),
            pltpu.SemaphoreType.DMA((9,)),
        ],
        compiler_params=pltpu.CompilerParams(vmem_limit_bytes=48 * 1024 * 1024),
        name="outputs",
    )(grads, dw)


def solution(mesh):
    in_specs = (
        P("dp", "seq"),
        P(None, "dp", "seq"),
        P(None, "dp", "seq", None),
        P("dp", "seq", None),
        P("dp", "seq", None, None),
        P("dp", "seq", None),
        P("dp", "seq", None, None),
        P(),
    )
    out_specs = (
        P("dp", "seq", None),
        P("dp", "seq", None, None),
        P("dp", "seq", None),
        P("dp", "seq", None, None),
        P(("dp", "seq"), None),
    )
    return jax.shard_map(shards, mesh=mesh, in_specs=in_specs, out_specs=out_specs, check_vma=False)
```

```python
import jax
import jax.numpy as jnp
from jax import lax
from jax.experimental import pallas as pl
from jax.experimental.pallas import tpu as pltpu
from jax.sharding import PartitionSpec as P

MESH = pl.DeviceIdType.MESH
F32, BF16, I32 = jnp.float32, jnp.bfloat16, jnp.int32

N = 16
DP = 8
E = 128
W = 2048
TOK = 256
NE, NL = 48, 24
NLP = 32
ROWS = NE + NLP
QKV_ROWS = 3 * NE + 80
OTHERS = (
    (2, 2), (1, 2), (2, 1), (2, 3), (3, 2), (0, 2), (2, 0), (1, 1),
    (3, 3), (1, 3), (3, 1), (0, 1), (1, 0), (0, 3), (3, 0),
)
KE, KL = N * NE, N * NL
SCALE = E**-0.5


def dot(a, b):
    return lax.dot_general(a, b, (((1,), (0,)), ((), ())), preferred_element_type=F32)


def dot_nt(a, b):
    return lax.dot_general(a, b, (((1,), (1,)), ((), ())), preferred_element_type=F32)


def dot_tn(a, b):
    return lax.dot_general(a, b, (((0,), (0,)), ((), ())), preferred_element_type=F32)


def iota(shape, dim):
    return lax.broadcasted_iota(I32, shape, dim)


def onehot(mask):
    return jnp.where(mask, 1.0, 0.0).astype(BF16)


def kernel(
    depths, owners, cot, query_early, keyval_early, query_late, keyval_late, weight,
    dquery_early, dkeyval_early, dquery_late, dkeyval_late, dw,
    depth_v, owner_v, cotv, wv, ql_v, kve_v, kvl_v, qkv_send,
    rows_send, rows_recv, meta_send, meta_recv, qkv_recv, rows_all,
    dout_send, dout_recv, att_send, att_recv, dqkv_send,
    sum1_send, sum1_recv, sum2_send, sum2_recv,
    out, dkve_v, dql_v, dkvl_v, dw_v,
    probs_e, probs_bf_e, ds_e, probs_l, probs_bf_l, ds_l,
    local_sem, send, recv, gsend, grecv, sum_send, sum_recv,
):
    d = lax.axis_index("dp")
    s = lax.axis_index("seq")
    chip = lax.div(d, 2)
    core = lax.rem(d, 2)
    partner = chip * 2 + 1 - core
    z, y = lax.div(s, 4), lax.rem(s, 4)

    def head_of(j):
        return lax.rem(chip + lax.div(j, 4) + 2 * core, 4) * 4 + lax.rem(j, 4)

    def holder(of_dp, head):
        turn = lax.div(head, 4) + 8 - lax.div(of_dp, 2) - 2 * lax.rem(of_dp, 2)
        return lax.rem(turn, 4) * 4 + lax.rem(head, 4)

    def same_core(i):
        return lax.rem(chip + i, 4) * 2 + core

    my_head = head_of(s)
    target_dp = lax.div(my_head, 2)
    parity = lax.rem(my_head, 2)

    cot_copy = pltpu.make_async_copy(cot, cotv, local_sem.at[0])
    weight_copy = pltpu.make_async_copy(weight, wv, local_sem.at[1])
    routing = [
        pltpu.make_async_copy(depths, depth_v, local_sem.at[6]),
        pltpu.make_async_copy(owners, owner_v, local_sem.at[7]),
    ]
    operands = [
        pltpu.make_async_copy(keyval_early, kve_v, local_sem.at[2]),
        pltpu.make_async_copy(query_late, ql_v, local_sem.at[5]),
        pltpu.make_async_copy(keyval_late, kvl_v, local_sem.at[3]),
        pltpu.make_async_copy(query_early.at[0], qkv_send.at[0:NE], local_sem.at[4]),
    ]
    for copy in routing + [cot_copy] + operands + [weight_copy]:
        copy.start()

    barrier = pltpu.get_barrier_semaphore()

    def greet(to_dp, to_seq):
        pl.semaphore_signal(barrier, inc=1, device_id=(to_dp, to_seq), device_id_type=MESH)

    def greet_seq(i, _):
        greet(d, lax.rem(s + i, N))
        return 0

    lax.fori_loop(1, N, greet_seq, 0)
    greet(partner, s)
    for i in (1, 3):
        greet(same_core(i), s)

    def greet_heads(i, _):
        from_dp = lax.div(i, 2)
        from_seq = holder(from_dp, 2 * d + lax.rem(i, 2))

        @pl.when(jnp.logical_or(from_dp != d, from_seq != s))
        def _():
            greet(from_dp, from_seq)

        return 0

    lax.fori_loop(0, 2 * DP, greet_heads, 0)

    for copy in routing:
        copy.wait()
    depth = depth_v[...]
    active_e, active_l = depth > 1, depth > 2
    owner_e, owner_l = owner_v[0], owner_v[1]
    flags = jnp.where(
        iota((16, TOK), 0) < 8,
        jnp.broadcast_to(active_e.astype(F32), (16, TOK)),
        jnp.broadcast_to(active_l.astype(F32), (16, TOK)),
    ).astype(BF16)
    below = onehot(iota((TOK, TOK), 0) < iota((TOK, TOK), 1))
    before = dot(flags, below).astype(I32)
    rank_e, rank_l = before[0:1] >> 4, before[8:9] >> 4
    token = (iota((8, TOK), 1) + 1).astype(F32).astype(BF16)
    line = iota((E, TOK), 0)
    meta_e = dot_nt(token, onehot((line == owner_e * 8 + rank_e) & active_e))
    meta_l = dot_nt(token, onehot((line == owner_l * 4 + rank_l) & active_l))
    meta_send[...] = jnp.where(iota((8, E), 0) < 4, meta_e, meta_l)

    cot_copy.wait()
    line = iota((TOK, TOK), 0)
    base = jnp.where(active_e, owner_e * 16 + rank_e, -64)
    packed = dot(onehot(line == base), cotv[0, :, 0:1024])
    packed += dot(onehot(line == base + 8), cotv[0, :, 1024:2048])
    rows_send[:, :, 0:1024] = packed.reshape(N, 16, 1024).astype(BF16)
    base = jnp.where(active_l, owner_l * 16 + rank_l, -64)
    packed = dot(onehot(line == base), cotv[1, :, 0:512])
    for q in range(1, 4):
        packed += dot(onehot(line == base + 4 * q), cotv[1, :, q * 512 : (q + 1) * 512])
    rows_send[:, :, 1024:1536] = packed.reshape(N, 16, 512).astype(BF16)

    elsewhere = jnp.where(target_dp == d, 0, 1)
    pl.semaphore_wait(barrier, N - 1 + 3 + N - 1 + elsewhere)

    def remote(src, dst, phase, to, to_dp):
        return pltpu.make_async_remote_copy(
            src_ref=src,
            dst_ref=dst,
            send_sem=send.at[phase],
            recv_sem=recv.at[phase],
            device_id=(to_dp, to),
            device_id_type=MESH,
        )

    def wait_bytes(ref, sem):
        pltpu.make_async_copy(ref, ref, sem).wait()

    def other(dz, dy):
        to_z = lax.rem(z + jnp.where(core == 0, dz, 4 - dz), 4)
        to_y = lax.rem(y + jnp.where(core == 0, dy, 4 - dy), 4)
        return to_z * 4 + to_y

    def exchange(phase, src, dst, whole):
        for dz, dy in OTHERS:
            to = other(dz, dy)
            remote(src(to), dst(s), phase, to, d).start()
        pltpu.make_async_copy(src(s), dst(s), recv.at[phase]).start()

    def arrive(phase, src, dst, whole):
        wait_bytes(whole, recv.at[phase])

    def columns(ref, j):
        return ref.at[:, pl.ds(pl.multiple_of(head_of(j) * E, E), E)]

    META = (0, lambda j: meta_send, lambda j: meta_recv.at[j], meta_recv)
    ROW = (1, lambda j: rows_send.at[j], lambda j: rows_recv.at[j], rows_recv)
    QKV = (2, lambda j: columns(qkv_send, j), lambda j: qkv_recv.at[j], qkv_recv)
    DOUT = (3, lambda j: columns(dout_send, j), lambda j: dout_recv.at[j], dout_recv)

    def grads(phase, first, last):
        return (
            phase,
            lambda j: dqkv_send.at[j, first:last],
            lambda j: columns(out.at[first:last], j),
            out.at[first:last],
        )

    GRAD_Q, GRAD_LATE = grads(4, 0, NE), grads(5, 3 * NE, QKV_ROWS)
    GRAD_KV = grads(6, NE, 3 * NE)
    ATT = 7

    exchange(*META)
    exchange(*ROW)
    for copy in operands:
        copy.wait()
    qkv_send[NE : 2 * NE] = kve_v[0, :, 0, :]
    qkv_send[2 * NE : 3 * NE] = kve_v[0, :, 1, :]
    for c in range(4):
        cut = slice(c * 512, (c + 1) * 512)
        pair = kvl_v[0, :, :, cut].astype(F32)
        qkv_send[3 * NE : QKV_ROWS, cut] = jnp.concatenate(
            [ql_v[0, :, cut].astype(F32), pair[:, 0], pair[:, 1], jnp.zeros((8, 512), F32)], axis=0
        ).astype(BF16)
    exchange(*QKV)

    arrive(*META)

    def spread(first, shift):
        lane = iota((N, E), 1)
        mine = (lane >> shift) == iota((N, E), 0)
        wide = jnp.concatenate(
            [jnp.where(mine, meta_recv[j, first : first + 1], 0.0) for j in range(N)], axis=0
        )
        low = (1 << shift) - 1
        same = onehot((iota((E, E), 0) & low) == (iota((E, E), 1) & low))
        wide = dot(wide.astype(BF16), same)
        total = jnp.zeros((N, E), F32)
        for j in range(N):
            total += jnp.where((lane >> shift) == j, wide[j * N : (j + 1) * N], 0.0)
        return total

    token_e = spread(0, 3)
    token_l = spread(4, 2)

    def tables(token, shift, slots, padded):
        peak = 1 << shift
        valid = onehot(token > 0.0)
        src, dst = iota((E, E), 0), iota((E, E), 1)
        offset = dot(valid, onehot((src >> shift) < (dst >> shift)))[0:1].astype(I32)
        in_lane = iota((1, E), 1)
        slot = jnp.where(token[0:1] > 0.0, offset + (in_lane & (peak - 1)), -1)
        select = onehot(iota((padded, E), 0) == slot)
        low = token.astype(BF16)
        high = jnp.where(token > 0.0, (iota((N, E), 1) >> shift).astype(F32), 0.0).astype(BF16)
        cols = dot_nt(select, high) * 256.0 + dot_nt(select, low) - 1.0
        total = N * slots
        mult = 1366 if slots == NE else 2731
        in_row = iota((padded, total), 1)
        tile = onehot(in_row - ((in_row * mult) >> 16) * slots == iota((padded, total), 0))
        wide_high = dot(dot_nt(high, select).astype(BF16), tile)
        wide_low = dot(dot_nt(low, select).astype(BF16), tile)
        in_row = iota((N, total), 1)
        mine = ((in_row * mult) >> 16) == iota((N, total), 0)
        row = jnp.sum(
            jnp.where(mine, wide_high * 256.0 + wide_low - 1.0, 0.0), axis=0, keepdims=True
        )
        src, dst = iota((E, TOK), 0), iota((E, TOK), 1)
        offset = dot(valid, onehot((src >> shift) < (dst >> 4)))[0:1].astype(I32)
        count = dot(valid, onehot((src >> shift) == (dst >> 4)))[0:1].astype(I32)
        in_lane = iota((1, TOK), 1)
        rank = in_lane & (peak - 1)
        slot = jnp.where(rank < count, offset + rank, -1)
        part = (in_lane & 15) >> shift
        return cols, row, slot, part

    cols_e, row_e, slot_e, part_e = tables(token_e, 3, NE, NE)
    cols_l, row_l, slot_l, part_l = tables(token_l, 2, NL, NLP)

    arrive(*ROW)
    for h in range(2):
        pick = onehot((iota((NE, TOK), 0) == slot_e) & (part_e == h))
        got = dot(pick, rows_recv[:, :, 0:1024].reshape(TOK, 1024))
        rows_all[d, 0:NE, h * 1024 : (h + 1) * 1024] = got.astype(BF16)
    for q in range(4):
        pick = onehot((iota((NLP, TOK), 0) == slot_l) & (part_l == q))
        got = dot(pick, rows_recv[:, :, 1024:1536].reshape(TOK, 512))
        rows_all[d, NE:ROWS, q * 512 : (q + 1) * 512] = got.astype(BF16)

    def gather(block, kind, to_dp, half=None):
        part = rows_all.at[block]
        if half is not None:
            part = part.at[:, half * 1024 : (half + 1) * 1024]
        return pltpu.make_async_remote_copy(
            src_ref=part,
            dst_ref=part,
            send_sem=gsend,
            recv_sem=grecv.at[kind],
            device_id=(to_dp, s),
            device_id_type=MESH,
        )

    ahead, behind, far = same_core(1), same_core(3), same_core(2)
    FROM_BEHIND, FROM_AHEAD, FROM_FAR, FROM_PARTNER = range(4)
    gather(d, FROM_BEHIND, ahead).start()
    gather(d, FROM_AHEAD, behind).start()
    gather(d, FROM_PARTNER, partner).start()

    def gather_near():
        wait_bytes(rows_all.at[behind], grecv.at[FROM_BEHIND])
        gather(behind, FROM_FAR, ahead, 1).start()
        gather(behind, FROM_PARTNER, partner).start()
        wait_bytes(rows_all.at[ahead], grecv.at[FROM_AHEAD])
        gather(ahead, FROM_FAR, behind, 0).start()
        gather(ahead, FROM_PARTNER, partner).start()

    def gather_far():
        wait_bytes(rows_all.at[far], grecv.at[FROM_FAR])
        gather(far, FROM_PARTNER, partner).start()

    weight_copy.wait()
    mine = rows_all[d]
    for c in range(8):
        part = dot_nt(mine, wv[c * 256 : (c + 1) * 256, :])
        dout_send[:, c * 256 : (c + 1) * 256] = part.astype(BF16)
    exchange(*DOUT)

    arrive(*QKV)
    gather_near()

    def late(wide, part):
        return wide[:, part * NL : (part + 1) * NL].reshape(KL, E)

    def softmax(query, key, value, row, col):
        scores = dot_nt(query, key) * SCALE
        scores = jnp.where(row <= col, scores, -1e30)
        top = jnp.max(scores, axis=1, keepdims=True)
        weights = jnp.exp(scores - top)
        probs = weights / jnp.sum(weights, axis=1, keepdims=True)
        probs_bf = probs.astype(BF16)
        return probs, probs_bf, dot(probs_bf, value)

    def attended_out(first, last):
        def copy(to):
            return remote(
                att_send.at[to, first:last], att_recv.at[d, parity, first:last], ATT, to, target_dp
            )

        for dz, dy in OTHERS:
            copy(other(dz, dy)).start()

        @pl.when(target_dp == d)
        def _():
            pltpu.make_async_copy(
                att_send.at[s, first:last], att_recv.at[d, parity, first:last], recv.at[ATT]
            ).start()

        @pl.when(target_dp != d)
        def _():
            copy(s).start()

    key_e = qkv_recv[:, NE : 2 * NE, :].reshape(KE, E)
    value_e = qkv_recv[:, 2 * NE : 3 * NE, :].reshape(KE, E)
    for b in range(4):
        query = qkv_recv[4 * b : 4 * b + 4, 0:NE, :].reshape(4 * NE, E)
        col = jnp.concatenate([cols_e[:, o : o + 1] for o in range(4 * b, 4 * b + 4)], axis=0)
        probs, probs_bf, attended = softmax(query, key_e, value_e, row_e, col)
        probs_e[b * 192 : (b + 1) * 192] = probs
        probs_bf_e[b * 192 : (b + 1) * 192] = probs_bf
        att_send[4 * b : 4 * b + 4, 0:NE, :] = attended.reshape(4, NE, E).astype(BF16)
    attended_out(0, NE)
    wide = qkv_recv[:, 3 * NE : QKV_ROWS, :].astype(F32)
    query_l, key_l, value_l = (late(wide, part).astype(BF16) for part in range(3))
    gap = jnp.zeros((8, NLP - NL, E), F32)
    for b in range(2):
        query = query_l[b * 192 : (b + 1) * 192]
        col = jnp.concatenate([cols_l[0:NL, o : o + 1] for o in range(8 * b, 8 * b + 8)], axis=0)
        probs, probs_bf, attended = softmax(query, key_l, value_l, row_l, col)
        probs_l[b * 192 : (b + 1) * 192] = probs
        probs_bf_l[b * 192 : (b + 1) * 192] = probs_bf
        attended = jnp.concatenate([attended.reshape(8, NL, E), gap], axis=1)
        att_send[8 * b : 8 * b + 8, NE:ROWS, :] = attended.astype(BF16)
    attended_out(NE, ROWS)

    arrive(*DOUT)

    def backward(query, key, value, dout, attended, probs):
        delta = jnp.sum(dout.astype(F32) * attended.astype(F32), axis=1, keepdims=True)
        dprobs = dot_nt(dout, value)
        dscores = (probs * (dprobs - delta)).astype(BF16)
        return dscores, dot(dscores, key) * SCALE

    for b in range(4):
        dout = dout_recv[4 * b : 4 * b + 4, 0:NE, :].reshape(192, E)
        attended = att_send[4 * b : 4 * b + 4, 0:NE, :].reshape(192, E)
        query = None
        dscores, dquery = backward(
            query, key_e, value_e, dout, attended, probs_e[b * 192 : (b + 1) * 192]
        )
        ds_e[b * 192 : (b + 1) * 192] = dscores
        dqkv_send[4 * b : 4 * b + 4, 0:NE, :] = dquery.reshape(4, NE, E).astype(BF16)
    exchange(*GRAD_Q)
    dout_l = late(dout_recv[:, NE:ROWS, :].astype(F32), 0).astype(BF16)
    attended_l = late(att_send[:, NE:ROWS, :].astype(F32), 0)
    dquery_l = []
    for b in range(2):
        dscores, dquery = backward(
            None, key_l, value_l, dout_l[b * 192 : (b + 1) * 192],
            attended_l[b * 192 : (b + 1) * 192], probs_l[b * 192 : (b + 1) * 192]
        )
        ds_l[b * 192 : (b + 1) * 192] = dscores
        dquery_l.append(dquery)
    query_e = qkv_recv[:, 0:NE, :].reshape(KE, E)
    dout_e = dout_recv[:, 0:NE, :].reshape(KE, E)
    for c in range(2):
        dkey = dot_tn(ds_e[:, c * 384 : (c + 1) * 384], query_e) * SCALE
        dqkv_send[8 * c : 8 * c + 8, NE : 2 * NE, :] = dkey.reshape(8, NE, E).astype(BF16)
        dvalue = dot_tn(probs_bf_e[:, c * 384 : (c + 1) * 384], dout_e)
        dqkv_send[8 * c : 8 * c + 8, 2 * NE : 3 * NE, :] = dvalue.reshape(8, NE, E).astype(BF16)
    dquery = jnp.concatenate(dquery_l, axis=0)
    dkey = dot_tn(ds_l[...], query_l) * SCALE
    dvalue = dot_tn(probs_bf_l[...], dout_l)
    parts = [part.reshape(N, NL, E) for part in (dquery, dkey, dvalue)]
    parts.append(jnp.zeros((N, 8, E), F32))
    dqkv_send[:, 3 * NE : QKV_ROWS, :] = jnp.concatenate(parts, axis=1).astype(BF16)
    exchange(*GRAD_LATE)
    gather_far()

    wait_bytes(att_recv, recv.at[ATT])
    wait_bytes(rows_all.at[0:4], grecv.at[FROM_PARTNER])
    rows = rows_all[...].reshape(DP * ROWS, W)
    for p in range(2):
        attended = att_recv[:, p].reshape(DP * ROWS, E)
        for c in range(4):
            half, cut = c // 2, slice((c % 2) * 512, (c % 2) * 512 + 512)
            part = dot_tn(attended, rows[:, c * 512 : (c + 1) * 512])
            part = part.reshape(2, 4, 16, 512).astype(BF16)
            if half == 0:
                sum1_send[0, 2 * p : 2 * p + 2, :, :, cut] = part
            else:
                for i in range(2):
                    for j in range(4):
                        sum1_send[1, j, 2 * p + i, :, cut] = part[i, j]

    def along(half, stage, i):
        if half == stage:
            to = lax.rem(z + i, 4)
            return to, to * 4 + y
        to = lax.rem(y + i, 4)
        return to, z * 4 + to

    def sum_copy(half, stage, i):
        source, target = (sum1_send, sum1_recv) if stage == 0 else (sum2_send, sum2_recv)
        to, device = along(half, stage, i)
        return pltpu.make_async_remote_copy(
            src_ref=source.at[half, to],
            dst_ref=target.at[half, i - 1],
            send_sem=sum_send.at[stage],
            recv_sem=sum_recv.at[stage, half],
            device_id=(d, device),
            device_id_type=MESH,
        )

    for i in (2, 1, 3):
        for half in range(2):
            sum_copy(half, 0, i).start()
    exchange(*GRAD_KV)
    for half in range(2):
        wait_bytes(sum1_recv.at[half], sum_recv.at[0, half])
        total = sum1_send[half, z if half == 0 else y].astype(F32)
        for i in range(3):
            total += sum1_recv[half, i].astype(F32)
        sum2_send[half] = total.astype(BF16)
        for i in (2, 1, 3):
            sum_copy(half, 1, i).start()

    wait_bytes(meta_recv.at[1:N], send.at[META[0]])
    wait_bytes(rows_recv.at[1:N], send.at[ROW[0]])
    wait_bytes(qkv_recv.at[1:N], send.at[QKV[0]])
    wait_bytes(dout_recv.at[1:N], send.at[DOUT[0]])

    @pl.when(target_dp == d)
    def _():
        wait_bytes(att_send.at[1:N], send.at[ATT])

    @pl.when(target_dp != d)
    def _():
        wait_bytes(att_send, send.at[ATT])

    wait_bytes(rows_all.at[1:DP], gsend)
    wait_bytes(sum1_recv, sum_send.at[0])

    writes = []

    def write(source, target):
        writes.append(pltpu.make_async_copy(source, target, local_sem.at[len(writes)]))
        writes[-1].start()

    arrive(*GRAD_Q)
    write(out.at[0:NE], dquery_early.at[0])
    arrive(*GRAD_LATE)
    for c in range(4):
        cut = slice(c * 512, (c + 1) * 512)
        wide = out[3 * NE : QKV_ROWS, cut].astype(F32)
        dql_v[0, :, cut] = wide[0:NL].astype(BF16)
        dkvl_v[0, :, :, cut] = jnp.stack(
            [wide[NL : 2 * NL].astype(BF16), wide[2 * NL : 3 * NL].astype(BF16)], axis=1
        )
    write(dql_v, dquery_late)
    write(dkvl_v, dkeyval_late)
    arrive(*GRAD_KV)
    dkve_v[0] = jnp.stack([out[NE : 2 * NE], out[2 * NE : 3 * NE]], axis=1)
    write(dkve_v, dkeyval_early)
    for half in range(2):
        wait_bytes(sum2_recv.at[half], sum_recv.at[1, half])
        total = sum2_send[half, y if half == 0 else z].astype(F32)
        for i in range(3):
            total += sum2_recv[half, i].astype(F32)
        dw_v[:, half * 1024 : (half + 1) * 1024] = total
    write(dw_v, dw)
    wait_bytes(sum2_recv, sum_send.at[1])
    for grad, (first, last) in (
        (GRAD_Q, (0, NE)),
        (GRAD_LATE, (3 * NE, QKV_ROWS)),
        (GRAD_KV, (NE, 3 * NE)),
    ):
        wait_bytes(dqkv_send.at[1:N, first:last], send.at[grad[0]])
    for copy in writes:
        copy.wait()


def finish(*refs):
    sources, targets, held, sem = refs[0:5], refs[5:10], refs[10:15], refs[15]
    loads = [pltpu.make_async_copy(sources[i], held[i], sem.at[i]) for i in range(5)]
    stores = [pltpu.make_async_copy(held[i], targets[i], sem.at[5 + i]) for i in range(5)]
    for copy in loads:
        copy.start()
    for load, store in zip(loads, stores, strict=True):
        load.wait()
        store.start()
    for copy in stores:
        copy.wait()


def shards(
    depths, owners, cotangent, query_early, keyval_early, query_late, keyval_late, out_weight
):
    hbm = pl.BlockSpec(memory_space=pl.ANY)
    results = (
        jax.ShapeDtypeStruct(query_early.shape, BF16),
        jax.ShapeDtypeStruct(keyval_early.shape, BF16),
        jax.ShapeDtypeStruct(query_late.shape, BF16),
        jax.ShapeDtypeStruct(keyval_late.shape, BF16),
        jax.ShapeDtypeStruct((N, W), F32),
    )
    outputs = pl.pallas_call(
        kernel,
        out_shape=results,
        in_specs=[hbm] * 8,
        out_specs=(hbm,) * 5,
        scratch_shapes=[
            pltpu.VMEM((1, TOK), I32),
            pltpu.VMEM((2, 1, TOK), I32),
            pltpu.VMEM((2, TOK, W), BF16),
            pltpu.VMEM((W, W), BF16),
            pltpu.VMEM((1, NL, W), BF16),
            pltpu.VMEM((1, NE, 2, W), BF16),
            pltpu.VMEM((1, NL, 2, W), BF16),
            pltpu.VMEM((QKV_ROWS, W), BF16),
            pltpu.VMEM((N, 16, 1536), BF16),
            pltpu.VMEM((N, 16, 1536), BF16),
            pltpu.VMEM((8, E), F32),
            pltpu.VMEM((N, 8, E), F32),
            pltpu.VMEM((N, QKV_ROWS, E), BF16),
            pltpu.VMEM((DP, ROWS, W), BF16),
            pltpu.VMEM((ROWS, W), BF16),
            pltpu.VMEM((N, ROWS, E), BF16),
            pltpu.VMEM((N, ROWS, E), BF16),
            pltpu.VMEM((DP, 2, ROWS, E), BF16),
            pltpu.VMEM((N, QKV_ROWS, E), BF16),
            pltpu.VMEM((2, 4, 4, 16, W // 2), BF16),
            pltpu.VMEM((2, 3, 4, 16, W // 2), BF16),
            pltpu.VMEM((2, 4, 16, W // 2), BF16),
            pltpu.VMEM((2, 3, 16, W // 2), BF16),
            pltpu.VMEM((QKV_ROWS, W), BF16),
            pltpu.VMEM((1, NE, 2, W), BF16),
            pltpu.VMEM((1, NL, W), BF16),
            pltpu.VMEM((1, NL, 2, W), BF16),
            pltpu.VMEM((N, W), F32),
            pltpu.VMEM((KE, KE), F32),
            pltpu.VMEM((KE, KE), BF16),
            pltpu.VMEM((KE, KE), BF16),
            pltpu.VMEM((KL, KL), F32),
            pltpu.VMEM((KL, KL), BF16),
            pltpu.VMEM((KL, KL), BF16),
            pltpu.SemaphoreType.DMA((8,)),
            pltpu.SemaphoreType.DMA((8,)),
            pltpu.SemaphoreType.DMA((8,)),
            pltpu.SemaphoreType.DMA,
            pltpu.SemaphoreType.DMA((4,)),
            pltpu.SemaphoreType.DMA((2,)),
            pltpu.SemaphoreType.DMA((2, 2)),
        ],
        compiler_params=pltpu.CompilerParams(
            collective_id=0, has_side_effects=True, vmem_limit_bytes=56 * 1024 * 1024
        ),
        cost_estimate=pl.CostEstimate(
            flops=3_000_000_000, bytes_accessed=20_000_000, transcendentals=800_000
        ),
        name="rows_attention_weight",
    )(
        depths, owners, cotangent[:, 0], query_early, keyval_early, query_late, keyval_late,
        out_weight,
    )
    return pl.pallas_call(
        finish,
        out_shape=results,
        in_specs=[hbm] * 5,
        out_specs=(hbm,) * 5,
        scratch_shapes=[pltpu.VMEM(result.shape, result.dtype) for result in results]
        + [pltpu.SemaphoreType.DMA((10,))],
        compiler_params=pltpu.CompilerParams(vmem_limit_bytes=56 * 1024 * 1024),
        name="outputs",
    )(*outputs)


def solution(mesh):
    in_specs = (
        P("dp", "seq"),
        P(None, "dp", "seq"),
        P(None, "dp", "seq", None),
        P("dp", "seq", None),
        P("dp", "seq", None, None),
        P("dp", "seq", None),
        P("dp", "seq", None, None),
        P(),
    )
    out_specs = (
        P("dp", "seq", None),
        P("dp", "seq", None, None),
        P("dp", "seq", None),
        P("dp", "seq", None, None),
        P(("dp", "seq"), None),
    )
    return jax.shard_map(shards, mesh=mesh, in_specs=in_specs, out_specs=out_specs, check_vma=False)
```

```python
import jax
import jax.numpy as jnp
from jax import lax
from jax.experimental import pallas as pl
from jax.experimental.pallas import tpu as pltpu
from jax.sharding import PartitionSpec as P

MESH = pl.DeviceIdType.MESH
F32, BF16, I32 = jnp.float32, jnp.bfloat16, jnp.int32

N = 16
DP = 8
E = 128
W = 2048
TOK = 256
NE, NL = 48, 24
NLP = 32
ROWS = NE + NLP
GRAD_ROWS = 3 * NE + 80
QKV_ROWS = 3 * NE + 64
OTHERS = (
    (2, 2), (1, 2), (2, 1), (2, 3), (3, 2), (0, 2), (2, 0), (1, 1),
    (3, 3), (1, 3), (3, 1), (0, 1), (1, 0), (0, 3), (3, 0),
)
KE, KL = N * NE, N * NL
SCALE = E**-0.5


def dot(a, b):
    return lax.dot_general(a, b, (((1,), (0,)), ((), ())), preferred_element_type=F32)


def dot_nt(a, b):
    return lax.dot_general(a, b, (((1,), (1,)), ((), ())), preferred_element_type=F32)


def dot_tn(a, b):
    return lax.dot_general(a, b, (((0,), (0,)), ((), ())), preferred_element_type=F32)


def iota(shape, dim):
    return lax.broadcasted_iota(I32, shape, dim)


def onehot(mask):
    return jnp.where(mask, 1.0, 0.0).astype(BF16)


def kernel(
    depths, owners, cot, query_early, keyval_early, query_late, keyval_late, weight,
    dquery_early, dkeyval_early, dquery_late, dkeyval_late, dw,
    depth_v, owner_v, cotv, wv, ql_v, kve_v, kvl_v, qkv_send,
    rows_send, rows_recv, meta_send, meta_recv, qkv_recv, rows_all,
    dout_send, dout_recv, att_send, att_recv, dqkv_send,
    sum1_send, sum1_recv, sum2_send, sum2_recv,
    out, dkve_v, dql_v, dkvl_v, dw_v,
    probs_e, probs_bf_e, ds_e, probs_l, probs_bf_l, ds_l,
    local_sem, send, recv, gsend, grecv, sum_send, sum_recv,
):
    d = lax.axis_index("dp")
    s = lax.axis_index("seq")
    chip = lax.div(d, 2)
    core = lax.rem(d, 2)
    partner = chip * 2 + 1 - core
    z, y = lax.div(s, 4), lax.rem(s, 4)

    def head_of(j):
        return lax.rem(chip + lax.div(j, 4) + 2 * core, 4) * 4 + lax.rem(j, 4)

    def same_core(i):
        return lax.rem(chip + i, 4) * 2 + core

    my_head = head_of(s)
    target_dp = lax.div(my_head, 2)
    parity = lax.rem(my_head, 2)

    cot_copy = pltpu.make_async_copy(cot, cotv, local_sem.at[0])
    weight_copy = pltpu.make_async_copy(weight, wv, local_sem.at[1])
    routing = [
        pltpu.make_async_copy(depths, depth_v, local_sem.at[6]),
        pltpu.make_async_copy(owners, owner_v, local_sem.at[7]),
    ]
    late_copy = pltpu.make_async_copy(keyval_late, kvl_v, local_sem.at[3])
    operands = [
        pltpu.make_async_copy(keyval_early, kve_v, local_sem.at[2]),
        pltpu.make_async_copy(query_late, ql_v, local_sem.at[5]),
        pltpu.make_async_copy(query_early.at[0], qkv_send.at[0:NE], local_sem.at[4]),
    ]
    for copy in routing + [late_copy, cot_copy] + operands + [weight_copy]:
        copy.start()

    barrier = pltpu.get_barrier_semaphore()

    def greet(to_dp, to_seq):
        pl.semaphore_signal(barrier, inc=1, device_id=(to_dp, to_seq), device_id_type=MESH)

    for i in range(1, N):
        greet(d, lax.rem(s + i, N))
    greet(partner, s)
    for i in (1, 3):
        greet(same_core(i), s)
    for from_dp in range(DP):
        turn = lax.rem(chip + 8 - from_dp // 2 - 2 * (from_dp % 2), 4)
        for p in range(2):
            from_seq = turn * 4 + 2 * core + p

            @pl.when(jnp.logical_or(d != from_dp, from_seq != s))
            def _(from_dp=from_dp, from_seq=from_seq):
                greet(from_dp, from_seq)

    for copy in routing:
        copy.wait()
    depth = depth_v[...]
    active_e, active_l = depth > 1, depth > 2
    owner_e, owner_l = owner_v[0], owner_v[1]
    flags = jnp.where(
        iota((16, TOK), 0) < 8,
        jnp.broadcast_to(active_e.astype(F32), (16, TOK)),
        jnp.broadcast_to(active_l.astype(F32), (16, TOK)),
    ).astype(BF16)
    below = onehot(iota((TOK, TOK), 0) < iota((TOK, TOK), 1))
    before = dot(flags, below).astype(I32)
    rank_e, rank_l = before[0:1] >> 4, before[8:9] >> 4
    token = (iota((8, TOK), 1) + 1).astype(F32).astype(BF16)
    line = iota((E, TOK), 0)
    meta_e = dot_nt(token, onehot((line == owner_e * 8 + rank_e) & active_e))
    meta_l = dot_nt(token, onehot((line == owner_l * 4 + rank_l) & active_l))
    meta = jnp.where(iota((8, E), 0) < 4, meta_e, meta_l)
    late_copy.wait()
    meta_send[...] = jnp.concatenate(
        [kvl_v[0, 16:NL, 1, :].astype(F32), jnp.concatenate([meta] * N, axis=1)], axis=0
    ).astype(BF16)

    cot_copy.wait()
    line = iota((TOK, TOK), 0)
    base = jnp.where(active_e, owner_e * 16 + rank_e, -64)
    packed = dot(onehot(line == base), cotv[0, :, 0:1024])
    packed += dot(onehot(line == base + 8), cotv[0, :, 1024:2048])
    rows_send[:, :, 0:1024] = packed.reshape(N, 16, 1024).astype(BF16)
    base = jnp.where(active_l, owner_l * 16 + rank_l, -64)
    packed = dot(onehot(line == base), cotv[1, :, 0:512])
    for q in range(1, 4):
        packed += dot(onehot(line == base + 4 * q), cotv[1, :, q * 512 : (q + 1) * 512])
    rows_send[:, :, 1024:1536] = packed.reshape(N, 16, 512).astype(BF16)

    elsewhere = jnp.where(target_dp == d, 0, 1)
    pl.semaphore_wait(barrier, N - 1 + 3 + N - 1 + elsewhere)

    def remote(src, dst, phase, to, to_dp):
        return pltpu.make_async_remote_copy(
            src_ref=src,
            dst_ref=dst,
            send_sem=send.at[phase],
            recv_sem=recv.at[phase],
            device_id=(to_dp, to),
            device_id_type=MESH,
        )

    def wait_bytes(ref, sem):
        pltpu.make_async_copy(ref, ref, sem).wait()

    def other(dz, dy):
        to_z = lax.rem(z + jnp.where(core == 0, dz, 4 - dz), 4)
        to_y = lax.rem(y + jnp.where(core == 0, dy, 4 - dy), 4)
        return to_z * 4 + to_y

    def exchange(phase, src, dst, whole):
        for dz, dy in OTHERS:
            to = other(dz, dy)
            remote(src(to), dst(s), phase, to, d).start()
        pltpu.make_async_copy(src(s), dst(s), recv.at[phase]).start()

    def arrive(phase, src, dst, whole):
        wait_bytes(whole, recv.at[phase])

    def columns(ref, j):
        return ref.at[:, pl.ds(pl.multiple_of(head_of(j) * E, E), E)]

    META = (0, lambda j: columns(meta_send, j), lambda j: meta_recv.at[j], meta_recv)
    ROW = (1, lambda j: rows_send.at[j], lambda j: rows_recv.at[j], rows_recv)
    QKV = (2, lambda j: columns(qkv_send, j), lambda j: qkv_recv.at[j], qkv_recv)
    DOUT = (3, lambda j: columns(dout_send, j), lambda j: dout_recv.at[j], dout_recv)

    def grads(phase, first, last):
        return (
            phase,
            lambda j: dqkv_send.at[j, first:last],
            lambda j: columns(out.at[first:last], j),
            out.at[first:last],
        )

    GRAD_Q, GRAD_LATE = grads(4, 0, NE), grads(5, 3 * NE, GRAD_ROWS)
    GRAD_KV = grads(6, NE, 3 * NE)
    ATT = 7

    exchange(*META)
    exchange(*ROW)
    for copy in operands:
        copy.wait()
    qkv_send[NE : 2 * NE] = kve_v[0, :, 0, :]
    qkv_send[2 * NE : 3 * NE] = kve_v[0, :, 1, :]
    for c in range(4):
        cut = slice(c * 512, (c + 1) * 512)
        pair = kvl_v[0, :, :, cut].astype(F32)
        qkv_send[3 * NE : QKV_ROWS, cut] = jnp.concatenate(
            [ql_v[0, :, cut].astype(F32), pair[:, 0], pair[0:16, 1]], axis=0
        ).astype(BF16)
    exchange(*QKV)

    arrive(*META)

    tokens = meta_recv[...].astype(F32)

    def spread(first, shift):
        lane = iota((N, E), 1)
        mine = (lane >> shift) == iota((N, E), 0)
        wide = jnp.concatenate(
            [jnp.where(mine, tokens[j, first : first + 1], 0.0) for j in range(N)], axis=0
        )
        low = (1 << shift) - 1
        same = onehot((iota((E, E), 0) & low) == (iota((E, E), 1) & low))
        wide = dot(wide.astype(BF16), same)
        total = jnp.zeros((N, E), F32)
        for j in range(N):
            total += jnp.where((lane >> shift) == j, wide[j * N : (j + 1) * N], 0.0)
        return total

    token_e = spread(8, 3)
    token_l = spread(12, 2)

    def tables(token, shift, slots, padded):
        peak = 1 << shift
        valid = onehot(token > 0.0)
        src, dst = iota((E, E), 0), iota((E, E), 1)
        offset = dot(valid, onehot((src >> shift) < (dst >> shift)))[0:1].astype(I32)
        in_lane = iota((1, E), 1)
        slot = jnp.where(token[0:1] > 0.0, offset + (in_lane & (peak - 1)), -1)
        select = onehot(iota((padded, E), 0) == slot)
        low = token.astype(BF16)
        high = jnp.where(token > 0.0, (iota((N, E), 1) >> shift).astype(F32), 0.0).astype(BF16)
        cols = dot_nt(select, high) * 256.0 + dot_nt(select, low) - 1.0
        total = N * slots
        mult = 1366 if slots == NE else 2731
        in_row = iota((padded, total), 1)
        tile = onehot(in_row - ((in_row * mult) >> 16) * slots == iota((padded, total), 0))
        wide_high = dot(dot_nt(high, select).astype(BF16), tile)
        wide_low = dot(dot_nt(low, select).astype(BF16), tile)
        in_row = iota((N, total), 1)
        mine = ((in_row * mult) >> 16) == iota((N, total), 0)
        row = jnp.sum(
            jnp.where(mine, wide_high * 256.0 + wide_low - 1.0, 0.0), axis=0, keepdims=True
        )
        src, dst = iota((E, TOK), 0), iota((E, TOK), 1)
        offset = dot(valid, onehot((src >> shift) < (dst >> 4)))[0:1].astype(I32)
        count = dot(valid, onehot((src >> shift) == (dst >> 4)))[0:1].astype(I32)
        in_lane = iota((1, TOK), 1)
        rank = in_lane & (peak - 1)
        slot = jnp.where(rank < count, offset + rank, -1)
        part = (in_lane & 15) >> shift
        return cols, row, slot, part

    cols_e, row_e, slot_e, part_e = tables(token_e, 3, NE, NE)
    cols_l, row_l, slot_l, part_l = tables(token_l, 2, NL, NLP)

    arrive(*ROW)
    for h in range(2):
        pick = onehot((iota((NE, TOK), 0) == slot_e) & (part_e == h))
        got = dot(pick, rows_recv[:, :, 0:1024].reshape(TOK, 1024))
        rows_all[d, 0:NE, h * 1024 : (h + 1) * 1024] = got.astype(BF16)
    for q in range(4):
        pick = onehot((iota((NLP, TOK), 0) == slot_l) & (part_l == q))
        got = dot(pick, rows_recv[:, :, 1024:1536].reshape(TOK, 512))
        rows_all[d, NE:ROWS, q * 512 : (q + 1) * 512] = got.astype(BF16)

    def gather(block, kind, to_dp, half=None):
        part = rows_all.at[block]
        if half is not None:
            part = part.at[:, half * 1024 : (half + 1) * 1024]
        return pltpu.make_async_remote_copy(
            src_ref=part,
            dst_ref=part,
            send_sem=gsend,
            recv_sem=grecv.at[kind],
            device_id=(to_dp, s),
            device_id_type=MESH,
        )

    ahead, behind, far = same_core(1), same_core(3), same_core(2)
    FROM_BEHIND, FROM_AHEAD, FROM_FAR, FROM_PARTNER = range(4)
    gather(d, FROM_BEHIND, ahead).start()
    gather(d, FROM_AHEAD, behind).start()
    gather(d, FROM_PARTNER, partner).start()

    def gather_near():
        wait_bytes(rows_all.at[behind], grecv.at[FROM_BEHIND])
        gather(behind, FROM_FAR, ahead, 1).start()
        gather(behind, FROM_PARTNER, partner).start()
        wait_bytes(rows_all.at[ahead], grecv.at[FROM_AHEAD])
        gather(ahead, FROM_FAR, behind, 0).start()
        gather(ahead, FROM_PARTNER, partner).start()

    def gather_far():
        wait_bytes(rows_all.at[far], grecv.at[FROM_FAR])
        gather(far, FROM_PARTNER, partner).start()

    weight_copy.wait()
    mine = rows_all[d]
    for c in range(8):
        part = dot_nt(mine, wv[c * 256 : (c + 1) * 256, :])
        dout_send[:, c * 256 : (c + 1) * 256] = part.astype(BF16)
    exchange(*DOUT)

    arrive(*QKV)
    gather_near()

    def late(wide, part):
        return wide[:, part * NL : (part + 1) * NL].reshape(KL, E)

    def softmax(query, key, value, row, col):
        scores = dot_nt(query, key) * SCALE
        scores = jnp.where(row <= col, scores, -1e30)
        top = jnp.max(scores, axis=1, keepdims=True)
        weights = jnp.exp(scores - top)
        probs = weights / jnp.sum(weights, axis=1, keepdims=True)
        probs_bf = probs.astype(BF16)
        return probs, probs_bf, dot(probs_bf, value)

    def attended_out(first, last):
        def copy(to):
            return remote(
                att_send.at[to, first:last], att_recv.at[d, parity, first:last], ATT, to, target_dp
            )

        for dz, dy in OTHERS:
            copy(other(dz, dy)).start()

        @pl.when(target_dp == d)
        def _():
            pltpu.make_async_copy(
                att_send.at[s, first:last], att_recv.at[d, parity, first:last], recv.at[ATT]
            ).start()

        @pl.when(target_dp != d)
        def _():
            copy(s).start()

    key_e = qkv_recv[:, NE : 2 * NE, :].reshape(KE, E)
    value_e = qkv_recv[:, 2 * NE : 3 * NE, :].reshape(KE, E)
    for b in range(4):
        query = qkv_recv[4 * b : 4 * b + 4, 0:NE, :].reshape(4 * NE, E)
        col = jnp.concatenate([cols_e[:, o : o + 1] for o in range(4 * b, 4 * b + 4)], axis=0)
        probs, probs_bf, attended = softmax(query, key_e, value_e, row_e, col)
        probs_e[b * 192 : (b + 1) * 192] = probs
        probs_bf_e[b * 192 : (b + 1) * 192] = probs_bf
        att_send[4 * b : 4 * b + 4, 0:NE, :] = attended.reshape(4, NE, E).astype(BF16)
    attended_out(0, NE)
    wide = jnp.concatenate(
        [qkv_recv[:, 3 * NE : QKV_ROWS, :].astype(F32), meta_recv[:, 0:8, :].astype(F32)], axis=1
    )
    query_l, key_l, value_l = (late(wide, part).astype(BF16) for part in range(3))
    gap = jnp.zeros((8, NLP - NL, E), F32)
    for b in range(2):
        query = query_l[b * 192 : (b + 1) * 192]
        col = jnp.concatenate([cols_l[0:NL, o : o + 1] for o in range(8 * b, 8 * b + 8)], axis=0)
        probs, probs_bf, attended = softmax(query, key_l, value_l, row_l, col)
        probs_l[b * 192 : (b + 1) * 192] = probs
        probs_bf_l[b * 192 : (b + 1) * 192] = probs_bf
        attended = jnp.concatenate([attended.reshape(8, NL, E), gap], axis=1)
        att_send[8 * b : 8 * b + 8, NE:ROWS, :] = attended.astype(BF16)
    attended_out(NE, ROWS)

    arrive(*DOUT)

    def backward(query, key, value, dout, attended, probs):
        delta = jnp.sum(dout.astype(F32) * attended.astype(F32), axis=1, keepdims=True)
        dprobs = dot_nt(dout, value)
        dscores = (probs * (dprobs - delta)).astype(BF16)
        return dscores, dot(dscores, key) * SCALE

    for b in range(4):
        dout = dout_recv[4 * b : 4 * b + 4, 0:NE, :].reshape(192, E)
        attended = att_send[4 * b : 4 * b + 4, 0:NE, :].reshape(192, E)
        query = None
        dscores, dquery = backward(
            query, key_e, value_e, dout, attended, probs_e[b * 192 : (b + 1) * 192]
        )
        ds_e[b * 192 : (b + 1) * 192] = dscores
        dqkv_send[4 * b : 4 * b + 4, 0:NE, :] = dquery.reshape(4, NE, E).astype(BF16)
    exchange(*GRAD_Q)
    dout_l = late(dout_recv[:, NE:ROWS, :].astype(F32), 0).astype(BF16)
    attended_l = late(att_send[:, NE:ROWS, :].astype(F32), 0)
    dquery_l = []
    for b in range(2):
        dscores, dquery = backward(
            None, key_l, value_l, dout_l[b * 192 : (b + 1) * 192],
            attended_l[b * 192 : (b + 1) * 192], probs_l[b * 192 : (b + 1) * 192]
        )
        ds_l[b * 192 : (b + 1) * 192] = dscores
        dquery_l.append(dquery)
    query_e = qkv_recv[:, 0:NE, :].reshape(KE, E)
    dout_e = dout_recv[:, 0:NE, :].reshape(KE, E)
    for c in range(2):
        dkey = dot_tn(ds_e[:, c * 384 : (c + 1) * 384], query_e) * SCALE
        dqkv_send[8 * c : 8 * c + 8, NE : 2 * NE, :] = dkey.reshape(8, NE, E).astype(BF16)
        dvalue = dot_tn(probs_bf_e[:, c * 384 : (c + 1) * 384], dout_e)
        dqkv_send[8 * c : 8 * c + 8, 2 * NE : 3 * NE, :] = dvalue.reshape(8, NE, E).astype(BF16)
    dquery = jnp.concatenate(dquery_l, axis=0)
    dkey = dot_tn(ds_l[...], query_l) * SCALE
    dvalue = dot_tn(probs_bf_l[...], dout_l)
    parts = [part.reshape(N, NL, E) for part in (dquery, dkey, dvalue)]
    parts.append(jnp.zeros((N, 8, E), F32))
    dqkv_send[:, 3 * NE : GRAD_ROWS, :] = jnp.concatenate(parts, axis=1).astype(BF16)
    exchange(*GRAD_LATE)
    gather_far()

    wait_bytes(att_recv, recv.at[ATT])
    wait_bytes(rows_all.at[0:4], grecv.at[FROM_PARTNER])
    def along(half, stage, i):
        if half == stage:
            to = lax.rem(z + i, 4)
            return to, to * 4 + y
        to = lax.rem(y + i, 4)
        return to, z * 4 + to

    def sum_copy(half, stage, i):
        source, target = (sum1_send, sum1_recv) if stage == 0 else (sum2_send, sum2_recv)
        to, device = along(half, stage, i)
        return pltpu.make_async_remote_copy(
            src_ref=source.at[half, to],
            dst_ref=target.at[half, i - 1],
            send_sem=sum_send.at[stage],
            recv_sem=sum_recv.at[stage, half],
            device_id=(d, device),
            device_id_type=MESH,
        )

    rows = rows_all[...].reshape(DP * ROWS, W)
    columns_of = [att_recv[:, p].reshape(DP * ROWS, E) for p in range(2)]
    for half in range(2):
        for p in range(2):
            for c in range(2):
                cut, first = slice(c * 512, (c + 1) * 512), half * 1024 + c * 512
                part = dot_tn(columns_of[p], rows[:, first : first + 512])
                part = part.reshape(2, 4, 16, 512).astype(BF16)
                if half == 0:
                    sum1_send[0, 2 * p : 2 * p + 2, :, :, cut] = part
                else:
                    for i in range(2):
                        for j in range(4):
                            sum1_send[1, j, 2 * p + i, :, cut] = part[i, j]
        for i in (2, 1, 3):
            sum_copy(half, 0, i).start()
    exchange(*GRAD_KV)
    for half in range(2):
        wait_bytes(sum1_recv.at[half], sum_recv.at[0, half])
        total = sum1_send[half, z if half == 0 else y].astype(F32)
        for i in range(3):
            total += sum1_recv[half, i].astype(F32)
        sum2_send[half] = total.astype(BF16)
        for i in (2, 1, 3):
            sum_copy(half, 1, i).start()

    wait_bytes(meta_recv.at[1:N], send.at[META[0]])
    wait_bytes(rows_recv.at[1:N], send.at[ROW[0]])
    wait_bytes(qkv_recv.at[1:N], send.at[QKV[0]])
    wait_bytes(dout_recv.at[1:N], send.at[DOUT[0]])

    @pl.when(target_dp == d)
    def _():
        wait_bytes(att_send.at[1:N], send.at[ATT])

    @pl.when(target_dp != d)
    def _():
        wait_bytes(att_send, send.at[ATT])

    wait_bytes(rows_all.at[1:DP], gsend)
    wait_bytes(sum1_recv, sum_send.at[0])

    writes = []

    def write(source, target):
        writes.append(pltpu.make_async_copy(source, target, local_sem.at[len(writes)]))
        writes[-1].start()

    arrive(*GRAD_Q)
    write(out.at[0:NE], dquery_early.at[0])
    arrive(*GRAD_LATE)
    for c in range(4):
        cut = slice(c * 512, (c + 1) * 512)
        wide = out[3 * NE : GRAD_ROWS, cut].astype(F32)
        dql_v[0, :, cut] = wide[0:NL].astype(BF16)
        dkvl_v[0, :, :, cut] = jnp.stack(
            [wide[NL : 2 * NL].astype(BF16), wide[2 * NL : 3 * NL].astype(BF16)], axis=1
        )
    write(dql_v, dquery_late)
    write(dkvl_v, dkeyval_late)
    arrive(*GRAD_KV)
    dkve_v[0] = jnp.stack([out[NE : 2 * NE], out[2 * NE : 3 * NE]], axis=1)
    write(dkve_v, dkeyval_early)
    for half in range(2):
        wait_bytes(sum2_recv.at[half], sum_recv.at[1, half])
        total = sum2_send[half, y if half == 0 else z].astype(F32)
        for i in range(3):
            total += sum2_recv[half, i].astype(F32)
        dw_v[:, half * 1024 : (half + 1) * 1024] = total
    write(dw_v, dw)
    wait_bytes(sum2_recv, sum_send.at[1])
    for grad, (first, last) in (
        (GRAD_Q, (0, NE)),
        (GRAD_LATE, (3 * NE, GRAD_ROWS)),
        (GRAD_KV, (NE, 3 * NE)),
    ):
        wait_bytes(dqkv_send.at[1:N, first:last], send.at[grad[0]])
    for copy in writes:
        copy.wait()


def finish(*refs):
    sources, targets, held, sem = refs[0:5], refs[5:10], refs[10:15], refs[15]
    loads = [pltpu.make_async_copy(sources[i], held[i], sem.at[i]) for i in range(5)]
    stores = [pltpu.make_async_copy(held[i], targets[i], sem.at[5 + i]) for i in range(5)]
    for copy in loads:
        copy.start()
    for load, store in zip(loads, stores, strict=True):
        load.wait()
        store.start()
    for copy in stores:
        copy.wait()


def shards(
    depths, owners, cotangent, query_early, keyval_early, query_late, keyval_late, out_weight
):
    hbm = pl.BlockSpec(memory_space=pl.ANY)
    results = (
        jax.ShapeDtypeStruct(query_early.shape, BF16),
        jax.ShapeDtypeStruct(keyval_early.shape, BF16),
        jax.ShapeDtypeStruct(query_late.shape, BF16),
        jax.ShapeDtypeStruct(keyval_late.shape, BF16),
        jax.ShapeDtypeStruct((N, W), F32),
    )
    outputs = pl.pallas_call(
        kernel,
        out_shape=results,
        in_specs=[hbm] * 8,
        out_specs=(hbm,) * 5,
        scratch_shapes=[
            pltpu.VMEM((1, TOK), I32),
            pltpu.VMEM((2, 1, TOK), I32),
            pltpu.VMEM((2, TOK, W), BF16),
            pltpu.VMEM((W, W), BF16),
            pltpu.VMEM((1, NL, W), BF16),
            pltpu.VMEM((1, NE, 2, W), BF16),
            pltpu.VMEM((1, NL, 2, W), BF16),
            pltpu.VMEM((QKV_ROWS, W), BF16),
            pltpu.VMEM((N, 16, 1536), BF16),
            pltpu.VMEM((N, 16, 1536), BF16),
            pltpu.VMEM((16, W), BF16),
            pltpu.VMEM((N, 16, E), BF16),
            pltpu.VMEM((N, QKV_ROWS, E), BF16),
            pltpu.VMEM((DP, ROWS, W), BF16),
            pltpu.VMEM((ROWS, W), BF16),
            pltpu.VMEM((N, ROWS, E), BF16),
            pltpu.VMEM((N, ROWS, E), BF16),
            pltpu.VMEM((DP, 2, ROWS, E), BF16),
            pltpu.VMEM((N, GRAD_ROWS, E), BF16),
            pltpu.VMEM((2, 4, 4, 16, W // 2), BF16),
            pltpu.VMEM((2, 3, 4, 16, W // 2), BF16),
            pltpu.VMEM((2, 4, 16, W // 2), BF16),
            pltpu.VMEM((2, 3, 16, W // 2), BF16),
            pltpu.VMEM((GRAD_ROWS, W), BF16),
            pltpu.VMEM((1, NE, 2, W), BF16),
            pltpu.VMEM((1, NL, W), BF16),
            pltpu.VMEM((1, NL, 2, W), BF16),
            pltpu.VMEM((N, W), F32),
            pltpu.VMEM((KE, KE), F32),
            pltpu.VMEM((KE, KE), BF16),
            pltpu.VMEM((KE, KE), BF16),
            pltpu.VMEM((KL, KL), F32),
            pltpu.VMEM((KL, KL), BF16),
            pltpu.VMEM((KL, KL), BF16),
            pltpu.SemaphoreType.DMA((8,)),
            pltpu.SemaphoreType.DMA((8,)),
            pltpu.SemaphoreType.DMA((8,)),
            pltpu.SemaphoreType.DMA,
            pltpu.SemaphoreType.DMA((4,)),
            pltpu.SemaphoreType.DMA((2,)),
            pltpu.SemaphoreType.DMA((2, 2)),
        ],
        compiler_params=pltpu.CompilerParams(
            collective_id=0, has_side_effects=True, vmem_limit_bytes=56 * 1024 * 1024
        ),
        cost_estimate=pl.CostEstimate(
            flops=3_000_000_000, bytes_accessed=20_000_000, transcendentals=800_000
        ),
        name="rows_attention_weight",
    )(
        depths, owners, cotangent[:, 0], query_early, keyval_early, query_late, keyval_late,
        out_weight,
    )
    return pl.pallas_call(
        finish,
        out_shape=results,
        in_specs=[hbm] * 5,
        out_specs=(hbm,) * 5,
        scratch_shapes=[pltpu.VMEM(result.shape, result.dtype) for result in results]
        + [pltpu.SemaphoreType.DMA((10,))],
        compiler_params=pltpu.CompilerParams(vmem_limit_bytes=56 * 1024 * 1024),
        name="outputs",
    )(*outputs)


def solution(mesh):
    in_specs = (
        P("dp", "seq"),
        P(None, "dp", "seq"),
        P(None, "dp", "seq", None),
        P("dp", "seq", None),
        P("dp", "seq", None, None),
        P("dp", "seq", None),
        P("dp", "seq", None, None),
        P(),
    )
    out_specs = (
        P("dp", "seq", None),
        P("dp", "seq", None, None),
        P("dp", "seq", None),
        P("dp", "seq", None, None),
        P(("dp", "seq"), None),
    )
    return jax.shard_map(shards, mesh=mesh, in_specs=in_specs, out_specs=out_specs, check_vma=False)
```

```python
import jax
import jax.numpy as jnp
from jax import lax
from jax.experimental import pallas as pl
from jax.experimental.pallas import tpu as pltpu
from jax.sharding import PartitionSpec as P

MESH = pl.DeviceIdType.MESH
F32, BF16, I32 = jnp.float32, jnp.bfloat16, jnp.int32

N = 16
DP = 8
E = 128
W = 2048
TOK = 256
NE, NL = 48, 24
NLP = 32
ROWS = NE + NLP
GRAD_ROWS = 3 * NE + 80
QKV_ROWS = 3 * NE + 64
OTHERS = (
    (2, 2), (1, 2), (2, 1), (2, 3), (3, 2), (0, 2), (2, 0), (1, 1),
    (3, 3), (1, 3), (3, 1), (0, 1), (1, 0), (0, 3), (3, 0),
)
KE, KL = N * NE, N * NL
SCALE = E**-0.5


def dot(a, b):
    return lax.dot_general(a, b, (((1,), (0,)), ((), ())), preferred_element_type=F32)


def dot_nt(a, b):
    return lax.dot_general(a, b, (((1,), (1,)), ((), ())), preferred_element_type=F32)


def dot_tn(a, b):
    return lax.dot_general(a, b, (((0,), (0,)), ((), ())), preferred_element_type=F32)


def iota(shape, dim):
    return lax.broadcasted_iota(I32, shape, dim)


def onehot(mask):
    return jnp.where(mask, 1.0, 0.0).astype(BF16)


def kernel(
    depths, owners, cot, query_early, keyval_early, query_late, keyval_late, weight,
    dquery_early, dkeyval_early, dquery_late, dkeyval_late, sums,
    depth_v, owner_v, cotv, wv, ql_v, kve_v, kvl_v, qkv_send,
    rows_send, rows_recv, meta_send, meta_recv, qkv_recv, rows_all,
    dout_send, dout_recv, att_send, att_recv, dqkv_send,
    sum1_send, sum1_recv, sum2_send,
    out, dkve_v, dql_v, dkvl_v,
    probs_e, probs_bf_e, ds_e, probs_l, probs_bf_l, ds_l,
    local_sem, send, recv, gsend, grecv, sum_send, sum_recv,
):
    d = lax.axis_index("dp")
    s = lax.axis_index("seq")
    chip = lax.div(d, 2)
    core = lax.rem(d, 2)
    partner = chip * 2 + 1 - core
    z, y = lax.div(s, 4), lax.rem(s, 4)

    def head_of(j):
        return lax.rem(chip + lax.div(j, 4) + 2 * core, 4) * 4 + lax.rem(j, 4)

    def same_core(i):
        return lax.rem(chip + i, 4) * 2 + core

    my_head = head_of(s)
    target_dp = lax.div(my_head, 2)
    parity = lax.rem(my_head, 2)

    cot_copies = [
        pltpu.make_async_copy(
            cot.at[r, 0, pl.ds(i * 128, 128)], cotv.at[r, pl.ds(i * 128, 128)],
            local_sem.at[8 + 2 * r + i],
        )
        for r in range(2)
        for i in range(2)
    ]
    weight_copy = pltpu.make_async_copy(weight, wv, local_sem.at[1])
    routing = [
        pltpu.make_async_copy(depths, depth_v, local_sem.at[6]),
        pltpu.make_async_copy(owners, owner_v, local_sem.at[7]),
    ]
    late_copy = pltpu.make_async_copy(keyval_late, kvl_v, local_sem.at[3])
    operands = [
        pltpu.make_async_copy(keyval_early, kve_v, local_sem.at[2]),
        pltpu.make_async_copy(query_late, ql_v, local_sem.at[5]),
        pltpu.make_async_copy(query_early.at[0], qkv_send.at[0:NE], local_sem.at[4]),
    ]
    for copy in routing + [late_copy] + cot_copies + operands + [weight_copy]:
        copy.start()

    barrier = pltpu.get_barrier_semaphore()

    def greet(to_dp, to_seq):
        pl.semaphore_signal(barrier, inc=1, device_id=(to_dp, to_seq), device_id_type=MESH)

    for i in range(1, N):
        greet(d, lax.rem(s + i, N))
    greet(partner, s)
    for i in (1, 3):
        greet(same_core(i), s)
    for from_dp in range(DP):
        turn = lax.rem(chip + 8 - from_dp // 2 - 2 * (from_dp % 2), 4)
        for p in range(2):
            from_seq = turn * 4 + 2 * core + p

            @pl.when(jnp.logical_or(d != from_dp, from_seq != s))
            def _(from_dp=from_dp, from_seq=from_seq):
                greet(from_dp, from_seq)

    for copy in routing:
        copy.wait()
    depth = depth_v[...]
    active_e, active_l = depth > 1, depth > 2
    owner_e, owner_l = owner_v[0], owner_v[1]
    flags = jnp.where(
        iota((16, TOK), 0) < 8,
        jnp.broadcast_to(active_e.astype(F32), (16, TOK)),
        jnp.broadcast_to(active_l.astype(F32), (16, TOK)),
    ).astype(BF16)
    below = onehot(iota((TOK, TOK), 0) < iota((TOK, TOK), 1))
    before = dot(flags, below).astype(I32)
    rank_e, rank_l = before[0:1] >> 4, before[8:9] >> 4
    token = (iota((8, TOK), 1) + 1).astype(F32).astype(BF16)
    line = iota((E, TOK), 0)
    meta_e = dot_nt(token, onehot((line == owner_e * 8 + rank_e) & active_e))
    meta_l = dot_nt(token, onehot((line == owner_l * 4 + rank_l) & active_l))
    meta = jnp.where(iota((8, E), 0) < 4, meta_e, meta_l)
    late_copy.wait()
    meta_send[...] = jnp.concatenate(
        [kvl_v[0, 16:NL, 1, :].astype(F32), jnp.concatenate([meta] * N, axis=1)], axis=0
    ).astype(BF16)

    for copy in cot_copies[0:2]:
        copy.wait()
    line = iota((TOK, TOK), 0)
    base = jnp.where(active_e, owner_e * 16 + rank_e, -64)
    packed = dot(onehot(line == base), cotv[0, :, 0:1024])
    packed += dot(onehot(line == base + 8), cotv[0, :, 1024:2048])
    rows_send[:, :, 0:1024] = packed.reshape(N, 16, 1024).astype(BF16)
    for copy in cot_copies[2:4]:
        copy.wait()
    base = jnp.where(active_l, owner_l * 16 + rank_l, -64)
    packed = dot(onehot(line == base), cotv[1, :, 0:512])
    for q in range(1, 4):
        packed += dot(onehot(line == base + 4 * q), cotv[1, :, q * 512 : (q + 1) * 512])
    rows_send[:, :, 1024:1536] = packed.reshape(N, 16, 512).astype(BF16)

    elsewhere = jnp.where(target_dp == d, 0, 1)
    pl.semaphore_wait(barrier, N - 1 + 3 + N - 1 + elsewhere)

    def remote(src, dst, phase, to, to_dp):
        return pltpu.make_async_remote_copy(
            src_ref=src,
            dst_ref=dst,
            send_sem=send.at[phase],
            recv_sem=recv.at[phase],
            device_id=(to_dp, to),
            device_id_type=MESH,
        )

    def wait_bytes(ref, sem):
        pltpu.make_async_copy(ref, ref, sem).wait()

    def other(dz, dy):
        to_z = lax.rem(z + jnp.where(core == 0, dz, 4 - dz), 4)
        to_y = lax.rem(y + jnp.where(core == 0, dy, 4 - dy), 4)
        return to_z * 4 + to_y

    def exchange(phase, src, dst, whole):
        for dz, dy in OTHERS:
            to = other(dz, dy)
            remote(src(to), dst(s), phase, to, d).start()
        pltpu.make_async_copy(src(s), dst(s), recv.at[phase]).start()

    def arrive(phase, src, dst, whole):
        wait_bytes(whole, recv.at[phase])

    def columns(ref, j):
        return ref.at[:, pl.ds(pl.multiple_of(head_of(j) * E, E), E)]

    META = (0, lambda j: columns(meta_send, j), lambda j: meta_recv.at[j], meta_recv)
    ROW = (1, lambda j: rows_send.at[j], lambda j: rows_recv.at[j], rows_recv)
    QKV = (2, lambda j: columns(qkv_send, j), lambda j: qkv_recv.at[j], qkv_recv)
    DOUT = (3, lambda j: columns(dout_send, j), lambda j: dout_recv.at[j], dout_recv)

    def grads(phase, first, last):
        return (
            phase,
            lambda j: dqkv_send.at[j, first:last],
            lambda j: columns(out.at[first:last], j),
            out.at[first:last],
        )

    GRAD_Q = (
        4,
        lambda j: dqkv_send.at[j, 0:NE],
        lambda j: columns(dquery_early.at[0], j),
        dquery_early.at[0],
    )
    GRAD_LATE = grads(5, 3 * NE, GRAD_ROWS)
    GRAD_K, GRAD_V = grads(6, NE, 2 * NE), grads(7, 2 * NE, 3 * NE)
    ATT = 8

    exchange(*META)
    exchange(*ROW)
    for copy in operands:
        copy.wait()
    qkv_send[NE : 2 * NE] = kve_v[0, :, 0, :]
    qkv_send[2 * NE : 3 * NE] = kve_v[0, :, 1, :]
    for c in range(4):
        cut = slice(c * 512, (c + 1) * 512)
        pair = kvl_v[0, :, :, cut].astype(F32)
        qkv_send[3 * NE : QKV_ROWS, cut] = jnp.concatenate(
            [ql_v[0, :, cut].astype(F32), pair[:, 0], pair[0:16, 1]], axis=0
        ).astype(BF16)
    exchange(*QKV)

    arrive(*META)

    tokens = meta_recv[...].astype(F32)

    def spread(first, shift):
        lane = iota((N, E), 1)
        mine = (lane >> shift) == iota((N, E), 0)
        wide = jnp.concatenate(
            [jnp.where(mine, tokens[j, first : first + 1], 0.0) for j in range(N)], axis=0
        )
        low = (1 << shift) - 1
        same = onehot((iota((E, E), 0) & low) == (iota((E, E), 1) & low))
        wide = dot(wide.astype(BF16), same)
        total = jnp.zeros((N, E), F32)
        for j in range(N):
            total += jnp.where((lane >> shift) == j, wide[j * N : (j + 1) * N], 0.0)
        return total

    token_e = spread(8, 3)
    token_l = spread(12, 2)

    def tables(token, shift, slots, padded):
        peak = 1 << shift
        valid = onehot(token > 0.0)
        src, dst = iota((E, E), 0), iota((E, E), 1)
        offset = dot(valid, onehot((src >> shift) < (dst >> shift)))[0:1].astype(I32)
        in_lane = iota((1, E), 1)
        slot = jnp.where(token[0:1] > 0.0, offset + (in_lane & (peak - 1)), -1)
        select = onehot(iota((padded, E), 0) == slot)
        low = token.astype(BF16)
        high = jnp.where(token > 0.0, (iota((N, E), 1) >> shift).astype(F32), 0.0).astype(BF16)
        cols = dot_nt(select, high) * 256.0 + dot_nt(select, low) - 1.0
        total = N * slots
        mult = 1366 if slots == NE else 2731
        in_row = iota((padded, total), 1)
        tile = onehot(in_row - ((in_row * mult) >> 16) * slots == iota((padded, total), 0))
        wide_high = dot(dot_nt(high, select).astype(BF16), tile)
        wide_low = dot(dot_nt(low, select).astype(BF16), tile)
        in_row = iota((N, total), 1)
        mine = ((in_row * mult) >> 16) == iota((N, total), 0)
        row = jnp.sum(
            jnp.where(mine, wide_high * 256.0 + wide_low - 1.0, 0.0), axis=0, keepdims=True
        )
        src, dst = iota((E, TOK), 0), iota((E, TOK), 1)
        offset = dot(valid, onehot((src >> shift) < (dst >> 4)))[0:1].astype(I32)
        count = dot(valid, onehot((src >> shift) == (dst >> 4)))[0:1].astype(I32)
        in_lane = iota((1, TOK), 1)
        rank = in_lane & (peak - 1)
        slot = jnp.where(rank < count, offset + rank, -1)
        part = (in_lane & 15) >> shift
        return cols, row, slot, part

    cols_e, row_e, slot_e, part_e = tables(token_e, 3, NE, NE)
    cols_l, row_l, slot_l, part_l = tables(token_l, 2, NL, NLP)

    arrive(*ROW)
    for h in range(2):
        pick = onehot((iota((NE, TOK), 0) == slot_e) & (part_e == h))
        got = dot(pick, rows_recv[:, :, 0:1024].reshape(TOK, 1024))
        rows_all[d, 0:NE, h * 1024 : (h + 1) * 1024] = got.astype(BF16)
    for q in range(4):
        pick = onehot((iota((NLP, TOK), 0) == slot_l) & (part_l == q))
        got = dot(pick, rows_recv[:, :, 1024:1536].reshape(TOK, 512))
        rows_all[d, NE:ROWS, q * 512 : (q + 1) * 512] = got.astype(BF16)

    def gather(block, kind, to_dp, half=None):
        part = rows_all.at[block]
        if half is not None:
            part = part.at[:, half * 1024 : (half + 1) * 1024]
        return pltpu.make_async_remote_copy(
            src_ref=part,
            dst_ref=part,
            send_sem=gsend,
            recv_sem=grecv.at[kind],
            device_id=(to_dp, s),
            device_id_type=MESH,
        )

    ahead, behind, far = same_core(1), same_core(3), same_core(2)
    FROM_BEHIND, FROM_AHEAD, FROM_FAR, FROM_PARTNER = range(4)
    gather(d, FROM_BEHIND, ahead).start()
    gather(d, FROM_AHEAD, behind).start()
    gather(d, FROM_PARTNER, partner).start()

    def gather_near():
        wait_bytes(rows_all.at[behind], grecv.at[FROM_BEHIND])
        gather(behind, FROM_FAR, ahead, 1).start()
        gather(behind, FROM_PARTNER, partner).start()
        wait_bytes(rows_all.at[ahead], grecv.at[FROM_AHEAD])
        gather(ahead, FROM_FAR, behind, 0).start()
        gather(ahead, FROM_PARTNER, partner).start()

    def gather_far():
        wait_bytes(rows_all.at[far], grecv.at[FROM_FAR])
        gather(far, FROM_PARTNER, partner).start()

    weight_copy.wait()
    mine = rows_all[d]
    for c in range(8):
        part = dot_nt(mine, wv[c * 256 : (c + 1) * 256, :])
        dout_send[:, c * 256 : (c + 1) * 256] = part.astype(BF16)
    exchange(*DOUT)

    arrive(*QKV)

    def late(wide, part):
        return wide[:, part * NL : (part + 1) * NL].reshape(KL, E)

    def softmax(query, key, value, row, col):
        scores = dot_nt(query, key) * SCALE
        scores = jnp.where(row <= col, scores, -1e30)
        top = jnp.max(scores, axis=1, keepdims=True)
        weights = jnp.exp(scores - top)
        probs = weights / jnp.sum(weights, axis=1, keepdims=True)
        probs_bf = probs.astype(BF16)
        return probs, probs_bf, dot(probs_bf, value)

    def attended_out(first, last):
        def copy(to):
            return remote(
                att_send.at[to, first:last], att_recv.at[d, parity, first:last], ATT, to, target_dp
            )

        for dz, dy in OTHERS:
            copy(other(dz, dy)).start()

        @pl.when(target_dp == d)
        def _():
            pltpu.make_async_copy(
                att_send.at[s, first:last], att_recv.at[d, parity, first:last], recv.at[ATT]
            ).start()

        @pl.when(target_dp != d)
        def _():
            copy(s).start()

    key_e = qkv_recv[:, NE : 2 * NE, :].reshape(KE, E)
    value_e = qkv_recv[:, 2 * NE : 3 * NE, :].reshape(KE, E)
    for b in range(4):
        query = qkv_recv[4 * b : 4 * b + 4, 0:NE, :].reshape(4 * NE, E)
        col = jnp.concatenate([cols_e[:, o : o + 1] for o in range(4 * b, 4 * b + 4)], axis=0)
        probs, probs_bf, attended = softmax(query, key_e, value_e, row_e, col)
        probs_e[b * 192 : (b + 1) * 192] = probs
        probs_bf_e[b * 192 : (b + 1) * 192] = probs_bf
        att_send[4 * b : 4 * b + 4, 0:NE, :] = attended.reshape(4, NE, E).astype(BF16)
    attended_out(0, NE)
    gather_near()
    wide = jnp.concatenate(
        [qkv_recv[:, 3 * NE : QKV_ROWS, :].astype(F32), meta_recv[:, 0:8, :].astype(F32)], axis=1
    )
    query_l, key_l, value_l = (late(wide, part).astype(BF16) for part in range(3))
    gap = jnp.zeros((8, NLP - NL, E), F32)
    for b in range(2):
        query = query_l[b * 192 : (b + 1) * 192]
        col = jnp.concatenate([cols_l[0:NL, o : o + 1] for o in range(8 * b, 8 * b + 8)], axis=0)
        probs, probs_bf, attended = softmax(query, key_l, value_l, row_l, col)
        probs_l[b * 192 : (b + 1) * 192] = probs
        probs_bf_l[b * 192 : (b + 1) * 192] = probs_bf
        attended = jnp.concatenate([attended.reshape(8, NL, E), gap], axis=1)
        att_send[8 * b : 8 * b + 8, NE:ROWS, :] = attended.astype(BF16)
    attended_out(NE, ROWS)

    arrive(*DOUT)
    dout_e = dout_recv[:, 0:NE, :].reshape(KE, E)
    for c in range(2):
        dvalue = dot_tn(probs_bf_e[:, c * 384 : (c + 1) * 384], dout_e)
        dqkv_send[8 * c : 8 * c + 8, 2 * NE : 3 * NE, :] = dvalue.reshape(8, NE, E).astype(BF16)
    exchange(*GRAD_V)

    def backward(query, key, value, dout, attended, probs):
        delta = jnp.sum(dout.astype(F32) * attended.astype(F32), axis=1, keepdims=True)
        dprobs = dot_nt(dout, value)
        dscores = (probs * (dprobs - delta)).astype(BF16)
        return dscores, dot(dscores, key) * SCALE

    for b in range(4):
        dout = dout_recv[4 * b : 4 * b + 4, 0:NE, :].reshape(192, E)
        attended = att_send[4 * b : 4 * b + 4, 0:NE, :].reshape(192, E)
        query = None
        dscores, dquery = backward(
            query, key_e, value_e, dout, attended, probs_e[b * 192 : (b + 1) * 192]
        )
        ds_e[b * 192 : (b + 1) * 192] = dscores
        dqkv_send[4 * b : 4 * b + 4, 0:NE, :] = dquery.reshape(4, NE, E).astype(BF16)
    query_e = qkv_recv[:, 0:NE, :].reshape(KE, E)
    for c in range(2):
        dkey = dot_tn(ds_e[:, c * 384 : (c + 1) * 384], query_e) * SCALE
        dqkv_send[8 * c : 8 * c + 8, NE : 2 * NE, :] = dkey.reshape(8, NE, E).astype(BF16)
    exchange(*GRAD_K)
    dout_l = late(dout_recv[:, NE:ROWS, :].astype(F32), 0).astype(BF16)
    attended_l = late(att_send[:, NE:ROWS, :].astype(F32), 0)
    dquery_l = []
    for b in range(2):
        dscores, dquery = backward(
            None, key_l, value_l, dout_l[b * 192 : (b + 1) * 192],
            attended_l[b * 192 : (b + 1) * 192], probs_l[b * 192 : (b + 1) * 192]
        )
        ds_l[b * 192 : (b + 1) * 192] = dscores
        dquery_l.append(dquery)
    dquery = jnp.concatenate(dquery_l, axis=0)
    dkey = dot_tn(ds_l[...], query_l) * SCALE
    dvalue = dot_tn(probs_bf_l[...], dout_l)
    parts = [part.reshape(N, NL, E) for part in (dquery, dkey, dvalue)]
    parts.append(jnp.zeros((N, 8, E), F32))
    dqkv_send[:, 3 * NE : GRAD_ROWS, :] = jnp.concatenate(parts, axis=1).astype(BF16)
    exchange(*GRAD_LATE)
    gather_far()

    wait_bytes(att_recv, recv.at[ATT])
    wait_bytes(rows_all.at[0:4], grecv.at[FROM_PARTNER])
    def along(half, stage, i):
        if half == stage:
            to = lax.rem(z + i, 4)
            return to, to * 4 + y
        to = lax.rem(y + i, 4)
        return to, z * 4 + to

    def sum_copy(half, stage, i):
        source, target = (sum1_send, sum1_recv) if stage == 0 else (sum2_send, sums)
        to, device = along(half, stage, i)
        return pltpu.make_async_remote_copy(
            src_ref=source.at[half, to],
            dst_ref=target.at[half, i - 1],
            send_sem=sum_send.at[stage],
            recv_sem=sum_recv.at[stage, half],
            device_id=(d, device),
            device_id_type=MESH,
        )

    rows = rows_all[...].reshape(DP * ROWS, W)
    columns_of = [att_recv[:, p].reshape(DP * ROWS, E) for p in range(2)]
    for half in range(2):
        for p in range(2):
            for c in range(2):
                cut, first = slice(c * 512, (c + 1) * 512), half * 1024 + c * 512
                part = dot_tn(columns_of[p], rows[:, first : first + 512])
                part = part.reshape(2, 4, 16, 512).astype(BF16)
                if half == 0:
                    sum1_send[0, 2 * p : 2 * p + 2, :, :, cut] = part
                else:
                    for i in range(2):
                        for j in range(4):
                            sum1_send[1, j, 2 * p + i, :, cut] = part[i, j]
        for i in (2, 1, 3):
            sum_copy(half, 0, i).start()
    exchange(*GRAD_Q)
    for half in range(2):
        wait_bytes(sum1_recv.at[half], sum_recv.at[0, half])
        total = sum1_send[half, z if half == 0 else y].astype(F32)
        for i in range(3):
            total += sum1_recv[half, i].astype(F32)
        sum2_send[half] = total.astype(BF16)
        for i in (2, 1, 3):
            sum_copy(half, 1, i).start()
        own = sum2_send.at[half, along(half, 1, 0)[0]]
        pltpu.make_async_copy(own, sums.at[half, 3], sum_recv.at[1, half]).start()

    wait_bytes(meta_recv.at[1:N], send.at[META[0]])
    wait_bytes(rows_recv.at[1:N], send.at[ROW[0]])
    wait_bytes(qkv_recv.at[1:N], send.at[QKV[0]])
    wait_bytes(dout_recv.at[1:N], send.at[DOUT[0]])

    @pl.when(target_dp == d)
    def _():
        wait_bytes(att_send.at[1:N], send.at[ATT])

    @pl.when(target_dp != d)
    def _():
        wait_bytes(att_send, send.at[ATT])

    wait_bytes(rows_all.at[1:DP], gsend)
    wait_bytes(sum1_recv, sum_send.at[0])

    writes = []

    def write(source, target):
        writes.append(pltpu.make_async_copy(source, target, local_sem.at[len(writes)]))
        writes[-1].start()

    arrive(*GRAD_LATE)
    for c in range(4):
        cut = slice(c * 512, (c + 1) * 512)
        wide = out[3 * NE : GRAD_ROWS, cut].astype(F32)
        dql_v[0, :, cut] = wide[0:NL].astype(BF16)
        dkvl_v[0, :, :, cut] = jnp.stack(
            [wide[NL : 2 * NL].astype(BF16), wide[2 * NL : 3 * NL].astype(BF16)], axis=1
        )
    write(dql_v, dquery_late)
    write(dkvl_v, dkeyval_late)
    arrive(*GRAD_V)
    arrive(*GRAD_K)
    dkve_v[0] = jnp.stack([out[NE : 2 * NE], out[2 * NE : 3 * NE]], axis=1)
    write(dkve_v, dkeyval_early)
    for grad, (first, last) in (
        (GRAD_Q, (0, NE)),
        (GRAD_LATE, (3 * NE, GRAD_ROWS)),
        (GRAD_K, (NE, 2 * NE)),
        (GRAD_V, (2 * NE, 3 * NE)),
    ):
        wait_bytes(dqkv_send.at[1:N, first:last], send.at[grad[0]])
    for copy in writes:
        copy.wait()
    arrive(*GRAD_Q)
    wait_bytes(sums.at[:, 0:3], sum_send.at[1])
    for half in range(2):
        wait_bytes(sums.at[half], sum_recv.at[1, half])


def finish(*refs):
    sources, targets, held, dw_v, sem = refs[0:5], refs[5:10], refs[10:15], refs[15], refs[16]
    order = (4, 1, 3, 0, 2)
    loads = {i: pltpu.make_async_copy(sources[i], held[i], sem.at[i]) for i in order}
    stores = {
        i: pltpu.make_async_copy(dw_v if i == 4 else held[i], targets[i], sem.at[5 + i])
        for i in order
    }
    for i in order:
        loads[i].start()
    for i in (1, 3, 0, 2):
        loads[i].wait()
        stores[i].start()
    loads[4].wait()
    for half in range(2):
        total = held[4][half, 3].astype(F32)
        for i in range(3):
            total += held[4][half, i].astype(F32)
        dw_v[:, half * 1024 : (half + 1) * 1024] = total
    stores[4].start()
    for i in order:
        stores[i].wait()


def shards(
    depths, owners, cotangent, query_early, keyval_early, query_late, keyval_late, out_weight
):
    hbm = pl.BlockSpec(memory_space=pl.ANY)
    results = (
        jax.ShapeDtypeStruct(query_early.shape, BF16),
        jax.ShapeDtypeStruct(keyval_early.shape, BF16),
        jax.ShapeDtypeStruct(query_late.shape, BF16),
        jax.ShapeDtypeStruct(keyval_late.shape, BF16),
        jax.ShapeDtypeStruct((N, W), F32),
    )
    between = results[0:4] + (jax.ShapeDtypeStruct((2, 4, 16, W // 2), BF16),)
    outputs = pl.pallas_call(
        kernel,
        out_shape=between,
        in_specs=[hbm] * 8,
        out_specs=(hbm,) * 5,
        scratch_shapes=[
            pltpu.VMEM((1, TOK), I32),
            pltpu.VMEM((2, 1, TOK), I32),
            pltpu.VMEM((2, TOK, W), BF16),
            pltpu.VMEM((W, W), BF16),
            pltpu.VMEM((1, NL, W), BF16),
            pltpu.VMEM((1, NE, 2, W), BF16),
            pltpu.VMEM((1, NL, 2, W), BF16),
            pltpu.VMEM((QKV_ROWS, W), BF16),
            pltpu.VMEM((N, 16, 1536), BF16),
            pltpu.VMEM((N, 16, 1536), BF16),
            pltpu.VMEM((16, W), BF16),
            pltpu.VMEM((N, 16, E), BF16),
            pltpu.VMEM((N, QKV_ROWS, E), BF16),
            pltpu.VMEM((DP, ROWS, W), BF16),
            pltpu.VMEM((ROWS, W), BF16),
            pltpu.VMEM((N, ROWS, E), BF16),
            pltpu.VMEM((N, ROWS, E), BF16),
            pltpu.VMEM((DP, 2, ROWS, E), BF16),
            pltpu.VMEM((N, GRAD_ROWS, E), BF16),
            pltpu.VMEM((2, 4, 4, 16, W // 2), BF16),
            pltpu.VMEM((2, 3, 4, 16, W // 2), BF16),
            pltpu.VMEM((2, 4, 16, W // 2), BF16),
            pltpu.VMEM((GRAD_ROWS, W), BF16),
            pltpu.VMEM((1, NE, 2, W), BF16),
            pltpu.VMEM((1, NL, W), BF16),
            pltpu.VMEM((1, NL, 2, W), BF16),
            pltpu.VMEM((KE, KE), F32),
            pltpu.VMEM((KE, KE), BF16),
            pltpu.VMEM((KE, KE), BF16),
            pltpu.VMEM((KL, KL), F32),
            pltpu.VMEM((KL, KL), BF16),
            pltpu.VMEM((KL, KL), BF16),
            pltpu.SemaphoreType.DMA((12,)),
            pltpu.SemaphoreType.DMA((9,)),
            pltpu.SemaphoreType.DMA((9,)),
            pltpu.SemaphoreType.DMA,
            pltpu.SemaphoreType.DMA((4,)),
            pltpu.SemaphoreType.DMA((2,)),
            pltpu.SemaphoreType.DMA((2, 2)),
        ],
        compiler_params=pltpu.CompilerParams(
            collective_id=0, has_side_effects=True, vmem_limit_bytes=56 * 1024 * 1024
        ),
        cost_estimate=pl.CostEstimate(
            flops=3_000_000_000, bytes_accessed=20_000_000, transcendentals=800_000
        ),
        name="rows_attention_weight",
    )(
        depths, owners, cotangent, query_early, keyval_early, query_late, keyval_late,
        out_weight,
    )
    return pl.pallas_call(
        finish,
        out_shape=results,
        in_specs=[hbm] * 5,
        out_specs=(hbm,) * 5,
        scratch_shapes=[pltpu.VMEM(array.shape, array.dtype) for array in between]
        + [pltpu.VMEM((N, W), F32), pltpu.SemaphoreType.DMA((10,))],
        compiler_params=pltpu.CompilerParams(vmem_limit_bytes=56 * 1024 * 1024),
        name="outputs",
    )(*outputs)


def solution(mesh):
    in_specs = (
        P("dp", "seq"),
        P(None, "dp", "seq"),
        P(None, "dp", "seq", None),
        P("dp", "seq", None),
        P("dp", "seq", None, None),
        P("dp", "seq", None),
        P("dp", "seq", None, None),
        P(),
    )
    out_specs = (
        P("dp", "seq", None),
        P("dp", "seq", None, None),
        P("dp", "seq", None),
        P("dp", "seq", None, None),
        P(("dp", "seq"), None),
    )
    return jax.shard_map(shards, mesh=mesh, in_specs=in_specs, out_specs=out_specs, check_vma=False)
```

```python
import jax
import jax.numpy as jnp
from jax import lax
from jax.experimental import pallas as pl
from jax.experimental.pallas import tpu as pltpu
from jax.sharding import PartitionSpec as P

MESH = pl.DeviceIdType.MESH
F32, BF16, I32 = jnp.float32, jnp.bfloat16, jnp.int32

N = 16
DP = 8
E = 128
W = 2048
TOK = 256
NE, NL = 48, 24
NLP = 32
ROWS = NE + NLP
GRAD_ROWS = 3 * NE + 80
QKV_ROWS = 3 * NE + 64
OTHERS = (
    (2, 2), (1, 2), (2, 1), (2, 3), (3, 2), (0, 2), (2, 0), (1, 1),
    (3, 3), (1, 3), (3, 1), (0, 1), (1, 0), (0, 3), (3, 0),
)
KE, KL = N * NE, N * NL
SCALE = E**-0.5


def dot(a, b):
    return lax.dot_general(a, b, (((1,), (0,)), ((), ())), preferred_element_type=F32)


def dot_nt(a, b):
    return lax.dot_general(a, b, (((1,), (1,)), ((), ())), preferred_element_type=F32)


def dot_tn(a, b):
    return lax.dot_general(a, b, (((0,), (0,)), ((), ())), preferred_element_type=F32)


def iota(shape, dim):
    return lax.broadcasted_iota(I32, shape, dim)


def onehot(mask):
    return jnp.where(mask, 1.0, 0.0).astype(BF16)


def kernel(
    depths, owners, cot, query_early, keyval_early, query_late, keyval_late, weight,
    dquery_early, dkeyval_early, dquery_late, dkeyval_late, sums,
    depth_v, owner_v, cotv, wv, ql_v, kve_v, kvl_v, qkv_send,
    rows_send, rows_recv, meta_send, meta_recv, qkv_recv, rows_all,
    dout_send, dout_recv, att_send, att_recv, dqkv_send,
    sum1_send, sum1_recv, sum2_send,
    out, dkve_v, dql_v, dkvl_v,
    probs_e, probs_bf_e, ds_e, probs_l, probs_bf_l, ds_l,
    local_sem, send, recv, gsend, grecv, sum_send, sum_recv,
):
    d = lax.axis_index("dp")
    s = lax.axis_index("seq")
    chip = lax.div(d, 2)
    core = lax.rem(d, 2)
    partner = chip * 2 + 1 - core
    z, y = lax.div(s, 4), lax.rem(s, 4)

    def head_of(j):
        return lax.rem(chip + lax.div(j, 4) + 2 * core, 4) * 4 + lax.rem(j, 4)

    def same_core(i):
        return lax.rem(chip + i, 4) * 2 + core

    my_head = head_of(s)
    target_dp = lax.div(my_head, 2)
    parity = lax.rem(my_head, 2)

    cot_copies = [
        pltpu.make_async_copy(
            cot.at[r, 0, pl.ds(i * 128, 128)], cotv.at[r, pl.ds(i * 128, 128)],
            local_sem.at[8 + 2 * r + i],
        )
        for r in range(2)
        for i in range(2)
    ]
    weight_copy = pltpu.make_async_copy(weight, wv, local_sem.at[1])
    routing = [
        pltpu.make_async_copy(depths, depth_v, local_sem.at[6]),
        pltpu.make_async_copy(owners, owner_v, local_sem.at[7]),
    ]
    late_copy = pltpu.make_async_copy(keyval_late, kvl_v, local_sem.at[3])
    operands = [
        pltpu.make_async_copy(keyval_early, kve_v, local_sem.at[2]),
        pltpu.make_async_copy(query_late, ql_v, local_sem.at[5]),
        pltpu.make_async_copy(query_early.at[0], qkv_send.at[0:NE], local_sem.at[4]),
    ]
    for copy in routing + [late_copy] + cot_copies + operands + [weight_copy]:
        copy.start()

    barrier = pltpu.get_barrier_semaphore()

    def greet(to_dp, to_seq):
        pl.semaphore_signal(barrier, inc=1, device_id=(to_dp, to_seq), device_id_type=MESH)

    for i in range(1, N):
        greet(d, lax.rem(s + i, N))
    greet(partner, s)
    for i in (1, 3):
        greet(same_core(i), s)
    for from_dp in range(DP):
        turn = lax.rem(chip + 8 - from_dp // 2 - 2 * (from_dp % 2), 4)
        for p in range(2):
            from_seq = turn * 4 + 2 * core + p

            @pl.when(jnp.logical_or(d != from_dp, from_seq != s))
            def _(from_dp=from_dp, from_seq=from_seq):
                greet(from_dp, from_seq)

    for copy in routing:
        copy.wait()
    depth = depth_v[...]
    active_e, active_l = depth > 1, depth > 2
    owner_e, owner_l = owner_v[0], owner_v[1]
    flags = jnp.where(
        iota((16, TOK), 0) < 8,
        jnp.broadcast_to(active_e.astype(F32), (16, TOK)),
        jnp.broadcast_to(active_l.astype(F32), (16, TOK)),
    ).astype(BF16)
    below = onehot(iota((TOK, TOK), 0) < iota((TOK, TOK), 1))
    before = dot(flags, below).astype(I32)
    rank_e, rank_l = before[0:1] >> 4, before[8:9] >> 4
    token = (iota((8, TOK), 1) + 1).astype(F32).astype(BF16)
    line = iota((E, TOK), 0)
    meta_e = dot_nt(token, onehot((line == owner_e * 8 + rank_e) & active_e))
    meta_l = dot_nt(token, onehot((line == owner_l * 4 + rank_l) & active_l))
    meta = jnp.where(iota((8, E), 0) < 4, meta_e, meta_l)
    late_copy.wait()
    meta_send[...] = jnp.concatenate(
        [kvl_v[0, 16:NL, 1, :].astype(F32), jnp.concatenate([meta] * N, axis=1)], axis=0
    ).astype(BF16)

    for copy in cot_copies[0:2]:
        copy.wait()
    line = iota((TOK, TOK), 0)
    base = jnp.where(active_e, owner_e * 16 + rank_e, -64)
    packed = dot(onehot(line == base), cotv[0, :, 0:1024])
    packed += dot(onehot(line == base + 8), cotv[0, :, 1024:2048])
    rows_send[:, :, 0:1024] = packed.reshape(N, 16, 1024).astype(BF16)
    for copy in cot_copies[2:4]:
        copy.wait()
    base = jnp.where(active_l, owner_l * 16 + rank_l, -64)
    packed = dot(onehot(line == base), cotv[1, :, 0:512])
    for q in range(1, 4):
        packed += dot(onehot(line == base + 4 * q), cotv[1, :, q * 512 : (q + 1) * 512])
    rows_send[:, :, 1024:1536] = packed.reshape(N, 16, 512).astype(BF16)

    elsewhere = jnp.where(target_dp == d, 0, 1)
    pl.semaphore_wait(barrier, N - 1 + 3 + N - 1 + elsewhere)

    def remote(src, dst, phase, to, to_dp):
        return pltpu.make_async_remote_copy(
            src_ref=src,
            dst_ref=dst,
            send_sem=send.at[phase],
            recv_sem=recv.at[phase],
            device_id=(to_dp, to),
            device_id_type=MESH,
        )

    def wait_bytes(ref, sem):
        pltpu.make_async_copy(ref, ref, sem).wait()

    def other(dz, dy):
        to_z = lax.rem(z + jnp.where(core == 0, dz, 4 - dz), 4)
        to_y = lax.rem(y + jnp.where(core == 0, dy, 4 - dy), 4)
        return to_z * 4 + to_y

    def exchange(phase, src, dst, whole):
        for dz, dy in OTHERS:
            to = other(dz, dy)
            remote(src(to), dst(s), phase, to, d).start()
        pltpu.make_async_copy(src(s), dst(s), recv.at[phase]).start()

    def arrive(phase, src, dst, whole):
        wait_bytes(whole, recv.at[phase])

    def columns(ref, j):
        return ref.at[:, pl.ds(pl.multiple_of(head_of(j) * E, E), E)]

    META = (0, lambda j: columns(meta_send, j), lambda j: meta_recv.at[j], meta_recv)
    ROW = (1, lambda j: rows_send.at[j], lambda j: rows_recv.at[j], rows_recv)
    QKV = (2, lambda j: columns(qkv_send, j), lambda j: qkv_recv.at[j], qkv_recv)
    DOUT = (3, lambda j: columns(dout_send, j), lambda j: dout_recv.at[j], dout_recv)

    def grads(phase, first, last):
        return (
            phase,
            lambda j: dqkv_send.at[j, first:last],
            lambda j: columns(out.at[first:last], j),
            out.at[first:last],
        )

    GRAD_Q = (
        4,
        lambda j: dqkv_send.at[j, 0:NE],
        lambda j: columns(dquery_early.at[0], j),
        dquery_early.at[0],
    )
    GRAD_LATE = grads(5, 3 * NE, GRAD_ROWS)
    GRAD_K, GRAD_V = grads(6, NE, 2 * NE), grads(7, 2 * NE, 3 * NE)
    ATT = 8

    exchange(*META)
    exchange(*ROW)
    for copy in operands:
        copy.wait()
    qkv_send[NE : 2 * NE] = kve_v[0, :, 0, :]
    qkv_send[2 * NE : 3 * NE] = kve_v[0, :, 1, :]
    for c in range(4):
        cut = slice(c * 512, (c + 1) * 512)
        pair = kvl_v[0, :, :, cut].astype(F32)
        qkv_send[3 * NE : QKV_ROWS, cut] = jnp.concatenate(
            [ql_v[0, :, cut].astype(F32), pair[:, 0], pair[0:16, 1]], axis=0
        ).astype(BF16)
    exchange(*QKV)

    arrive(*META)

    tokens = meta_recv[...].astype(F32)

    def spread(first, shift):
        lane = iota((N, E), 1)
        mine = (lane >> shift) == iota((N, E), 0)
        wide = jnp.concatenate(
            [jnp.where(mine, tokens[j, first : first + 1], 0.0) for j in range(N)], axis=0
        )
        low = (1 << shift) - 1
        same = onehot((iota((E, E), 0) & low) == (iota((E, E), 1) & low))
        wide = dot(wide.astype(BF16), same)
        total = jnp.zeros((N, E), F32)
        for j in range(N):
            total += jnp.where((lane >> shift) == j, wide[j * N : (j + 1) * N], 0.0)
        return total

    token_e = spread(8, 3)
    token_l = spread(12, 2)

    def tables(token, shift, slots, padded):
        peak = 1 << shift
        valid = onehot(token > 0.0)
        src, dst = iota((E, E), 0), iota((E, E), 1)
        offset = dot(valid, onehot((src >> shift) < (dst >> shift)))[0:1].astype(I32)
        in_lane = iota((1, E), 1)
        slot = jnp.where(token[0:1] > 0.0, offset + (in_lane & (peak - 1)), -1)
        select = onehot(iota((padded, E), 0) == slot)
        low = token.astype(BF16)
        high = jnp.where(token > 0.0, (iota((N, E), 1) >> shift).astype(F32), 0.0).astype(BF16)
        cols = dot_nt(select, high) * 256.0 + dot_nt(select, low) - 1.0
        total = N * slots
        mult = 1366 if slots == NE else 2731
        in_row = iota((padded, total), 1)
        tile = onehot(in_row - ((in_row * mult) >> 16) * slots == iota((padded, total), 0))
        wide_high = dot(dot_nt(high, select).astype(BF16), tile)
        wide_low = dot(dot_nt(low, select).astype(BF16), tile)
        in_row = iota((N, total), 1)
        mine = ((in_row * mult) >> 16) == iota((N, total), 0)
        row = jnp.sum(
            jnp.where(mine, wide_high * 256.0 + wide_low - 1.0, 0.0), axis=0, keepdims=True
        )
        src, dst = iota((E, TOK), 0), iota((E, TOK), 1)
        offset = dot(valid, onehot((src >> shift) < (dst >> 4)))[0:1].astype(I32)
        count = dot(valid, onehot((src >> shift) == (dst >> 4)))[0:1].astype(I32)
        in_lane = iota((1, TOK), 1)
        rank = in_lane & (peak - 1)
        slot = jnp.where(rank < count, offset + rank, -1)
        part = (in_lane & 15) >> shift
        return cols, row, slot, part

    cols_e, row_e, slot_e, part_e = tables(token_e, 3, NE, NE)
    cols_l, row_l, slot_l, part_l = tables(token_l, 2, NL, NLP)

    arrive(*ROW)
    for h in range(2):
        pick = onehot((iota((NE, TOK), 0) == slot_e) & (part_e == h))
        got = dot(pick, rows_recv[:, :, 0:1024].reshape(TOK, 1024))
        rows_all[d, 0:NE, h * 1024 : (h + 1) * 1024] = got.astype(BF16)
    for q in range(4):
        pick = onehot((iota((NLP, TOK), 0) == slot_l) & (part_l == q))
        got = dot(pick, rows_recv[:, :, 1024:1536].reshape(TOK, 512))
        rows_all[d, NE:ROWS, q * 512 : (q + 1) * 512] = got.astype(BF16)

    def block_part(block, half):
        part = rows_all.at[block]
        return part if half is None else part.at[:, half * 1024 : (half + 1) * 1024]

    def gather(block, kind, to_dp, half=None):
        part = block_part(block, half)
        return pltpu.make_async_remote_copy(
            src_ref=part,
            dst_ref=part,
            send_sem=gsend,
            recv_sem=grecv.at[kind],
            device_id=(to_dp, s),
            device_id_type=MESH,
        )

    ahead, behind, far = same_core(1), same_core(3), same_core(2)
    FROM_FAR, FROM_PARTNER = 4, 5
    gather(d, 0, ahead, 1).start()
    gather(d, 1, behind, 0).start()
    gather(d, 2, ahead, 0).start()
    gather(d, 3, behind, 1).start()
    gather(d, FROM_PARTNER, partner).start()

    def gather_pass():
        wait_bytes(block_part(behind, 1), grecv.at[0])
        gather(behind, FROM_FAR, ahead, 1).start()
        wait_bytes(block_part(ahead, 0), grecv.at[1])
        gather(ahead, FROM_FAR, behind, 0).start()

    def gather_near():
        wait_bytes(block_part(behind, 0), grecv.at[2])
        gather(behind, FROM_PARTNER, partner).start()
        wait_bytes(block_part(ahead, 1), grecv.at[3])
        gather(ahead, FROM_PARTNER, partner).start()

    def gather_far():
        wait_bytes(rows_all.at[far], grecv.at[FROM_FAR])
        gather(far, FROM_PARTNER, partner).start()

    weight_copy.wait()
    mine = rows_all[d]
    for c in range(8):
        part = dot_nt(mine, wv[c * 256 : (c + 1) * 256, :])
        dout_send[:, c * 256 : (c + 1) * 256] = part.astype(BF16)
    exchange(*DOUT)

    gather_pass()
    arrive(*QKV)

    def late(wide, part):
        return wide[:, part * NL : (part + 1) * NL].reshape(KL, E)

    def softmax(query, key, value, row, col):
        scores = dot_nt(query, key) * SCALE
        scores = jnp.where(row <= col, scores, -1e30)
        top = jnp.max(scores, axis=1, keepdims=True)
        weights = jnp.exp(scores - top)
        probs = weights / jnp.sum(weights, axis=1, keepdims=True)
        probs_bf = probs.astype(BF16)
        return probs, probs_bf, dot(probs_bf, value)

    def attended_out(first, last):
        def copy(to):
            return remote(
                att_send.at[to, first:last], att_recv.at[d, parity, first:last], ATT, to, target_dp
            )

        for dz, dy in OTHERS:
            copy(other(dz, dy)).start()

        @pl.when(target_dp == d)
        def _():
            pltpu.make_async_copy(
                att_send.at[s, first:last], att_recv.at[d, parity, first:last], recv.at[ATT]
            ).start()

        @pl.when(target_dp != d)
        def _():
            copy(s).start()

    key_e = qkv_recv[:, NE : 2 * NE, :].reshape(KE, E)
    value_e = qkv_recv[:, 2 * NE : 3 * NE, :].reshape(KE, E)
    for b in range(4):
        query = qkv_recv[4 * b : 4 * b + 4, 0:NE, :].reshape(4 * NE, E)
        col = jnp.concatenate([cols_e[:, o : o + 1] for o in range(4 * b, 4 * b + 4)], axis=0)
        probs, probs_bf, attended = softmax(query, key_e, value_e, row_e, col)
        probs_e[b * 192 : (b + 1) * 192] = probs
        probs_bf_e[b * 192 : (b + 1) * 192] = probs_bf
        att_send[4 * b : 4 * b + 4, 0:NE, :] = attended.reshape(4, NE, E).astype(BF16)
    attended_out(0, NE)
    gather_near()
    wide = jnp.concatenate(
        [qkv_recv[:, 3 * NE : QKV_ROWS, :].astype(F32), meta_recv[:, 0:8, :].astype(F32)], axis=1
    )
    query_l, key_l, value_l = (late(wide, part).astype(BF16) for part in range(3))
    gap = jnp.zeros((8, NLP - NL, E), F32)
    for b in range(2):
        query = query_l[b * 192 : (b + 1) * 192]
        col = jnp.concatenate([cols_l[0:NL, o : o + 1] for o in range(8 * b, 8 * b + 8)], axis=0)
        probs, probs_bf, attended = softmax(query, key_l, value_l, row_l, col)
        probs_l[b * 192 : (b + 1) * 192] = probs
        probs_bf_l[b * 192 : (b + 1) * 192] = probs_bf
        attended = jnp.concatenate([attended.reshape(8, NL, E), gap], axis=1)
        att_send[8 * b : 8 * b + 8, NE:ROWS, :] = attended.astype(BF16)
    attended_out(NE, ROWS)

    arrive(*DOUT)
    dout_e = dout_recv[:, 0:NE, :].reshape(KE, E)
    for c in range(2):
        dvalue = dot_tn(probs_bf_e[:, c * 384 : (c + 1) * 384], dout_e)
        dqkv_send[8 * c : 8 * c + 8, 2 * NE : 3 * NE, :] = dvalue.reshape(8, NE, E).astype(BF16)
    exchange(*GRAD_V)

    def backward(query, key, value, dout, attended, probs):
        delta = jnp.sum(dout.astype(F32) * attended.astype(F32), axis=1, keepdims=True)
        dprobs = dot_nt(dout, value)
        dscores = (probs * (dprobs - delta)).astype(BF16)
        return dscores, dot(dscores, key) * SCALE

    for b in range(4):
        dout = dout_recv[4 * b : 4 * b + 4, 0:NE, :].reshape(192, E)
        attended = att_send[4 * b : 4 * b + 4, 0:NE, :].reshape(192, E)
        query = None
        dscores, dquery = backward(
            query, key_e, value_e, dout, attended, probs_e[b * 192 : (b + 1) * 192]
        )
        ds_e[b * 192 : (b + 1) * 192] = dscores
        dqkv_send[4 * b : 4 * b + 4, 0:NE, :] = dquery.reshape(4, NE, E).astype(BF16)
    query_e = qkv_recv[:, 0:NE, :].reshape(KE, E)
    for c in range(2):
        dkey = dot_tn(ds_e[:, c * 384 : (c + 1) * 384], query_e) * SCALE
        dqkv_send[8 * c : 8 * c + 8, NE : 2 * NE, :] = dkey.reshape(8, NE, E).astype(BF16)
    exchange(*GRAD_K)
    dout_l = late(dout_recv[:, NE:ROWS, :].astype(F32), 0).astype(BF16)
    attended_l = late(att_send[:, NE:ROWS, :].astype(F32), 0)
    dquery_l = []
    for b in range(2):
        dscores, dquery = backward(
            None, key_l, value_l, dout_l[b * 192 : (b + 1) * 192],
            attended_l[b * 192 : (b + 1) * 192], probs_l[b * 192 : (b + 1) * 192]
        )
        ds_l[b * 192 : (b + 1) * 192] = dscores
        dquery_l.append(dquery)
    dquery = jnp.concatenate(dquery_l, axis=0)
    dkey = dot_tn(ds_l[...], query_l) * SCALE
    dvalue = dot_tn(probs_bf_l[...], dout_l)
    parts = [part.reshape(N, NL, E) for part in (dquery, dkey, dvalue)]
    parts.append(jnp.zeros((N, 8, E), F32))
    dqkv_send[:, 3 * NE : GRAD_ROWS, :] = jnp.concatenate(parts, axis=1).astype(BF16)
    gather_far()

    wait_bytes(att_recv, recv.at[ATT])
    wait_bytes(rows_all.at[0:4], grecv.at[FROM_PARTNER])
    def along(half, stage, i):
        if half == stage:
            to = lax.rem(z + i, 4)
            return to, to * 4 + y
        to = lax.rem(y + i, 4)
        return to, z * 4 + to

    def sum_copy(half, stage, i):
        source, target = (sum1_send, sum1_recv) if stage == 0 else (sum2_send, sums)
        to, device = along(half, stage, i)
        return pltpu.make_async_remote_copy(
            src_ref=source.at[half, to],
            dst_ref=target.at[half, i - 1],
            send_sem=sum_send.at[stage],
            recv_sem=sum_recv.at[stage, half],
            device_id=(d, device),
            device_id_type=MESH,
        )

    rows = rows_all[...].reshape(DP * ROWS, W)
    columns_of = [att_recv[:, p].reshape(DP * ROWS, E) for p in range(2)]
    for half in range(2):
        for p in range(2):
            for c in range(2):
                cut, first = slice(c * 512, (c + 1) * 512), half * 1024 + c * 512
                part = dot_tn(columns_of[p], rows[:, first : first + 512])
                part = part.reshape(2, 4, 16, 512).astype(BF16)
                if half == 0:
                    sum1_send[0, 2 * p : 2 * p + 2, :, :, cut] = part
                else:
                    for i in range(2):
                        for j in range(4):
                            sum1_send[1, j, 2 * p + i, :, cut] = part[i, j]
        for i in (2, 1, 3):
            sum_copy(half, 0, i).start()
    exchange(*GRAD_LATE)
    exchange(*GRAD_Q)
    for half in range(2):
        wait_bytes(sum1_recv.at[half], sum_recv.at[0, half])
        total = sum1_send[half, z if half == 0 else y].astype(F32)
        for i in range(3):
            total += sum1_recv[half, i].astype(F32)
        sum2_send[half] = total.astype(BF16)
        for i in (2, 1, 3):
            sum_copy(half, 1, i).start()
        own = sum2_send.at[half, along(half, 1, 0)[0]]
        pltpu.make_async_copy(own, sums.at[half, 3], sum_recv.at[1, half]).start()

    wait_bytes(meta_recv.at[1:N], send.at[META[0]])
    wait_bytes(rows_recv.at[1:N], send.at[ROW[0]])
    wait_bytes(qkv_recv.at[1:N], send.at[QKV[0]])
    wait_bytes(dout_recv.at[1:N], send.at[DOUT[0]])

    @pl.when(target_dp == d)
    def _():
        wait_bytes(att_send.at[1:N], send.at[ATT])

    @pl.when(target_dp != d)
    def _():
        wait_bytes(att_send, send.at[ATT])

    wait_bytes(rows_all.at[1:DP], gsend)
    wait_bytes(sum1_recv, sum_send.at[0])

    writes = []

    def write(source, target):
        writes.append(pltpu.make_async_copy(source, target, local_sem.at[len(writes)]))
        writes[-1].start()

    arrive(*GRAD_V)
    arrive(*GRAD_K)
    dkve_v[0] = jnp.stack([out[NE : 2 * NE], out[2 * NE : 3 * NE]], axis=1)
    write(dkve_v, dkeyval_early)
    arrive(*GRAD_LATE)
    for c in range(4):
        cut = slice(c * 512, (c + 1) * 512)
        wide = out[3 * NE : GRAD_ROWS, cut].astype(F32)
        dql_v[0, :, cut] = wide[0:NL].astype(BF16)
        dkvl_v[0, :, :, cut] = jnp.stack(
            [wide[NL : 2 * NL].astype(BF16), wide[2 * NL : 3 * NL].astype(BF16)], axis=1
        )
    write(dql_v, dquery_late)
    write(dkvl_v, dkeyval_late)
    for grad, (first, last) in (
        (GRAD_Q, (0, NE)),
        (GRAD_LATE, (3 * NE, GRAD_ROWS)),
        (GRAD_K, (NE, 2 * NE)),
        (GRAD_V, (2 * NE, 3 * NE)),
    ):
        wait_bytes(dqkv_send.at[1:N, first:last], send.at[grad[0]])
    for copy in writes:
        copy.wait()
    arrive(*GRAD_Q)
    wait_bytes(sums.at[:, 0:3], sum_send.at[1])
    for half in range(2):
        wait_bytes(sums.at[half], sum_recv.at[1, half])


def finish(*refs):
    sources, targets, held, dw_v, sem = refs[0:5], refs[5:10], refs[10:15], refs[15], refs[16]
    order = (4, 1, 3, 0, 2)
    loads = {i: pltpu.make_async_copy(sources[i], held[i], sem.at[i]) for i in order}
    stores = {
        i: pltpu.make_async_copy(dw_v if i == 4 else held[i], targets[i], sem.at[5 + i])
        for i in order
    }
    for i in order:
        loads[i].start()
    for i in (1, 3, 0, 2):
        loads[i].wait()
        stores[i].start()
    loads[4].wait()
    for half in range(2):
        total = held[4][half, 3].astype(F32)
        for i in range(3):
            total += held[4][half, i].astype(F32)
        dw_v[:, half * 1024 : (half + 1) * 1024] = total
    stores[4].start()
    for i in order:
        stores[i].wait()


def shards(
    depths, owners, cotangent, query_early, keyval_early, query_late, keyval_late, out_weight
):
    hbm = pl.BlockSpec(memory_space=pl.ANY)
    results = (
        jax.ShapeDtypeStruct(query_early.shape, BF16),
        jax.ShapeDtypeStruct(keyval_early.shape, BF16),
        jax.ShapeDtypeStruct(query_late.shape, BF16),
        jax.ShapeDtypeStruct(keyval_late.shape, BF16),
        jax.ShapeDtypeStruct((N, W), F32),
    )
    between = results[0:4] + (jax.ShapeDtypeStruct((2, 4, 16, W // 2), BF16),)
    outputs = pl.pallas_call(
        kernel,
        out_shape=between,
        in_specs=[hbm] * 8,
        out_specs=(hbm,) * 5,
        scratch_shapes=[
            pltpu.VMEM((1, TOK), I32),
            pltpu.VMEM((2, 1, TOK), I32),
            pltpu.VMEM((2, TOK, W), BF16),
            pltpu.VMEM((W, W), BF16),
            pltpu.VMEM((1, NL, W), BF16),
            pltpu.VMEM((1, NE, 2, W), BF16),
            pltpu.VMEM((1, NL, 2, W), BF16),
            pltpu.VMEM((QKV_ROWS, W), BF16),
            pltpu.VMEM((N, 16, 1536), BF16),
            pltpu.VMEM((N, 16, 1536), BF16),
            pltpu.VMEM((16, W), BF16),
            pltpu.VMEM((N, 16, E), BF16),
            pltpu.VMEM((N, QKV_ROWS, E), BF16),
            pltpu.VMEM((DP, ROWS, W), BF16),
            pltpu.VMEM((ROWS, W), BF16),
            pltpu.VMEM((N, ROWS, E), BF16),
            pltpu.VMEM((N, ROWS, E), BF16),
            pltpu.VMEM((DP, 2, ROWS, E), BF16),
            pltpu.VMEM((N, GRAD_ROWS, E), BF16),
            pltpu.VMEM((2, 4, 4, 16, W // 2), BF16),
            pltpu.VMEM((2, 3, 4, 16, W // 2), BF16),
            pltpu.VMEM((2, 4, 16, W // 2), BF16),
            pltpu.VMEM((GRAD_ROWS, W), BF16),
            pltpu.VMEM((1, NE, 2, W), BF16),
            pltpu.VMEM((1, NL, W), BF16),
            pltpu.VMEM((1, NL, 2, W), BF16),
            pltpu.VMEM((KE, KE), F32),
            pltpu.VMEM((KE, KE), BF16),
            pltpu.VMEM((KE, KE), BF16),
            pltpu.VMEM((KL, KL), F32),
            pltpu.VMEM((KL, KL), BF16),
            pltpu.VMEM((KL, KL), BF16),
            pltpu.SemaphoreType.DMA((12,)),
            pltpu.SemaphoreType.DMA((9,)),
            pltpu.SemaphoreType.DMA((9,)),
            pltpu.SemaphoreType.DMA,
            pltpu.SemaphoreType.DMA((6,)),
            pltpu.SemaphoreType.DMA((2,)),
            pltpu.SemaphoreType.DMA((2, 2)),
        ],
        compiler_params=pltpu.CompilerParams(
            collective_id=0, has_side_effects=True, vmem_limit_bytes=56 * 1024 * 1024
        ),
        cost_estimate=pl.CostEstimate(
            flops=3_000_000_000, bytes_accessed=20_000_000, transcendentals=800_000
        ),
        name="rows_attention_weight",
    )(
        depths, owners, cotangent, query_early, keyval_early, query_late, keyval_late,
        out_weight,
    )
    return pl.pallas_call(
        finish,
        out_shape=results,
        in_specs=[hbm] * 5,
        out_specs=(hbm,) * 5,
        scratch_shapes=[pltpu.VMEM(array.shape, array.dtype) for array in between]
        + [pltpu.VMEM((N, W), F32), pltpu.SemaphoreType.DMA((10,))],
        compiler_params=pltpu.CompilerParams(vmem_limit_bytes=56 * 1024 * 1024),
        name="outputs",
    )(*outputs)


def solution(mesh):
    in_specs = (
        P("dp", "seq"),
        P(None, "dp", "seq"),
        P(None, "dp", "seq", None),
        P("dp", "seq", None),
        P("dp", "seq", None, None),
        P("dp", "seq", None),
        P("dp", "seq", None, None),
        P(),
    )
    out_specs = (
        P("dp", "seq", None),
        P("dp", "seq", None, None),
        P("dp", "seq", None),
        P("dp", "seq", None, None),
        P(("dp", "seq"), None),
    )
    return jax.shard_map(shards, mesh=mesh, in_specs=in_specs, out_specs=out_specs, check_vma=False)
```

```python
import jax
import jax.numpy as jnp
from jax import lax
from jax.experimental import pallas as pl
from jax.experimental.pallas import tpu as pltpu
from jax.sharding import PartitionSpec as P

MESH = pl.DeviceIdType.MESH
F32, BF16, I32 = jnp.float32, jnp.bfloat16, jnp.int32

N = 16
DP = 8
E = 128
W = 2048
TOK = 256
NE, NL = 48, 24
NLP = 32
ROWS = NE + NLP
GRAD_ROWS = 3 * NE + 80
QKV_ROWS = 3 * NE + 64
OTHERS = (
    (2, 2), (1, 2), (2, 1), (2, 3), (3, 2), (0, 2), (2, 0), (1, 1),
    (3, 3), (1, 3), (3, 1), (0, 1), (1, 0), (0, 3), (3, 0),
)
KE, KL = N * NE, N * NL
SCALE = E**-0.5
LOG2_E = 1.4426950408889634


def dot(a, b):
    return lax.dot_general(a, b, (((1,), (0,)), ((), ())), preferred_element_type=F32)


def dot_nt(a, b):
    return lax.dot_general(a, b, (((1,), (1,)), ((), ())), preferred_element_type=F32)


def dot_tn(a, b):
    return lax.dot_general(a, b, (((0,), (0,)), ((), ())), preferred_element_type=F32)


def iota(shape, dim):
    return lax.broadcasted_iota(I32, shape, dim)


def onehot(mask):
    return jnp.where(mask, 1.0, 0.0).astype(BF16)


def kernel(
    depths, owners, cot, query_early, keyval_early, query_late, keyval_late, weight,
    dquery_early, dkeyval_early, dquery_late, dkeyval_late, sums,
    depth_v, owner_v, cotv, wv, ql_v, kve_v, kvl_v, qkv_send,
    rows_send, rows_recv, meta_send, meta_recv, qkv_recv, rows_all,
    dout_send, dout_recv, att_send, att_recv, dqkv_send,
    sum1_send, sum1_recv, sum2_send,
    out, dkve_v, dql_v, dkvl_v,
    probs_e, probs_bf_e, ds_e, probs_l, probs_bf_l, ds_l,
    local_sem, send, recv, gsend, grecv, sum_send, sum_recv,
):
    d = lax.axis_index("dp")
    s = lax.axis_index("seq")
    chip = lax.div(d, 2)
    core = lax.rem(d, 2)
    partner = chip * 2 + 1 - core
    z, y = lax.div(s, 4), lax.rem(s, 4)

    def head_of(j):
        return lax.rem(chip + lax.rem(j, 4) + 2 * core, 4) * 4 + lax.div(j, 4)

    def same_core(i):
        return lax.rem(chip + i, 4) * 2 + core

    my_head = head_of(s)
    target_dp = lax.div(my_head, 2)
    parity = lax.rem(my_head, 2)

    cot_copies = [
        pltpu.make_async_copy(
            cot.at[r, 0, pl.ds(i * 128, 128)], cotv.at[r, pl.ds(i * 128, 128)],
            local_sem.at[8 + 2 * r + i],
        )
        for r in range(2)
        for i in range(2)
    ]
    weight_copy = pltpu.make_async_copy(weight, wv, local_sem.at[1])
    routing = [
        pltpu.make_async_copy(depths, depth_v, local_sem.at[6]),
        pltpu.make_async_copy(owners, owner_v, local_sem.at[7]),
    ]
    late_copy = pltpu.make_async_copy(keyval_late, kvl_v, local_sem.at[3])
    operands = [
        pltpu.make_async_copy(keyval_early, kve_v, local_sem.at[2]),
        pltpu.make_async_copy(query_late, ql_v, local_sem.at[5]),
        pltpu.make_async_copy(query_early.at[0], qkv_send.at[0:NE], local_sem.at[4]),
    ]
    for copy in routing + [late_copy] + cot_copies + operands + [weight_copy]:
        copy.start()

    barrier = pltpu.get_barrier_semaphore()

    def greet(to_dp, to_seq):
        pl.semaphore_signal(barrier, inc=1, device_id=(to_dp, to_seq), device_id_type=MESH)

    for i in range(1, N):
        greet(d, lax.rem(s + i, N))
    greet(partner, s)
    for i in (1, 3):
        greet(same_core(i), s)
    for from_dp in range(DP):
        turn = lax.rem(chip + 8 - from_dp // 2 - 2 * (from_dp % 2), 4)
        for p in range(2):
            from_seq = (2 * core + p) * 4 + turn

            @pl.when(jnp.logical_or(d != from_dp, from_seq != s))
            def _(from_dp=from_dp, from_seq=from_seq):
                greet(from_dp, from_seq)

    for copy in routing:
        copy.wait()
    depth = depth_v[...]
    active_e, active_l = depth > 1, depth > 2
    owner_e, owner_l = owner_v[0], owner_v[1]
    flags = jnp.where(
        iota((16, TOK), 0) < 8,
        jnp.broadcast_to(active_e.astype(F32), (16, TOK)),
        jnp.broadcast_to(active_l.astype(F32), (16, TOK)),
    ).astype(BF16)
    below = onehot(iota((TOK, TOK), 0) < iota((TOK, TOK), 1))
    before = dot(flags, below).astype(I32)
    rank_e, rank_l = before[0:1] >> 4, before[8:9] >> 4
    token = (iota((8, TOK), 1) + 1).astype(F32).astype(BF16)
    line = iota((E, TOK), 0)
    meta_e = dot_nt(token, onehot((line == owner_e * 8 + rank_e) & active_e))
    meta_l = dot_nt(token, onehot((line == owner_l * 4 + rank_l) & active_l))
    meta = jnp.where(iota((8, E), 0) < 4, meta_e, meta_l)
    late_copy.wait()
    meta_send[...] = jnp.concatenate(
        [kvl_v[0, 16:NL, 1, :].astype(F32), jnp.concatenate([meta] * N, axis=1)], axis=0
    ).astype(BF16)

    for copy in cot_copies[0:2]:
        copy.wait()
    line = iota((TOK, TOK), 0)
    base = jnp.where(active_e, owner_e * 16 + rank_e, -64)
    packed = dot(onehot(line == base), cotv[0, :, 0:1024])
    packed += dot(onehot(line == base + 8), cotv[0, :, 1024:2048])
    rows_send[:, :, 0:1024] = packed.reshape(N, 16, 1024).astype(BF16)
    for copy in cot_copies[2:4]:
        copy.wait()
    base = jnp.where(active_l, owner_l * 16 + rank_l, -64)
    packed = dot(onehot(line == base), cotv[1, :, 0:512])
    for q in range(1, 4):
        packed += dot(onehot(line == base + 4 * q), cotv[1, :, q * 512 : (q + 1) * 512])
    rows_send[:, :, 1024:1536] = packed.reshape(N, 16, 512).astype(BF16)

    elsewhere = jnp.where(target_dp == d, 0, 1)
    pl.semaphore_wait(barrier, N - 1 + 3 + N - 1 + elsewhere)

    def remote(src, dst, phase, to, to_dp):
        return pltpu.make_async_remote_copy(
            src_ref=src,
            dst_ref=dst,
            send_sem=send.at[phase],
            recv_sem=recv.at[phase],
            device_id=(to_dp, to),
            device_id_type=MESH,
        )

    def wait_bytes(ref, sem):
        pltpu.make_async_copy(ref, ref, sem).wait()

    def other(dz, dy):
        to_z = lax.rem(z + jnp.where(core == 0, dz, 4 - dz), 4)
        to_y = lax.rem(y + jnp.where(core == 0, dy, 4 - dy), 4)
        return to_z * 4 + to_y

    def exchange(phase, src, dst, whole):
        for dz, dy in OTHERS:
            to = other(dz, dy)
            remote(src(to), dst(s), phase, to, d).start()
        pltpu.make_async_copy(src(s), dst(s), recv.at[phase]).start()

    def arrive(phase, src, dst, whole):
        wait_bytes(whole, recv.at[phase])

    def columns(ref, j):
        return ref.at[:, pl.ds(pl.multiple_of(head_of(j) * E, E), E)]

    META = (0, lambda j: columns(meta_send, j), lambda j: meta_recv.at[j], meta_recv)
    ROW = (1, lambda j: rows_send.at[j], lambda j: rows_recv.at[j], rows_recv)
    QKV = (2, lambda j: columns(qkv_send, j), lambda j: qkv_recv.at[j], qkv_recv)
    DOUT = (3, lambda j: columns(dout_send, j), lambda j: dout_recv.at[j], dout_recv)

    def grads(phase, first, last):
        return (
            phase,
            lambda j: dqkv_send.at[j, first:last],
            lambda j: columns(out.at[first:last], j),
            out.at[first:last],
        )

    GRAD_Q = (
        4,
        lambda j: dqkv_send.at[j, 0:NE],
        lambda j: columns(dquery_early.at[0], j),
        dquery_early.at[0],
    )
    GRAD_LATE = grads(5, 3 * NE, GRAD_ROWS)
    GRAD_K, GRAD_V = grads(6, NE, 2 * NE), grads(7, 2 * NE, 3 * NE)
    ATT = 8

    exchange(*META)
    exchange(*ROW)
    for copy in operands:
        copy.wait()
    qkv_send[NE : 2 * NE] = kve_v[0, :, 0, :]
    qkv_send[2 * NE : 3 * NE] = kve_v[0, :, 1, :]
    for c in range(4):
        cut = slice(c * 512, (c + 1) * 512)
        pair = kvl_v[0, :, :, cut].astype(F32)
        qkv_send[3 * NE : QKV_ROWS, cut] = jnp.concatenate(
            [ql_v[0, :, cut].astype(F32), pair[:, 0], pair[0:16, 1]], axis=0
        ).astype(BF16)
    exchange(*QKV)

    arrive(*META)

    tokens = meta_recv[...].astype(F32)

    def spread(first, shift):
        lane = iota((N, E), 1)
        mine = (lane >> shift) == iota((N, E), 0)
        wide = jnp.concatenate(
            [jnp.where(mine, tokens[j, first : first + 1], 0.0) for j in range(N)], axis=0
        )
        low = (1 << shift) - 1
        same = onehot((iota((E, E), 0) & low) == (iota((E, E), 1) & low))
        wide = dot(wide.astype(BF16), same)
        total = jnp.zeros((N, E), F32)
        for j in range(N):
            total += jnp.where((lane >> shift) == j, wide[j * N : (j + 1) * N], 0.0)
        return total

    token_e = spread(8, 3)
    token_l = spread(12, 2)

    def tables(token, shift, slots, padded):
        peak = 1 << shift
        valid = onehot(token > 0.0)
        src, dst = iota((E, E), 0), iota((E, E), 1)
        offset = dot(valid, onehot((src >> shift) < (dst >> shift)))[0:1].astype(I32)
        in_lane = iota((1, E), 1)
        slot = jnp.where(token[0:1] > 0.0, offset + (in_lane & (peak - 1)), -1)
        select = onehot(iota((padded, E), 0) == slot)
        low = token.astype(BF16)
        high = jnp.where(token > 0.0, (iota((N, E), 1) >> shift).astype(F32), 0.0).astype(BF16)
        cols = dot_nt(select, high) * 256.0 + dot_nt(select, low) - 1.0
        total = N * slots
        mult = 1366 if slots == NE else 2731
        in_row = iota((padded, total), 1)
        tile = onehot(in_row - ((in_row * mult) >> 16) * slots == iota((padded, total), 0))
        wide_high = dot(dot_nt(high, select).astype(BF16), tile)
        wide_low = dot(dot_nt(low, select).astype(BF16), tile)
        in_row = iota((N, total), 1)
        mine = ((in_row * mult) >> 16) == iota((N, total), 0)
        row = jnp.sum(
            jnp.where(mine, wide_high * 256.0 + wide_low - 1.0, 0.0), axis=0, keepdims=True
        )
        src, dst = iota((E, TOK), 0), iota((E, TOK), 1)
        offset = dot(valid, onehot((src >> shift) < (dst >> 4)))[0:1].astype(I32)
        count = dot(valid, onehot((src >> shift) == (dst >> 4)))[0:1].astype(I32)
        in_lane = iota((1, TOK), 1)
        rank = in_lane & (peak - 1)
        slot = jnp.where(rank < count, offset + rank, -1)
        part = (in_lane & 15) >> shift
        return cols, row, slot, part

    cols_e, row_e, slot_e, part_e = tables(token_e, 3, NE, NE)
    cols_l, row_l, slot_l, part_l = tables(token_l, 2, NL, NLP)

    arrive(*ROW)
    for h in range(2):
        pick = onehot((iota((NE, TOK), 0) == slot_e) & (part_e == h))
        got = dot(pick, rows_recv[:, :, 0:1024].reshape(TOK, 1024))
        rows_all[d, 0:NE, h * 1024 : (h + 1) * 1024] = got.astype(BF16)
    for q in range(4):
        pick = onehot((iota((NLP, TOK), 0) == slot_l) & (part_l == q))
        got = dot(pick, rows_recv[:, :, 1024:1536].reshape(TOK, 512))
        rows_all[d, NE:ROWS, q * 512 : (q + 1) * 512] = got.astype(BF16)

    def block_part(block, half):
        part = rows_all.at[block]
        return part if half is None else part.at[:, half * 1024 : (half + 1) * 1024]

    def gather(block, kind, to_dp, half=None):
        part = block_part(block, half)
        return pltpu.make_async_remote_copy(
            src_ref=part,
            dst_ref=part,
            send_sem=gsend,
            recv_sem=grecv.at[kind],
            device_id=(to_dp, s),
            device_id_type=MESH,
        )

    ahead, behind, far = same_core(1), same_core(3), same_core(2)
    FROM_FAR, FROM_PARTNER = 4, 5
    gather(d, 0, ahead, 1).start()
    gather(d, 1, behind, 0).start()
    gather(d, 2, ahead, 0).start()
    gather(d, 3, behind, 1).start()
    gather(d, FROM_PARTNER, partner).start()

    def gather_pass():
        wait_bytes(block_part(behind, 1), grecv.at[0])
        gather(behind, FROM_FAR, ahead, 1).start()
        wait_bytes(block_part(ahead, 0), grecv.at[1])
        gather(ahead, FROM_FAR, behind, 0).start()

    def gather_near():
        wait_bytes(block_part(behind, 0), grecv.at[2])
        gather(behind, FROM_PARTNER, partner).start()
        wait_bytes(block_part(ahead, 1), grecv.at[3])
        gather(ahead, FROM_PARTNER, partner).start()

    def gather_far():
        wait_bytes(rows_all.at[far], grecv.at[FROM_FAR])
        gather(far, FROM_PARTNER, partner).start()

    weight_copy.wait()
    mine = rows_all[d]
    for c in range(8):
        part = dot_nt(mine, wv[c * 256 : (c + 1) * 256, :])
        dout_send[:, c * 256 : (c + 1) * 256] = part.astype(BF16)
    exchange(*DOUT)

    gather_pass()
    arrive(*QKV)

    def late(wide, part):
        return wide[:, part * NL : (part + 1) * NL].reshape(KL, E)

    def softmax(query, key, value, row, col):
        scores = dot_nt(query, key) * (SCALE * LOG2_E)
        scores = jnp.where(row <= col, scores, -1e30)
        top = jnp.max(scores, axis=1, keepdims=True)
        weights = jnp.exp2(scores - top)
        probs = weights * (1.0 / jnp.sum(weights, axis=1, keepdims=True))
        probs_bf = probs.astype(BF16)
        return probs, probs_bf, dot(probs_bf, value)

    def attended_out(first, last):
        def copy(to):
            return remote(
                att_send.at[to, first:last], att_recv.at[d, parity, first:last], ATT, to, target_dp
            )

        for dz, dy in OTHERS:
            copy(other(dz, dy)).start()

        @pl.when(target_dp == d)
        def _():
            pltpu.make_async_copy(
                att_send.at[s, first:last], att_recv.at[d, parity, first:last], recv.at[ATT]
            ).start()

        @pl.when(target_dp != d)
        def _():
            copy(s).start()

    key_e = qkv_recv[:, NE : 2 * NE, :].reshape(KE, E)
    value_e = qkv_recv[:, 2 * NE : 3 * NE, :].reshape(KE, E)
    for b in range(4):
        query = qkv_recv[4 * b : 4 * b + 4, 0:NE, :].reshape(4 * NE, E)
        col = jnp.concatenate([cols_e[:, o : o + 1] for o in range(4 * b, 4 * b + 4)], axis=0)
        probs, probs_bf, attended = softmax(query, key_e, value_e, row_e, col)
        probs_e[b * 192 : (b + 1) * 192] = probs
        probs_bf_e[b * 192 : (b + 1) * 192] = probs_bf
        att_send[4 * b : 4 * b + 4, 0:NE, :] = attended.reshape(4, NE, E).astype(BF16)
    attended_out(0, NE)
    gather_near()
    wide = jnp.concatenate(
        [qkv_recv[:, 3 * NE : QKV_ROWS, :].astype(F32), meta_recv[:, 0:8, :].astype(F32)], axis=1
    )
    query_l, key_l, value_l = (late(wide, part).astype(BF16) for part in range(3))
    gap = jnp.zeros((8, NLP - NL, E), F32)
    for b in range(2):
        query = query_l[b * 192 : (b + 1) * 192]
        col = jnp.concatenate([cols_l[0:NL, o : o + 1] for o in range(8 * b, 8 * b + 8)], axis=0)
        probs, probs_bf, attended = softmax(query, key_l, value_l, row_l, col)
        probs_l[b * 192 : (b + 1) * 192] = probs
        probs_bf_l[b * 192 : (b + 1) * 192] = probs_bf
        attended = jnp.concatenate([attended.reshape(8, NL, E), gap], axis=1)
        att_send[8 * b : 8 * b + 8, NE:ROWS, :] = attended.astype(BF16)
    attended_out(NE, ROWS)

    arrive(*DOUT)
    dout_e = dout_recv[:, 0:NE, :].reshape(KE, E)
    for c in range(2):
        dvalue = dot_tn(probs_bf_e[:, c * 384 : (c + 1) * 384], dout_e)
        dqkv_send[8 * c : 8 * c + 8, 2 * NE : 3 * NE, :] = dvalue.reshape(8, NE, E).astype(BF16)
    exchange(*GRAD_V)

    def backward(query, key, value, dout, attended, probs):
        delta = jnp.sum(dout.astype(F32) * attended.astype(F32), axis=1, keepdims=True)
        dprobs = dot_nt(dout, value)
        dscores = (probs * (dprobs - delta)).astype(BF16)
        return dscores, dot(dscores, key) * SCALE

    for b in range(4):
        dout = dout_recv[4 * b : 4 * b + 4, 0:NE, :].reshape(192, E)
        attended = att_send[4 * b : 4 * b + 4, 0:NE, :].reshape(192, E)
        query = None
        dscores, dquery = backward(
            query, key_e, value_e, dout, attended, probs_e[b * 192 : (b + 1) * 192]
        )
        ds_e[b * 192 : (b + 1) * 192] = dscores
        dqkv_send[4 * b : 4 * b + 4, 0:NE, :] = dquery.reshape(4, NE, E).astype(BF16)
    query_e = qkv_recv[:, 0:NE, :].reshape(KE, E)
    for c in range(2):
        dkey = dot_tn(ds_e[:, c * 384 : (c + 1) * 384], query_e) * SCALE
        dqkv_send[8 * c : 8 * c + 8, NE : 2 * NE, :] = dkey.reshape(8, NE, E).astype(BF16)
    exchange(*GRAD_K)
    dout_l = late(dout_recv[:, NE:ROWS, :].astype(F32), 0).astype(BF16)
    attended_l = late(att_send[:, NE:ROWS, :].astype(F32), 0)
    dquery_l = []
    for b in range(2):
        dscores, dquery = backward(
            None, key_l, value_l, dout_l[b * 192 : (b + 1) * 192],
            attended_l[b * 192 : (b + 1) * 192], probs_l[b * 192 : (b + 1) * 192]
        )
        ds_l[b * 192 : (b + 1) * 192] = dscores
        dquery_l.append(dquery)
    dquery = jnp.concatenate(dquery_l, axis=0)
    dkey = dot_tn(ds_l[...], query_l) * SCALE
    dvalue = dot_tn(probs_bf_l[...], dout_l)
    parts = [part.reshape(N, NL, E) for part in (dquery, dkey, dvalue)]
    parts.append(jnp.zeros((N, 8, E), F32))
    dqkv_send[:, 3 * NE : GRAD_ROWS, :] = jnp.concatenate(parts, axis=1).astype(BF16)
    exchange(*GRAD_Q)
    gather_far()

    wait_bytes(att_recv, recv.at[ATT])
    wait_bytes(rows_all.at[0:4], grecv.at[FROM_PARTNER])
    def along(half, stage, i):
        if half == stage:
            to = lax.rem(z + i, 4)
            return to, to * 4 + y
        to = lax.rem(y + i, 4)
        return to, z * 4 + to

    def sum_copy(half, stage, i):
        source, target = (sum1_send, sum1_recv) if stage == 0 else (sum2_send, sums)
        to, device = along(half, stage, i)
        return pltpu.make_async_remote_copy(
            src_ref=source.at[half, to],
            dst_ref=target.at[half, i - 1],
            send_sem=sum_send.at[stage],
            recv_sem=sum_recv.at[stage, half],
            device_id=(d, device),
            device_id_type=MESH,
        )

    rows = rows_all[...].reshape(DP * ROWS, W)
    columns_of = [att_recv[:, p].reshape(DP * ROWS, E) for p in range(2)]
    for half in range(2):
        for p in range(2):
            for c in range(2):
                cut, first = slice(c * 512, (c + 1) * 512), half * 1024 + c * 512
                part = dot_tn(columns_of[p], rows[:, first : first + 512])
                part = part.reshape(2, 4, 16, 512).astype(BF16)
                if half == 0:
                    sum1_send[0, 2 * p : 2 * p + 2, :, :, cut] = part
                else:
                    for i in range(2):
                        for j in range(4):
                            sum1_send[1, j, 2 * p + i, :, cut] = part[i, j]
        for i in (2, 1, 3):
            sum_copy(half, 0, i).start()
    exchange(*GRAD_LATE)
    for half in range(2):
        wait_bytes(sum1_recv.at[half], sum_recv.at[0, half])
        total = sum1_send[half, z if half == 0 else y].astype(F32)
        for i in range(3):
            total += sum1_recv[half, i].astype(F32)
        sum2_send[half] = total.astype(BF16)
        for i in (2, 1, 3):
            sum_copy(half, 1, i).start()
        own = sum2_send.at[half, along(half, 1, 0)[0]]
        pltpu.make_async_copy(own, sums.at[half, 3], sum_recv.at[1, half]).start()

    wait_bytes(meta_recv.at[1:N], send.at[META[0]])
    wait_bytes(rows_recv.at[1:N], send.at[ROW[0]])
    wait_bytes(qkv_recv.at[1:N], send.at[QKV[0]])
    wait_bytes(dout_recv.at[1:N], send.at[DOUT[0]])

    @pl.when(target_dp == d)
    def _():
        wait_bytes(att_send.at[1:N], send.at[ATT])

    @pl.when(target_dp != d)
    def _():
        wait_bytes(att_send, send.at[ATT])

    wait_bytes(rows_all.at[1:DP], gsend)
    wait_bytes(sum1_recv, sum_send.at[0])

    writes = []

    def write(source, target):
        writes.append(pltpu.make_async_copy(source, target, local_sem.at[len(writes)]))
        writes[-1].start()

    arrive(*GRAD_V)
    arrive(*GRAD_K)
    dkve_v[0] = jnp.stack([out[NE : 2 * NE], out[2 * NE : 3 * NE]], axis=1)
    write(dkve_v, dkeyval_early)
    arrive(*GRAD_LATE)
    for c in range(4):
        cut = slice(c * 512, (c + 1) * 512)
        wide = out[3 * NE : GRAD_ROWS, cut].astype(F32)
        dql_v[0, :, cut] = wide[0:NL].astype(BF16)
        dkvl_v[0, :, :, cut] = jnp.stack(
            [wide[NL : 2 * NL].astype(BF16), wide[2 * NL : 3 * NL].astype(BF16)], axis=1
        )
    write(dql_v, dquery_late)
    write(dkvl_v, dkeyval_late)
    for grad, (first, last) in (
        (GRAD_Q, (0, NE)),
        (GRAD_LATE, (3 * NE, GRAD_ROWS)),
        (GRAD_K, (NE, 2 * NE)),
        (GRAD_V, (2 * NE, 3 * NE)),
    ):
        wait_bytes(dqkv_send.at[1:N, first:last], send.at[grad[0]])
    for copy in writes:
        copy.wait()
    arrive(*GRAD_Q)
    wait_bytes(sums.at[:, 0:3], sum_send.at[1])
    for half in range(2):
        wait_bytes(sums.at[half], sum_recv.at[1, half])


def finish(*refs):
    sources, targets, held, dw_v, sem = refs[0:5], refs[5:10], refs[10:15], refs[15], refs[16]
    order = (1, 4, 3, 0, 2)
    loads = {i: pltpu.make_async_copy(sources[i], held[i], sem.at[i]) for i in order}
    stores = {
        i: pltpu.make_async_copy(dw_v if i == 4 else held[i], targets[i], sem.at[5 + i])
        for i in order
    }
    for i in order:
        loads[i].start()
    for i in (1, 3, 0, 2):
        loads[i].wait()
        stores[i].start()
    loads[4].wait()
    for half in range(2):
        total = held[4][half, 3].astype(F32)
        for i in range(3):
            total += held[4][half, i].astype(F32)
        dw_v[:, half * 1024 : (half + 1) * 1024] = total
    stores[4].start()
    for i in order:
        stores[i].wait()


def shards(
    depths, owners, cotangent, query_early, keyval_early, query_late, keyval_late, out_weight
):
    hbm = pl.BlockSpec(memory_space=pl.ANY)
    results = (
        jax.ShapeDtypeStruct(query_early.shape, BF16),
        jax.ShapeDtypeStruct(keyval_early.shape, BF16),
        jax.ShapeDtypeStruct(query_late.shape, BF16),
        jax.ShapeDtypeStruct(keyval_late.shape, BF16),
        jax.ShapeDtypeStruct((N, W), F32),
    )
    between = results[0:4] + (jax.ShapeDtypeStruct((2, 4, 16, W // 2), BF16),)
    outputs = pl.pallas_call(
        kernel,
        out_shape=between,
        in_specs=[hbm] * 8,
        out_specs=(hbm,) * 5,
        scratch_shapes=[
            pltpu.VMEM((1, TOK), I32),
            pltpu.VMEM((2, 1, TOK), I32),
            pltpu.VMEM((2, TOK, W), BF16),
            pltpu.VMEM((W, W), BF16),
            pltpu.VMEM((1, NL, W), BF16),
            pltpu.VMEM((1, NE, 2, W), BF16),
            pltpu.VMEM((1, NL, 2, W), BF16),
            pltpu.VMEM((QKV_ROWS, W), BF16),
            pltpu.VMEM((N, 16, 1536), BF16),
            pltpu.VMEM((N, 16, 1536), BF16),
            pltpu.VMEM((16, W), BF16),
            pltpu.VMEM((N, 16, E), BF16),
            pltpu.VMEM((N, QKV_ROWS, E), BF16),
            pltpu.VMEM((DP, ROWS, W), BF16),
            pltpu.VMEM((ROWS, W), BF16),
            pltpu.VMEM((N, ROWS, E), BF16),
            pltpu.VMEM((N, ROWS, E), BF16),
            pltpu.VMEM((DP, 2, ROWS, E), BF16),
            pltpu.VMEM((N, GRAD_ROWS, E), BF16),
            pltpu.VMEM((2, 4, 4, 16, W // 2), BF16),
            pltpu.VMEM((2, 3, 4, 16, W // 2), BF16),
            pltpu.VMEM((2, 4, 16, W // 2), BF16),
            pltpu.VMEM((GRAD_ROWS, W), BF16),
            pltpu.VMEM((1, NE, 2, W), BF16),
            pltpu.VMEM((1, NL, W), BF16),
            pltpu.VMEM((1, NL, 2, W), BF16),
            pltpu.VMEM((KE, KE), F32),
            pltpu.VMEM((KE, KE), BF16),
            pltpu.VMEM((KE, KE), BF16),
            pltpu.VMEM((KL, KL), F32),
            pltpu.VMEM((KL, KL), BF16),
            pltpu.VMEM((KL, KL), BF16),
            pltpu.SemaphoreType.DMA((12,)),
            pltpu.SemaphoreType.DMA((9,)),
            pltpu.SemaphoreType.DMA((9,)),
            pltpu.SemaphoreType.DMA,
            pltpu.SemaphoreType.DMA((6,)),
            pltpu.SemaphoreType.DMA((2,)),
            pltpu.SemaphoreType.DMA((2, 2)),
        ],
        compiler_params=pltpu.CompilerParams(
            collective_id=0, has_side_effects=True, vmem_limit_bytes=56 * 1024 * 1024
        ),
        cost_estimate=pl.CostEstimate(
            flops=3_000_000_000, bytes_accessed=20_000_000, transcendentals=800_000
        ),
        name="rows_attention_weight",
    )(
        depths, owners, cotangent, query_early, keyval_early, query_late, keyval_late,
        out_weight,
    )
    return pl.pallas_call(
        finish,
        out_shape=results,
        in_specs=[hbm] * 5,
        out_specs=(hbm,) * 5,
        scratch_shapes=[pltpu.VMEM(array.shape, array.dtype) for array in between]
        + [pltpu.VMEM((N, W), F32), pltpu.SemaphoreType.DMA((10,))],
        compiler_params=pltpu.CompilerParams(vmem_limit_bytes=56 * 1024 * 1024),
        name="outputs",
    )(*outputs)


def solution(mesh):
    in_specs = (
        P("dp", "seq"),
        P(None, "dp", "seq"),
        P(None, "dp", "seq", None),
        P("dp", "seq", None),
        P("dp", "seq", None, None),
        P("dp", "seq", None),
        P("dp", "seq", None, None),
        P(),
    )
    out_specs = (
        P("dp", "seq", None),
        P("dp", "seq", None, None),
        P("dp", "seq", None),
        P("dp", "seq", None, None),
        P(("dp", "seq"), None),
    )
    return jax.shard_map(shards, mesh=mesh, in_specs=in_specs, out_specs=out_specs, check_vma=False)
```
